128 devices in a mesh: batch: 128 (over y, z, x, core).
Axes of the slice: x: 4, y: 4, z: 4, core: 2. Of those that a mesh axis runs over, the one named last changes fastest.
Arguments:
- tokens: bfloat16 [65536, 256], P('batch'), may hold values from -5 to 5
- labels: int32 [65536, 2], P('batch'), may hold values from 0 to 1
- lengths: int32 [512], replicated, may hold values from 1 to 200, 65536 in all
- codes_one: bfloat16 [256, 32], replicated, may hold values from -0.375 to 0.375
- mixing_one: bfloat16 [256, 8], replicated, may hold values from -0.1875 to 0.1875
- inner_one: bfloat16 [256, 4096], replicated, may hold values from -0.375 to 0.375
- inner_bias_one: bfloat16 [4096], replicated, may hold values from -1.5 to 1.5
- outer_one: bfloat16 [16, 256, 256], replicated, may hold values from -1.5 to 1.5
- outer_bias_one: bfloat16 [16, 256], replicated, may hold values from -3 to 3
- codes_two: bfloat16 [256, 32], replicated, may hold values from -0.75 to 0.75
- mixing_two: bfloat16 [256, 8], replicated, may hold values from -0.375 to 0.375
- inner_two: bfloat16 [256, 4096], replicated, may hold values from -0.75 to 0.75
- inner_bias_two: bfloat16 [4096], replicated, may hold values from -1.5 to 1.5
- outer_two: bfloat16 [16, 256, 256], replicated, may hold values from -1.5 to 1.5
- outer_bias_two: bfloat16 [16, 256], replicated, may hold values from -3 to 3
- tower_inner: bfloat16 [2, 256, 128], replicated, may hold values from -0.75 to 0.75
- tower_inner_bias: bfloat16 [2, 128], replicated, may hold values from -1.5 to 1.5
- tower_outer: bfloat16 [2, 128], replicated, may hold values from -1 to 1
- tower_outer_bias: bfloat16 [2], replicated, may hold values from 1 to 2
Outputs:
- predictions: float32 [65536, 2], P('batch')
- grad_tokens: float32 [65536, 256], P('batch')
- grad_codes_one: float32 [256, 32], replicated
- grad_mixing_one: float32 [256, 8], replicated
- grad_inner_one: float32 [256, 4096], replicated
- grad_inner_bias_one: float32 [4096], replicated
- grad_outer_one: float32 [16, 256, 256], replicated
- grad_outer_bias_one: float32 [16, 256], replicated
- grad_codes_two: float32 [256, 32], replicated
- grad_mixing_two: float32 [256, 8], replicated
- grad_inner_two: float32 [256, 4096], replicated
- grad_inner_bias_two: float32 [4096], replicated
- grad_outer_two: float32 [16, 256, 256], replicated
- grad_outer_bias_two: float32 [16, 256], replicated
- grad_tower_inner: float32 [2, 256, 128], replicated
- grad_tower_inner_bias: float32 [2, 128], replicated
- grad_tower_outer: float32 [2, 128], replicated
- grad_tower_outer_bias: float32 [2], replicated
The draws below stay inside these ranges and needn't reach their ends.
Inputs may be any that keep to these rules, and one draw needn't show every extreme that they name: Session lengths sum to 65536; the longest session has exactly 200 rows.
All inputs are finite; a program needn't handle non-finite values.
Results may differ from the reference program's by a relative error of at most 0.012.
The reference program's roundings to bfloat16 on the way count: a program that leaves them out, or rounds other values in their place, can miss the bound.
Values sent between devices are 32-bit elements; how exact they have to be, the bound alone decides.
No kernel may reach another device: no remote copies, remote signals or barrier semaphores. Data moves between devices by JAX's collectives and lax.ppermute only.
A program may use at most 256 MiB of HBM per device.

```python
import math
import jax
import jax.numpy as jnp
import numpy as np
from jax import lax

D = 256
HID = 256
TOWER = 128
EXPERTS = 16
SEL = 4
BITS = 4
TASKS = 2
MAXLEN = 200
TOKENS = 65536
SESS = 512


def draw_labels(key, part):
    key = jax.random.fold_in(key, 5)
    row_ids = jnp.arange(TOKENS, dtype=jnp.int32)
    rising = 100 + 400 * row_ids // TOKENS
    falling = 500 - 400 * row_ids // TOKENS
    limits = jnp.stack([rising, falling], axis=1)
    picks = jax.random.randint(key, (TOKENS, TASKS), 0, 1000, dtype=jnp.int32)
    return (picks < limits).astype(jnp.int32)


def draw_tokens(key, part):
    key = jax.random.fold_in(key, 11)
    mean_key = jax.random.fold_in(key, 1)
    row_key = jax.random.fold_in(key, 2)
    column_means = jax.random.uniform(mean_key, (1, D), jnp.float32, -0.8, 0.8)
    spread = jnp.clip(jax.random.normal(row_key, (TOKENS, D), jnp.float32), -4.0, 4.0)
    return (spread + column_means).astype(jnp.bfloat16)


def length_profile(amount, total, reach, lean):
    portions = [(1 << 20) // math.isqrt(grade ** lean) + 1 for grade in range(2, amount + 1)]
    spare, counts = total - reach - (amount - 1), [1] * (amount - 1)
    while spare > 0:
        free = [i for i in range(amount - 1) if counts[i] < reach]
        pool, budget = sum([portions[i] for i in free]), spare
        for i in free:
            more = min(reach - counts[i], max(1, budget * portions[i] // pool), spare)
            counts[i] = counts[i] + more
            spare = spare - more
    return np.array([reach] + counts)


def uneven(rng, count, total, limit, slope):
    if count == 2:
        one = jax.random.randint(rng, (), max(1, total - limit), min(limit, total - 1) + 1)
        return jnp.stack([one, total - one])
    sizes = jnp.asarray(length_profile(count, total, limit, slope), jnp.int32)
    twos = (count - 1) // 2
    source_of, taker = sizes[1:1 + 2 * twos:2], sizes[2:2 + 2 * twos:2]
    slack = jnp.minimum(source_of - 1, limit - taker)
    shifted = jax.random.randint(jax.random.fold_in(rng, 1), (twos,), 0, 1 << 20) % (slack + 1)
    sizes = sizes.at[1:1 + 2 * twos:2].set(source_of - shifted).at[2:2 + 2 * twos:2].set(taker + shifted)
    return sizes[jax.random.permutation(jax.random.fold_in(rng, 2), count)]


def scatter_about(stream_key, shape, width, bound, kind=jnp.bfloat16):
    array = width * jax.random.normal(stream_key, shape, jnp.float32)
    return jnp.clip(array, min=-bound, max=bound).astype(kind)


def setup_inputs(seed: int = 0) -> dict:
    splits = jax.random.split(jax.random.key(seed), 20)
    return {
        "tokens": draw_tokens(jax.random.fold_in(splits[19], 71), 0),
        "labels": draw_labels(jax.random.fold_in(splits[19], 71), 0),
        "lengths": uneven(splits[2], SESS, TOKENS, MAXLEN, 1).astype(jnp.int32),
        "codes_one": scatter_about(splits[3], (D, TASKS * SEL * BITS), D ** -0.5, 0.375),
        "mixing_one": scatter_about(splits[4], (D, TASKS * SEL), (4 * D) ** -0.5, 0.1875),
        "inner_one": scatter_about(splits[5], (D, EXPERTS * HID), D ** -0.5, 0.375),
        "inner_bias_one": scatter_about(splits[6], (EXPERTS * HID,), 0.1, 1.5),
        "outer_one": scatter_about(splits[7], (EXPERTS, HID, D), (HID // 16) ** -0.5, 1.5),
        "outer_bias_one": scatter_about(splits[8], (EXPERTS, D), 0.2, 3.0),
        "codes_two": scatter_about(splits[9], (D, TASKS * SEL * BITS), (D // 4) ** -0.5, 0.75),
        "mixing_two": scatter_about(splits[10], (D, TASKS * SEL), D ** -0.5, 0.375),
        "inner_two": scatter_about(splits[11], (D, EXPERTS * HID), (D // 4) ** -0.5, 0.75),
        "inner_bias_two": scatter_about(splits[12], (EXPERTS * HID,), 0.1, 1.5),
        "outer_two": scatter_about(splits[13], (EXPERTS, HID, D), (HID // 16) ** -0.5, 1.5),
        "outer_bias_two": scatter_about(splits[14], (EXPERTS, D), 0.2, 3.0),
        "tower_inner": scatter_about(splits[15], (TASKS, D, TOWER), (D // 4) ** -0.5, 0.75),
        "tower_inner_bias": scatter_about(splits[16], (TASKS, TOWER), 0.1, 1.5),
        "tower_outer": scatter_about(splits[17], (TASKS, TOWER), (TOWER // 4) ** -0.5, 1.0),
        "tower_outer_bias": jnp.clip(jax.random.uniform(splits[18], (TASKS,), jnp.float32, 1.0, 2.0), 1.0, 2.0).astype(jnp.bfloat16),
    }


highest = lax.Precision.HIGHEST
smooth_gamma = 10.0

@jax.custom_vjp
def low(v):
    return lax.optimization_barrier(v.astype(jnp.bfloat16)).astype(jnp.float32)

@jax.custom_vjp
def low_back(v):
    return v

def low_keep(v):
    return (low(v), None)

def low_pass(kept, grad):
    return (grad,)

def back_keep(v):
    return (v, None)

def back_low(kept, grad):
    return (low(grad),)
low.defvjp(low_keep, low_pass)
low_back.defvjp(back_keep, back_low)

def smooth_gates(code_logits, mixing):
    half_span = 0.5 * smooth_gamma
    clipped = jnp.clip(code_logits, -half_span, half_span)
    step_val = -2.0 / smooth_gamma ** 3 * clipped ** 3 + 1.5 / smooth_gamma * clipped + 0.5
    shaped = step_val.reshape(code_logits.shape[:-1] + (SEL, BITS, 1))
    expert_ids = jnp.arange(EXPERTS, dtype=jnp.int32)
    bit_ids = jnp.arange(BITS, dtype=jnp.int32)
    bit_table = (expert_ids[None, :] // (2 ** bit_ids)[:, None] % 2).astype(jnp.float32)
    factors = bit_table * shaped + (1.0 - bit_table) * (1.0 - shaped)
    select_prob = jnp.prod(factors, axis=-2)
    mix_weights = jax.nn.softmax(mixing, axis=-1)
    return lax.optimization_barrier(jnp.sum(mix_weights[..., None] * select_prob, axis=-2))

def experts_forward(inputs, inner, inner_bias, outer, outer_bias):
    num_rows = inputs.shape[0]
    pre_act = low_back(jnp.dot(inputs, inner, precision=highest) + inner_bias)
    hidden = low(jax.nn.gelu(pre_act)).reshape(num_rows, EXPERTS, HID)
    return low_back(jnp.einsum('nej,ejd->ned', hidden, outer, precision=highest) + outer_bias)

def block_loss(block_in, params, block_labels, block_weight, pos_ratio):
    codes_one, mixing_one, inner_one, inner_bias_one, outer_one, outer_bias_one, codes_two, mixing_two, inner_two, inner_bias_two, outer_two, outer_bias_two, tower_inner, tower_inner_bias, tower_outer, tower_outer_bias = params
    num_rows = block_in.shape[0]
    out_one = experts_forward(block_in, inner_one, inner_bias_one, outer_one, outer_bias_one)
    code_one = low_back(jnp.dot(block_in, codes_one, precision=highest)).reshape(num_rows, TASKS, SEL * BITS)
    mix_one = low_back(jnp.dot(block_in, mixing_one, precision=highest)).reshape(num_rows, TASKS, SEL)
    gate_one = smooth_gates(code_one, mix_one)
    y_one = jnp.einsum('nte,ned->ntd', gate_one, out_one, precision=highest)
    u_two = low(y_one)
    out_two = experts_forward(u_two.reshape(num_rows * TASKS, D), inner_two, inner_bias_two, outer_two, outer_bias_two)
    out_two = out_two.reshape(num_rows, TASKS, EXPERTS, D)
    code_two = low_back(jnp.einsum('ntd,dtc->ntc', u_two, codes_two.reshape(D, TASKS, SEL * BITS), precision=highest))
    mix_two = low_back(jnp.einsum('ntd,dtc->ntc', u_two, mixing_two.reshape(D, TASKS, SEL), precision=highest))
    gate_two = smooth_gates(code_two, mix_two)
    y_two = jnp.einsum('nte,nted->ntd', gate_two, out_two, precision=highest)
    tower_in = low(y_two)
    tower_pre = low_back(jnp.einsum('ntd,tdh->nth', tower_in, tower_inner, precision=highest) + tower_inner_bias)
    tower_hid = low(jax.nn.gelu(tower_pre))
    logit = low_back(jnp.einsum('nth,th->nt', tower_hid, tower_outer, precision=highest) + tower_outer_bias)
    row_loss = -(pos_ratio * block_labels * jax.nn.log_sigmoid(logit) + (1.0 - block_labels) * jax.nn.log_sigmoid(-logit))
    return (jnp.sum(block_weight[:, None] * row_loss), jax.nn.sigmoid(logit))

def reference(tokens, labels, lengths, codes_one, mixing_one, inner_one, inner_bias_one, outer_one, outer_bias_one, codes_two, mixing_two, inner_two, inner_bias_two, outer_two, outer_bias_two, tower_inner, tower_inner_bias, tower_outer, tower_outer_bias):
    params = tuple((weight.astype(jnp.float32) for weight in (codes_one, mixing_one, inner_one, inner_bias_one, outer_one, outer_bias_one, codes_two, mixing_two, inner_two, inner_bias_two, outer_two, outer_bias_two, tower_inner, tower_inner_bias, tower_outer, tower_outer_bias)))
    labels_f = labels.astype(jnp.float32)
    positives = lax.optimization_barrier(jnp.sum(labels_f, axis=0))
    pos_ratio = (TOKENS - positives) / positives
    session_weight = TOKENS / SESS / lengths.astype(jnp.float32)
    row_weight = jnp.repeat(session_weight, lengths, total_repeat_length=TOKENS)
    block_rows = math.gcd(TOKENS, 4096)
    num_blocks = TOKENS // block_rows
    slabs = (tokens.astype(jnp.float32).reshape(num_blocks, block_rows, D), labels_f.reshape(num_blocks, block_rows, TASKS), row_weight.reshape(num_blocks, block_rows))

    def one_block(running, slab_in):
        block_x, block_labels, block_weight = slab_in

        def loss_fn(block_in, *weights):
            return block_loss(block_in, weights, block_labels, block_weight, pos_ratio)
        loss_val, pull_back, probs_out = jax.vjp(loss_fn, block_x, *params, has_aux=True)
        gradients = pull_back(jnp.ones((), loss_val.dtype))
        summed = tuple((accum + update for accum, update in zip(running, gradients[1:])))
        return (summed, (probs_out, gradients[0]))
    zero_grads = tuple((jnp.zeros_like(weight) for weight in params))
    grad_sums, (probs_all, grad_rows) = lax.scan(one_block, zero_grads, slabs)
    return (probs_all.reshape(TOKENS, TASKS), grad_rows.reshape(TOKENS, D), grad_sums[0], grad_sums[1], grad_sums[2], grad_sums[3], grad_sums[4], grad_sums[5], grad_sums[6], grad_sums[7], grad_sums[8], grad_sums[9], grad_sums[10], grad_sums[11], grad_sums[12], grad_sums[13], grad_sums[14], grad_sums[15])
```

```python
import functools

import jax
import jax.numpy as jnp
from jax import lax
from jax.experimental import pallas as pl
from jax.experimental.pallas import tpu as pltpu
from jax.sharding import PartitionSpec as P

EXPERTS = 16
SEL = 4
BITS = 4
TASKS = 2
WIDTH = 256
HID = 256
TOWER = 128
PAIR = 2
STEPS = EXPERTS // PAIR
F32 = jnp.float32
BF16 = jnp.bfloat16
ROOT = 0.7978845608028654
CUBE = 0.044715
BYTES = 56 * 1024 * 1024


def nn(a, b):
    return lax.dot_general(a, b, (((1,), (0,)), ((), ())), preferred_element_type=F32)


def nt(a, b):
    return lax.dot_general(a, b, (((1,), (1,)), ((), ())), preferred_element_type=F32)


def tn(a, b):
    return lax.dot_general(a, b, (((0,), (0,)), ((), ())), preferred_element_type=F32)


def pieces(x):
    hi = x.astype(BF16)
    rest = x - hi.astype(F32)
    mid = rest.astype(BF16)
    return hi, mid, (rest - mid.astype(F32)).astype(BF16)


def gelu_both(x):
    square = x * x
    slope = square * (ROOT * CUBE) + ROOT
    s = 0.5 + 0.5 * jnp.tanh(x * slope)
    value = x * s
    return value, s + value * (1.0 - s) * (slope * 6.0 - 4.0 * ROOT)


def soft_parts(mix):
    top = jnp.maximum(jnp.maximum(mix[0], mix[1]), jnp.maximum(mix[2], mix[3]))
    raised = [jnp.exp(m - top) for m in mix]
    total = raised[0] + raised[1] + raised[2] + raised[3]
    return [r / total for r in raised]


def bit_factors(code):
    rows = code[0].shape[1]
    expert = lax.broadcasted_iota(jnp.int32, (EXPERTS, rows), 0)
    found = []
    for i in range(SEL):
        per_bit = []
        for b in range(BITS):
            k = jnp.clip(code[i * BITS + b], -5.0, 5.0)
            s = -0.002 * (k * k * k) + 0.15 * k + 0.5
            on = (expert >> b) & 1 == 1
            per_bit.append(jnp.where(on, s, 1.0 - s))
        found.append(per_bit)
    return found


def gate_of(code, mix):
    w = soft_parts(mix)
    total = None
    for i, f in enumerate(bit_factors(code)):
        r = w[i] * ((f[0] * f[1]) * (f[2] * f[3]))
        total = r if total is None else total + r
    return total


def gate_back(code, mix, grad):
    rows = grad.shape[1]
    expert = lax.broadcasted_iota(jnp.int32, (EXPERTS, rows), 0)
    w = soft_parts(mix)
    grad_w, grad_code = [], []
    for i, f in enumerate(bit_factors(code)):
        low, high = f[0] * f[1], f[2] * f[3]
        grad_w.append(jnp.sum(grad * (low * high), axis=0, keepdims=True))
        up = grad * w[i]
        others = (f[1] * high, f[0] * high, low * f[3], low * f[2])
        for b in range(BITS):
            on = (expert >> b) & 1 == 1
            term = up * others[b]
            ds = jnp.sum(jnp.where(on, term, -term), axis=0, keepdims=True)
            c = code[i * BITS + b]
            k = jnp.clip(c, -5.0, 5.0)
            inside = jnp.where(jnp.abs(c) <= 5.0, 0.15 - 0.006 * (k * k), 0.0)
            grad_code.append(ds * inside)
    mean = w[0] * grad_w[0] + w[1] * grad_w[1] + w[2] * grad_w[2] + w[3] * grad_w[3]
    return grad_code, [w[i] * (grad_w[i] - mean) for i in range(SEL)]


def task_rows(logits, mixes, task, lanes):
    code = [logits[task * 16 + k : task * 16 + k + 1, lanes] for k in range(16)]
    mix = [mixes[task * 4 + k : task * 4 + k + 1, lanes] for k in range(4)]
    return code, mix


def task_lanes(task, rows, shared):
    return slice(0, rows) if shared else slice(task * rows, (task + 1) * rows)


def forward_kernel(
    shared,
    rows,
    u_ref,
    codes_ref,
    mixing_ref,
    inner_ref,
    bias_ref,
    outer_ref,
    outer_bias_ref,
    hid_ref,
    slope_ref,
    out_ref,
    next_ref,
    gate_ref,
    code_ref,
    mix_ref,
    *rest,
):
    step = pl.program_id(0)
    if shared:
        turned_ref, acc_ref = rest
    else:
        (acc_ref,) = rest
        turned_ref = u_ref

    @pl.when(step == 0)
    def _():
        if shared:
            turned_ref[...] = u_ref[...].astype(F32).T.astype(BF16)
        u = turned_ref[...]
        code_ref[...] = tn(codes_ref[...], u)
        mix_ref[...] = tn(mixing_ref[...], u)
        outer_bias = outer_bias_ref[...]
        for t in range(TASKS):
            lanes = task_lanes(t, rows, shared)
            code, mix = task_rows(code_ref, mix_ref, t, lanes)
            gate = gate_of(code, mix)
            gate_ref[:, t * rows : (t + 1) * rows] = gate
            hi, mid, low = pieces(gate)
            acc_ref[:, t * rows : (t + 1) * rows] = (
                tn(outer_bias, hi) + tn(outer_bias, mid) + tn(outer_bias, low)
            )

    u = turned_ref[...]
    bias = bias_ref[0].astype(F32).T
    for p in range(PAIR):
        e = step * PAIR + p
        pre = tn(inner_ref[:, p * HID : (p + 1) * HID], u) + bias[:, p : p + 1]
        hid, slope = gelu_both(pre)
        hid = hid.astype(BF16)
        hid_ref[p] = hid
        slope_ref[p] = slope.astype(BF16)
        out = tn(outer_ref[p], hid)
        out_ref[p] = out.astype(BF16)
        gate = gate_ref[pl.ds(e, 1), :]
        if shared:
            acc_ref[:, :rows] += gate[:, :rows] * out
            acc_ref[:, rows:] += gate[:, rows:] * out
        else:
            acc_ref[...] += gate * out

    @pl.when(step == STEPS - 1)
    def _():
        next_ref[...] = acc_ref[...].astype(BF16)


def whole(shape):
    return pl.BlockSpec(shape, lambda *_: (0,) * len(shape))


def forward(shared, u, codes, mixing, inner, inner_bias, outer, outer_bias):
    rows = u.shape[0] if shared else u.shape[1] // TASKS
    lanes = rows if shared else rows * TASKS
    state = jax.ShapeDtypeStruct((EXPERTS, HID, lanes), BF16)
    state_spec = pl.BlockSpec((PAIR, HID, lanes), lambda i: (i, 0, 0))
    out_shape = [
        state,
        state,
        state,
        jax.ShapeDtypeStruct((WIDTH, TASKS * rows), BF16),
        jax.ShapeDtypeStruct((EXPERTS, TASKS * rows), F32),
        jax.ShapeDtypeStruct((32, lanes), F32),
        jax.ShapeDtypeStruct((8, lanes), F32),
    ]
    out_specs = [state_spec] * 3 + [whole(s.shape) for s in out_shape[3:]]
    if shared:
        out_shape.append(jax.ShapeDtypeStruct((WIDTH, rows), BF16))
        out_specs.append(whole((WIDTH, rows)))
    return pl.pallas_call(
        functools.partial(forward_kernel, shared, rows),
        grid=(STEPS,),
        in_specs=[
            whole(u.shape),
            whole(codes.shape),
            whole(mixing.shape),
            pl.BlockSpec((WIDTH, PAIR * HID), lambda i: (0, i)),
            pl.BlockSpec((1, PAIR, HID), lambda i: (i, 0, 0)),
            pl.BlockSpec((PAIR, HID, WIDTH), lambda i: (i, 0, 0)),
            whole(outer_bias.shape),
        ],
        out_specs=out_specs,
        out_shape=out_shape,
        scratch_shapes=[pltpu.VMEM((WIDTH, TASKS * rows), F32)],
        compiler_params=pltpu.CompilerParams(
            dimension_semantics=("arbitrary",), vmem_limit_bytes=BYTES
        ),
        name="forward_one" if shared else "forward_two",
    )(u, codes, mixing, inner, inner_bias.reshape(STEPS, PAIR, HID), outer, outer_bias)


def tower(
    rows,
    v_ref,
    labels_ref,
    counts_ref,
    lengths_ref,
    base_ref,
    inner_ref,
    bias_ref,
    outer_ref,
    outer_bias_ref,
    predictions_ref,
    small_ref,
    grad_inner_ref,
    dy_ref,
):
    sessions = lengths_ref.shape[1]
    lens = jnp.broadcast_to(lengths_ref[...], (8, sessions)).astype(F32).astype(BF16)
    before = lax.broadcasted_iota(jnp.int32, (sessions, sessions), 0)
    after = lax.broadcasted_iota(jnp.int32, (sessions, sessions), 1)
    upto = jnp.where(before <= after, 1.0, 0.0).astype(BF16)
    ends = nn(lens, upto)[0:1, :]
    starts = ends - lens[0:1, :].astype(F32)
    ids = (lax.broadcasted_iota(jnp.int32, (rows, sessions), 0) + base_ref[0]).astype(F32)
    inside = jnp.where((ids >= starts) & (ids < ends), 1.0, 0.0).astype(BF16)
    row_length = nt(lens, inside)[0:1, :]
    all_rows = float(rows * counts_ref.shape[0])
    weight = (all_rows / sessions) / row_length
    positives = jnp.sum(counts_ref[...], axis=0, keepdims=True)
    bias = bias_ref[...].astype(F32).T
    columns = outer_ref[...].astype(F32).T
    small_ref[...] = jnp.zeros_like(small_ref)
    for t in range(TASKS):
        lanes = slice(t * rows, (t + 1) * rows)
        v = v_ref[:, lanes]
        pre = tn(inner_ref[t], v) + bias[:, t : t + 1]
        hid, slope = gelu_both(pre)
        hid = hid.astype(BF16)
        column = columns[:, t : t + 1]
        logit = jnp.sum(hid.astype(F32) * column, axis=0, keepdims=True)
        logit = logit + outer_bias_ref[0:1, t : t + 1].astype(F32)
        y = labels_ref[t : t + 1, :].astype(F32)
        count = positives[:, t : t + 1]
        ratio = (all_rows - count) / count
        chance = jax.nn.sigmoid(logit)
        predictions_ref[t : t + 1, :] = chance
        grad = weight * (-ratio * y * jax.nn.sigmoid(-logit) + (1.0 - y) * chance)
        grad = grad.astype(BF16)
        back = (grad.astype(F32) * column * slope).astype(BF16)
        picked = lax.broadcasted_iota(jnp.int32, (16, rows), 0)
        stack = jnp.where(picked == 0, grad.astype(F32), jnp.where(picked == 1, 1.0, 0.0))
        stack = stack.astype(BF16)
        by_hid = nt(stack, hid)
        by_back = nt(stack, back)
        small_ref[t : t + 1, :TOWER] = by_hid[0:1]
        small_ref[2 + t : 3 + t, :TOWER] = by_back[1:2]
        total = jnp.sum(grad.astype(F32), axis=1, keepdims=True)
        small_ref[4 + t : 5 + t, :TOWER] = jnp.broadcast_to(total, (1, TOWER))
        grad_inner_ref[t] = nt(v, back)
        dy_ref[:, lanes] = nn(inner_ref[t], back)


def backward_kernel(shared, rows, *refs):
    (u_ref, codes_ref, mixing_ref, inner_ref, outer_ref, outer_bias_ref) = refs[:6]
    (hid_ref, slope_ref, out_ref, gate_ref, code_ref, mix_ref) = refs[6:12]
    refs = refs[12:]
    if shared:
        dy_ref, refs = refs[0], refs[1:]
    else:
        tower_in, refs = refs[:9], refs[9:]
    grad_inner_ref, grad_outer_ref, grad_bias_ref, grad_rest_ref, back_ref = refs[:5]
    refs = refs[5:]
    if not shared:
        tower_out, refs = refs[:3], refs[3:]
        dy_ref, refs = refs[0], refs[1:]
    aug_ref, dgate_ref, acc_ref, dcode_ref, dmix_ref = refs
    step = pl.program_id(0)
    lanes = rows if shared else rows * TASKS

    @pl.when(step == 0)
    def _():
        if not shared:
            tower(rows, *tower_in, *tower_out, dy_ref)
        aug_ref[:WIDTH, :] = u_ref[...]
        first = lax.broadcasted_iota(jnp.int32, (16, lanes), 0) == 0
        aug_ref[WIDTH:, :] = jnp.where(first, 1.0, 0.0).astype(BF16)
        acc_ref[...] = jnp.zeros_like(acc_ref)

    pre_pair = []
    for p in range(PAIR):
        e = step * PAIR + p
        gate = gate_ref[pl.ds(e, 1), :]
        out = out_ref[p].astype(F32)
        if shared:
            one, two = dy_ref[:, :rows], dy_ref[:, rows:]
            dout = (gate[:, :rows] * one + gate[:, rows:] * two).astype(BF16)
            dgate_ref[pl.ds(e, 1), :rows] = jnp.sum(out * one, axis=0, keepdims=True)
            dgate_ref[pl.ds(e, 1), rows:] = jnp.sum(out * two, axis=0, keepdims=True)
        else:
            dy = dy_ref[...]
            dout = (gate * dy).astype(BF16)
            dgate_ref[pl.ds(e, 1), :] = jnp.sum(out * dy, axis=0, keepdims=True)
        dpre = (nn(outer_ref[p], dout) * slope_ref[p].astype(F32)).astype(BF16)
        grad_outer_ref[p] = nt(hid_ref[p], dout)
        grad = nt(aug_ref[...], dpre)
        grad_inner_ref[:, p * HID : (p + 1) * HID] = grad[:WIDTH]
        grad_bias_ref[0, p : p + 1, :] = grad[WIDTH : WIDTH + 1]
        pre_pair.append(dpre)
    acc_ref[...] += nn(inner_ref[...], jnp.concatenate(pre_pair, axis=0))

    @pl.when(step == STEPS - 1)
    def _():
        dcode_ref[...] = jnp.zeros_like(dcode_ref)
        dmix_ref[...] = jnp.zeros_like(dmix_ref)
        outer_bias = outer_bias_ref[...]
        for t in range(TASKS):
            span = slice(t * rows, (t + 1) * rows)
            here = task_lanes(t, rows, shared)
            hi, mid, low = pieces(dy_ref[:, span])
            upto = nn(outer_bias, hi) + nn(outer_bias, mid) + nn(outer_bias, low)
            code, mix = task_rows(code_ref, mix_ref, t, here)
            grad_code, grad_mix = gate_back(code, mix, dgate_ref[:, span] + upto)
            for k in range(16):
                dcode_ref[t * 16 + k : t * 16 + k + 1, here] = grad_code[k]
            for k in range(4):
                dmix_ref[t * 4 + k : t * 4 + k + 1, here] = grad_mix[k]
        dcode = dcode_ref[...].astype(BF16)
        dmix = dmix_ref[...].astype(BF16)
        u = u_ref[...]
        grad_rest_ref[:32, :] = nt(dcode, u)
        grad_rest_ref[32:40, :] = nt(dmix, u)
        g_hi, g_mid, _ = pieces(gate_ref[...])
        y_hi, y_mid, _ = pieces(dy_ref[...])
        grad_rest_ref[40:56, :] = nt(g_hi, y_hi) + nt(g_hi, y_mid) + nt(g_mid, y_hi)
        du = acc_ref[...] + nn(codes_ref[...], dcode) + nn(mixing_ref[...], dmix)
        back_ref[...] = du.T if shared else du


def backward(shared, u, codes, mixing, inner, outer, outer_bias, state, extra):
    rows = u.shape[1] if shared else u.shape[1] // TASKS
    lanes = u.shape[1]
    state_spec = pl.BlockSpec((PAIR, HID, lanes), lambda i: (i, 0, 0))
    in_arrays = [u, codes, mixing, inner, outer, outer_bias, *state, *extra]
    in_specs = [
        whole(u.shape),
        whole(codes.shape),
        whole(mixing.shape),
        pl.BlockSpec((WIDTH, PAIR * HID), lambda i: (0, i)),
        pl.BlockSpec((PAIR, HID, WIDTH), lambda i: (i, 0, 0)),
        whole(outer_bias.shape),
        state_spec,
        state_spec,
        state_spec,
    ]
    in_specs += [whole(a.shape) for a in in_arrays[9:]]
    if not shared:
        in_specs[16] = pl.BlockSpec(memory_space=pltpu.SMEM)
    back_shape = (rows, WIDTH) if shared else (WIDTH, lanes)
    out_shape = [
        jax.ShapeDtypeStruct((WIDTH, EXPERTS * HID), F32),
        jax.ShapeDtypeStruct((EXPERTS, HID, WIDTH), F32),
        jax.ShapeDtypeStruct((STEPS, PAIR, HID), F32),
        jax.ShapeDtypeStruct((56, WIDTH), F32),
        jax.ShapeDtypeStruct(back_shape, F32),
    ]
    out_specs = [
        pl.BlockSpec((WIDTH, PAIR * HID), lambda i: (0, i)),
        pl.BlockSpec((PAIR, HID, WIDTH), lambda i: (i, 0, 0)),
        pl.BlockSpec((1, PAIR, HID), lambda i: (i, 0, 0)),
        whole((56, WIDTH)),
        whole(back_shape),
    ]
    scratch = []
    if not shared:
        more = [
            jax.ShapeDtypeStruct((TASKS, rows), F32),
            jax.ShapeDtypeStruct((8, TOWER), F32),
            jax.ShapeDtypeStruct((TASKS, WIDTH, TOWER), F32),
        ]
        out_shape += more
        out_specs += [whole(s.shape) for s in more]
        scratch.append(pltpu.VMEM((WIDTH, lanes), F32))
    scratch += [
        pltpu.VMEM((WIDTH + 16, lanes), BF16),
        pltpu.VMEM((EXPERTS, TASKS * rows), F32),
        pltpu.VMEM((WIDTH, lanes), F32),
        pltpu.VMEM((32, lanes), F32),
        pltpu.VMEM((8, lanes), F32),
    ]
    return pl.pallas_call(
        functools.partial(backward_kernel, shared, rows),
        grid=(STEPS,),
        in_specs=in_specs,
        out_specs=out_specs,
        out_shape=out_shape,
        scratch_shapes=scratch,
        compiler_params=pltpu.CompilerParams(
            dimension_semantics=("arbitrary",), vmem_limit_bytes=BYTES
        ),
        name="backward_one" if shared else "backward_two",
    )(*in_arrays)


def local_part(
    tokens,
    labels,
    lengths,
    counts,
    base,
    codes_one,
    mixing_one,
    inner_one,
    inner_bias_one,
    outer_one,
    outer_bias_one,
    codes_two,
    mixing_two,
    inner_two,
    inner_bias_two,
    outer_two,
    outer_bias_two,
    tower_inner,
    tower_inner_bias,
    tower_outer,
    tower_outer_bias,
):
    one = forward(
        True, tokens, codes_one, mixing_one, inner_one, inner_bias_one, outer_one, outer_bias_one
    )
    hid_one, slope_one, out_one, u_two, gate_one, code_one, mix_one, u_one = one
    two = forward(
        False, u_two, codes_two, mixing_two, inner_two, inner_bias_two, outer_two, outer_bias_two
    )
    hid_two, slope_two, out_two, v_two, gate_two, code_two, mix_two = two
    extra = (
        v_two,
        labels.T,
        counts(two),
        lengths.reshape(1, -1),
        base,
        tower_inner,
        tower_inner_bias,
        tower_outer,
        tower_outer_bias.reshape(1, TASKS),
    )
    back_two = backward(
        False,
        u_two,
        codes_two,
        mixing_two,
        inner_two,
        outer_two,
        outer_bias_two,
        (hid_two, slope_two, out_two, gate_two, code_two, mix_two),
        extra,
    )
    back_one = backward(
        True,
        u_one,
        codes_one,
        mixing_one,
        inner_one,
        outer_one,
        outer_bias_one,
        (hid_one, slope_one, out_one, gate_one, code_one, mix_one),
        (back_two[4],),
    )
    return back_one, back_two


def on_device(tokens, labels, lengths, *params):
    local_rows = tokens.shape[0]
    devices = lax.axis_size("batch")
    count = jnp.sum(labels.astype(F32), axis=0)
    sent = jnp.broadcast_to(jnp.pad(count, (0, 126))[None, :], (devices, 128))
    counts = lax.all_to_all(sent, "batch", 0, 0, tiled=True)
    base = (lax.axis_index("batch") * local_rows).astype(jnp.int32).reshape(1)
    back_one, back_two = local_part(
        tokens, labels, lengths, lambda _: counts, base, *params
    )
    inner_one, outer_one, bias_one, rest_one, grad_tokens = back_one
    inner_two, outer_two, bias_two, rest_two, _, predictions, small, tower_inner = back_two
    pack = jnp.concatenate(
        [
            rest_one,
            bias_one.reshape(16, 256),
            rest_two,
            bias_two.reshape(16, 256),
            jnp.pad(small, ((0, 0), (0, 128))),
        ],
        axis=0,
    )
    inner_one, outer_one, inner_two, outer_two, tower_inner, pack = lax.psum(
        (inner_one, outer_one, inner_two, outer_two, tower_inner, pack), "batch"
    )
    return (
        predictions.T,
        grad_tokens,
        pack[0:32].T,
        pack[32:40].T,
        inner_one,
        pack[56:72].reshape(-1),
        outer_one,
        pack[40:56],
        pack[72:104].T,
        pack[104:112].T,
        inner_two,
        pack[128:144].reshape(-1),
        outer_two,
        pack[112:128],
        tower_inner,
        pack[146:148, :128],
        pack[144:146, :128],
        pack[148:150, 0],
    )


def solution(mesh):
    rows, copied = P("batch", None), P()
    return jax.shard_map(
        on_device,
        mesh=mesh,
        in_specs=(rows, rows) + (copied,) * 17,
        out_specs=(rows, rows) + (copied,) * 16,
        check_vma=False,
    )
```

```python
import functools

import jax
import jax.numpy as jnp
from jax import lax
from jax.experimental import pallas as pl
from jax.experimental.pallas import tpu as pltpu
from jax.sharding import Mesh, PartitionSpec as P

EXPERTS = 16
SEL = 4
BITS = 4
TASKS = 2
WIDTH = 256
HID = 256
TOWER = 128
PAIR = 2
STEPS = EXPERTS // PAIR
HALF = STEPS // 2
GROUP = 4
WAVES = EXPERTS // GROUP
SLAB = 1024
SMALL = 1024
HALF_ROWS = 8 * SLAB
ONE = (48, 48, 40)
TWO = (40, 40, 48)
CHUNK = 88
AXES = ((0, 4, 2), (4, 2, 0), (2, 0, 4))
F32 = jnp.float32
BF16 = jnp.bfloat16
ROOT = 0.7978845608028654
CUBE = 0.044715
BYTES = 61 * 1024 * 1024


def nn(a, b):
    return lax.dot_general(a, b, (((1,), (0,)), ((), ())), preferred_element_type=F32)


def nt(a, b):
    return lax.dot_general(a, b, (((1,), (1,)), ((), ())), preferred_element_type=F32)


def tn(a, b):
    return lax.dot_general(a, b, (((0,), (0,)), ((), ())), preferred_element_type=F32)


def pieces(x):
    hi = x.astype(BF16)
    rest = x - hi.astype(F32)
    mid = rest.astype(BF16)
    return hi, mid, (rest - mid.astype(F32)).astype(BF16)


def gelu_both(x):
    square = x * x
    slope = square * (ROOT * CUBE) + ROOT
    s = 0.5 + 0.5 * jnp.tanh(x * slope)
    value = x * s
    return value, s + value * (1.0 - s) * (slope * 6.0 - 4.0 * ROOT)


def soft_parts(mix):
    top = jnp.maximum(jnp.maximum(mix[0], mix[1]), jnp.maximum(mix[2], mix[3]))
    raised = [jnp.exp(m - top) for m in mix]
    total = raised[0] + raised[1] + raised[2] + raised[3]
    return [r / total for r in raised]


def bit_factors(code):
    rows = code[0].shape[1]
    expert = lax.broadcasted_iota(jnp.int32, (EXPERTS, rows), 0)
    found = []
    for i in range(SEL):
        per_bit = []
        for b in range(BITS):
            k = jnp.clip(code[i * BITS + b], -5.0, 5.0)
            s = -0.002 * (k * k * k) + 0.15 * k + 0.5
            on = (expert >> b) & 1 == 1
            per_bit.append(jnp.where(on, s, 1.0 - s))
        found.append(per_bit)
    return found


def gate_of(code, mix):
    w = soft_parts(mix)
    total = None
    for i, f in enumerate(bit_factors(code)):
        r = w[i] * ((f[0] * f[1]) * (f[2] * f[3]))
        total = r if total is None else total + r
    return total


def gate_back(code, mix, grad):
    rows = grad.shape[1]
    expert = lax.broadcasted_iota(jnp.int32, (EXPERTS, rows), 0)
    w = soft_parts(mix)
    grad_w, grad_code = [], []
    for i, f in enumerate(bit_factors(code)):
        low, high = f[0] * f[1], f[2] * f[3]
        grad_w.append(jnp.sum(grad * (low * high), axis=0, keepdims=True))
        up = grad * w[i]
        others = (f[1] * high, f[0] * high, low * f[3], low * f[2])
        for b in range(BITS):
            on = (expert >> b) & 1 == 1
            term = up * others[b]
            ds = jnp.sum(jnp.where(on, term, -term), axis=0, keepdims=True)
            c = code[i * BITS + b]
            k = jnp.clip(c, -5.0, 5.0)
            inside = jnp.where(jnp.abs(c) <= 5.0, 0.15 - 0.006 * (k * k), 0.0)
            grad_code.append(ds * inside)
    mean = w[0] * grad_w[0] + w[1] * grad_w[1] + w[2] * grad_w[2] + w[3] * grad_w[3]
    return grad_code, [w[i] * (grad_w[i] - mean) for i in range(SEL)]


def task_rows(logits, mixes, task, lanes):
    code = [logits[task * 16 + k : task * 16 + k + 1, lanes] for k in range(16)]
    mix = [mixes[task * 4 + k : task * 4 + k + 1, lanes] for k in range(4)]
    return code, mix


def task_lanes(task, rows, shared):
    return slice(0, rows) if shared else slice(task * rows, (task + 1) * rows)


def whole(shape):
    return pl.BlockSpec(shape, lambda *_: (0,) * len(shape))


def tower(
    rows,
    v_ref,
    labels_ref,
    counts_ref,
    lengths_ref,
    base_ref,
    inner_ref,
    bias_ref,
    outer_ref,
    outer_bias_ref,
    predictions_ref,
    small_ref,
    grad_inner_ref,
    dy_ref,
):
    sessions = lengths_ref.shape[1]
    lens = jnp.broadcast_to(lengths_ref[...], (8, sessions)).astype(F32).astype(BF16)
    before = lax.broadcasted_iota(jnp.int32, (sessions, sessions), 0)
    after = lax.broadcasted_iota(jnp.int32, (sessions, sessions), 1)
    upto = jnp.where(before <= after, 1.0, 0.0).astype(BF16)
    ends = nn(lens, upto)[0:1, :]
    starts = ends - lens[0:1, :].astype(F32)
    ids = (lax.broadcasted_iota(jnp.int32, (rows, sessions), 0) + base_ref[0]).astype(F32)
    inside = jnp.where((ids >= starts) & (ids < ends), 1.0, 0.0).astype(BF16)
    row_length = nt(lens, inside)[0:1, :]
    all_rows = float(rows * counts_ref.shape[0])
    weight = (all_rows / sessions) / row_length
    positives = jnp.sum(counts_ref[...], axis=0, keepdims=True)
    bias = bias_ref[...].astype(F32).T
    columns = outer_ref[...].astype(F32).T
    small_ref[...] = jnp.zeros_like(small_ref)
    for t in range(TASKS):
        lanes = slice(t * rows, (t + 1) * rows)
        v = v_ref[:, lanes]
        pre = tn(inner_ref[t], v) + bias[:, t : t + 1]
        hid, slope = gelu_both(pre)
        hid = hid.astype(BF16)
        column = columns[:, t : t + 1]
        logit = jnp.sum(hid.astype(F32) * column, axis=0, keepdims=True)
        logit = logit + outer_bias_ref[0:1, t : t + 1].astype(F32)
        y = labels_ref[t : t + 1, :].astype(F32)
        count = positives[:, t : t + 1]
        ratio = (all_rows - count) / count
        chance = jax.nn.sigmoid(logit)
        predictions_ref[t : t + 1, :] = chance
        grad = weight * (-ratio * y * jax.nn.sigmoid(-logit) + (1.0 - y) * chance)
        grad = grad.astype(BF16)
        back = (grad.astype(F32) * column * slope).astype(BF16)
        picked = lax.broadcasted_iota(jnp.int32, (16, rows), 0)
        stack = jnp.where(picked == 0, grad.astype(F32), jnp.where(picked == 1, 1.0, 0.0))
        stack = stack.astype(BF16)
        by_hid = nt(stack, hid)
        by_back = nt(stack, back)
        small_ref[t : t + 1, :TOWER] = by_hid[0:1]
        small_ref[2 + t : 3 + t, :TOWER] = by_back[1:2]
        total = jnp.sum(grad.astype(F32), axis=1, keepdims=True)
        small_ref[4 + t : 5 + t, :TOWER] = jnp.broadcast_to(total, (1, TOWER))
        grad_inner_ref[t] = nt(v, back)
        dy_ref[:, lanes] = nn(inner_ref[t], back)


def pipeline(count, tiles, stages):
    for slot in range(count + len(stages) - 1):
        for q in range(tiles):
            for late, stage in enumerate(stages):
                if 0 <= slot - late < count:
                    stage(slot - late, q)


def prepare(shared, rows, u, codes_ref, mixing_ref, outer_bias_ref, code_ref, mix_ref, gate_ref, acc_ref):
    code_ref[...] = nn(codes_ref[...], u)
    mix_ref[...] = nn(mixing_ref[...], u)
    outer_bias = outer_bias_ref[...]
    for t in range(TASKS):
        code, mix = task_rows(code_ref, mix_ref, t, task_lanes(t, rows, shared))
        gate = gate_of(code, mix)
        span = slice(t * rows, (t + 1) * rows)
        gate_ref[:, span] = gate
        hi, mid, low = pieces(gate)
        acc_ref[:, span] = tn(outer_bias, hi) + tn(outer_bias, mid) + tn(outer_bias, low)


def forward_wave(shared, rows, wave, u_ref, inner_ref, bias_ref, outer_ref, state, gate_ref, acc_ref, work):
    bias = bias_ref[0].astype(F32).T
    lanes = rows if shared else rows * TASKS
    tiles = lanes // 256
    part = WIDTH // tiles
    tall = 16 * 1024 // lanes
    pre_refs, mid_refs = work[:2], work[2:]
    kept = {}

    def start_pre(p, q):
        if q == 0:
            kept["inner", p] = inner_ref[:, p * HID : (p + 1) * HID].T
        span = slice(q * 256, (q + 1) * 256)
        pre_refs[p % 2][:, span] = nn(kept["inner", p], u_ref[:WIDTH, span])

    def bend(p, q):
        hid_ref, slope_ref, _ = state(p)
        for at in range(q * part, (q + 1) * part, tall):
            here = slice(at, at + tall)
            hid, slope = gelu_both(pre_refs[p % 2][here, :lanes] + bias[here, p : p + 1])
            hid_ref[here, :] = hid.astype(BF16)
            slope_ref[here, :] = slope.astype(BF16)

    def start_out(p, q):
        if q == 0:
            kept["outer", p] = outer_ref[p].T
        span = slice(q * 256, (q + 1) * 256)
        mid_refs[p % 2][:, span] = nn(kept["outer", p], state(p)[0][:, span])

    def combine(p, q):
        if q == 0:
            kept["gate", p] = gate_ref[pl.ds(wave * GROUP + p, 1), :]
        gate = kept["gate", p]
        for at in range(q * part, (q + 1) * part, tall):
            here = slice(at, at + tall)
            out = mid_refs[p % 2][here, :lanes]
            state(p)[2][here, :] = out.astype(BF16)
            for t in range(TASKS if shared else 1):
                span = slice(t * rows, (t + 1) * rows) if shared else slice(0, lanes)
                acc_ref[here, span] += gate[:, span] * out

    pipeline(GROUP, tiles, (start_pre, bend, start_out, combine))


def backward_wave(shared, rows, wave, aug_ref, inner_ref, outer_ref, state, gate_ref, dy_ref, acc_ref, dgate_ref, slab_ref, bias_ref, dout_ref, dpre_ref, work):
    lanes = rows if shared else rows * TASKS
    tiles = lanes // 256
    part = WIDTH // tiles
    tall = 16 * 1024 // lanes
    tasks = TASKS if shared else 1
    spans = [slice(t * rows, (t + 1) * rows) if shared else slice(0, lanes) for t in range(tasks)]
    kept = {}

    def share(p, q):
        e = pl.ds(wave * GROUP + p, 1)
        if q == 0:
            kept["gate", p] = gate_ref[e, :]
            kept["sum", p] = [None] * tasks
        gate, sums = kept["gate", p], kept["sum", p]
        for at in range(q * part, (q + 1) * part, tall):
            here = slice(at, at + tall)
            dys = [dy_ref[here, s] for s in spans]
            dout = gate[:, spans[0]] * dys[0]
            if shared:
                dout = dout + gate[:, spans[1]] * dys[1]
            dout_ref[p, here, :] = dout.astype(BF16)
            out = state(p)[2][here, :].astype(F32)
            for t in range(tasks):
                term = jnp.sum((out * dys[t]).reshape(tall // 8, 8, -1), axis=0)
                sums[t] = term if at == 0 else sums[t] + term
        if q == tiles - 1:
            for t in range(tasks):
                dgate_ref[e, spans[t]] = jnp.sum(sums[t], axis=0, keepdims=True)

    def back_out(p, q):
        span = slice(q * 256, (q + 1) * 256)
        work[p % 2][:, span] = nn(outer_ref[p], dout_ref[p, :, span])

    def unbend(p, q):
        slope_ref = state(p)[1]
        for at in range(q * part, (q + 1) * part, tall):
            here = slice(at, at + tall)
            dpre = work[p % 2][here, :lanes] * slope_ref[here, :].astype(F32)
            dpre_ref[p * HID + at : p * HID + at + tall, :] = dpre.astype(BF16)

    def grads(p, q):
        if q == 0:
            grad = nt(state(p)[0][...], dout_ref[p])
            slab_ref[p, :HID] = grad[:, :128]
            slab_ref[p, 512 : 512 + HID] = grad[:, 128:]
        if q == tiles // 2:
            grad = nt(aug_ref[...], dpre_ref[p * HID : (p + 1) * HID, :])
            slab_ref[p, HID:512] = grad[:WIDTH, :128]
            slab_ref[p, 512 + HID :] = grad[:WIDTH, 128:]
            bias_ref[0, p : p + 1, :] = grad[WIDTH : WIDTH + 1]

    pipeline(GROUP, tiles, (share, back_out, unbend, grads))
    acc_ref[...] += nn(inner_ref[...], dpre_ref[...])


def finish(shared, rows, u, codes_ref, mixing_ref, outer_bias_ref, code_ref, mix_ref, gate_ref, dy_ref, dgate_ref, acc_ref, dcode_ref, dmix_ref, rest_ref):
    dcode_ref[...] = jnp.zeros_like(dcode_ref)
    dmix_ref[...] = jnp.zeros_like(dmix_ref)
    outer_bias = outer_bias_ref[...]
    for t in range(TASKS):
        span = slice(t * rows, (t + 1) * rows)
        here = task_lanes(t, rows, shared)
        hi, mid, low = pieces(dy_ref[:, span])
        upto = nn(outer_bias, hi) + nn(outer_bias, mid) + nn(outer_bias, low)
        code, mix = task_rows(code_ref, mix_ref, t, here)
        grad_code, grad_mix = gate_back(code, mix, dgate_ref[:, span] + upto)
        for k in range(16):
            dcode_ref[t * 16 + k : t * 16 + k + 1, here] = grad_code[k]
        for k in range(4):
            dmix_ref[t * 4 + k : t * 4 + k + 1, here] = grad_mix[k]
    dcode = dcode_ref[...].astype(BF16)
    dmix = dmix_ref[...].astype(BF16)
    rest_ref[:32, :] = nt(dcode, u)
    rest_ref[32:40, :] = nt(dmix, u)
    g_hi, g_mid, _ = pieces(gate_ref[...])
    y_hi, y_mid, _ = pieces(dy_ref[...])
    rest_ref[40:56, :] = nt(g_hi, y_hi) + nt(g_hi, y_mid) + nt(g_mid, y_hi)
    return acc_ref[...] + tn(codes_ref[...], dcode) + tn(mixing_ref[...], dmix)


def extend(aug_ref, u):
    aug_ref[:WIDTH, :] = u
    one = lax.broadcasted_iota(jnp.int32, (16, u.shape[1]), 0) == 0
    aug_ref[WIDTH:, :] = jnp.where(one, 1.0, 0.0).astype(BF16)


def first_kernel(rows, tokens_ref, codes_ref, mixing_ref, inner_ref, bias_ref, outer_ref, outer_bias_ref, *refs):
    (hid_ref, slope_ref, out_ref, gate_ref, code_ref, mix_ref, turned, next_ref, acc_ref), work = refs[:9], refs[9:]
    step = pl.program_id(0)

    @pl.when(step == 0)
    def _():
        turned[...] = tokens_ref[...].astype(F32).T.astype(BF16)
        prepare(True, rows, turned[...], codes_ref, mixing_ref, outer_bias_ref, code_ref, mix_ref, gate_ref, acc_ref)

    def state(p):
        return hid_ref.at[p], slope_ref.at[p], out_ref.at[p]

    forward_wave(True, rows, step, turned, inner_ref, bias_ref, outer_ref, state, gate_ref, acc_ref, work)

    @pl.when(step == WAVES - 1)
    def _():
        next_ref[...] = acc_ref[...].astype(BF16)


def first_part(tokens, codes, mixing, inner, inner_bias, outer, outer_bias):
    rows = tokens.shape[0]
    wide = rows * TASKS
    state = jax.ShapeDtypeStruct((EXPERTS, HID, rows), BF16)
    plain = [
        jax.ShapeDtypeStruct((EXPERTS, wide), F32),
        jax.ShapeDtypeStruct((32, rows), F32),
        jax.ShapeDtypeStruct((8, rows), F32),
        jax.ShapeDtypeStruct((WIDTH, rows), BF16),
        jax.ShapeDtypeStruct((WIDTH, wide), BF16),
    ]
    state_spec = pl.BlockSpec((GROUP, HID, rows), lambda i: (i, 0, 0))
    return pl.pallas_call(
        functools.partial(first_kernel, rows),
        grid=(WAVES,),
        in_specs=[
            whole(tokens.shape),
            whole(codes.shape),
            whole(mixing.shape),
            pl.BlockSpec((WIDTH, GROUP * HID), lambda i: (0, i)),
            pl.BlockSpec((1, GROUP, HID), lambda i: (i, 0, 0)),
            pl.BlockSpec((GROUP, HID, WIDTH), lambda i: (i, 0, 0)),
            whole(outer_bias.shape),
        ],
        out_specs=[state_spec] * 3 + [whole(s.shape) for s in plain],
        out_shape=[state] * 3 + plain,
        scratch_shapes=[pltpu.VMEM((WIDTH, wide), F32)] + [pltpu.VMEM((HID, rows), F32)] * 4,
        cost_estimate=pl.CostEstimate(flops=8_000_000_000, bytes_accessed=20_000_000, transcendentals=0),
        compiler_params=pltpu.CompilerParams(
            dimension_semantics=("arbitrary",), vmem_limit_bytes=BYTES
        ),
        name="first_part",
    )(tokens, codes, mixing, inner, inner_bias.reshape(WAVES, GROUP, HID), outer, outer_bias)


def main_kernel(rows, core_ref, *refs):
    (u_ref, codes_two, mixing_two, inner_two, bias_two, outer_two, outer_bias_two), refs = refs[:7], refs[7:]
    tower_in, refs = refs[:8], refs[8:]
    (send_ref, keep_ref, grad_bias, rest_ref, dy_one), refs = refs[:5], refs[5:]
    tower_out, refs = refs[:3], refs[3:]
    (hid_two, slope_two, out_two, gate_two, code_two, mix_two, aug, v_ref), refs = refs[:8], refs[8:]
    (acc_ref, dy_two, dgate_ref, dcode_ref, dmix_ref, dout_ref, dpre_ref), work = refs[:7], refs[7:]
    step = pl.program_id(0)

    def state_two(wave):
        return lambda p: tuple(r.at[wave * GROUP + p] for r in (hid_two, slope_two, out_two))

    @pl.when(step == 0)
    def _():
        extend(aug, u_ref[...])
        prepare(False, rows, u_ref[...], codes_two, mixing_two, outer_bias_two, code_two, mix_two, gate_two, acc_ref)

    @pl.when(step < WAVES)
    def _():
        forward_wave(False, rows, step, aug, inner_two, bias_two, outer_two, state_two(step), gate_two, acc_ref, work)

    @pl.when(step == WAVES)
    def _():
        v_ref[...] = acc_ref[...].astype(BF16)
        tower(rows, v_ref, *tower_in, *tower_out, dy_two)
        acc_ref[...] = jnp.zeros_like(acc_ref)

    def back(slab_ref):
        wave = (step + 2 * (1 - core_ref[0])) % WAVES
        backward_wave(False, rows, wave, aug, inner_two, outer_two, state_two(wave), gate_two, dy_two, acc_ref, dgate_ref, slab_ref, grad_bias, dout_ref, dpre_ref, work)

    @pl.when((step >= WAVES) & (step < WAVES + 2))
    def _():
        back(send_ref)

    @pl.when(step >= WAVES + 2)
    def _():
        back(keep_ref)

    @pl.when(step == 2 * WAVES - 1)
    def _():
        dy_one[...] = finish(False, rows, u_ref[...], codes_two, mixing_two, outer_bias_two, code_two, mix_two, gate_two, dy_two, dgate_ref, acc_ref, dcode_ref, dmix_ref, rest_ref)


def fixed(shape):
    return pl.BlockSpec(shape, lambda i, core: (0,) * len(shape))


def main_part(core, u, codes, mixing, inner, inner_bias, outer, outer_bias, tower_in):
    wide = u.shape[1]
    rows = wide // TASKS

    def order(i, core):
        return jnp.where(i < WAVES, i, (i + 2 * (1 - core[0])) % WAVES)

    def back(i, core):
        return (jnp.maximum(i, WAVES) + 2 * (1 - core[0])) % WAVES

    slab = jax.ShapeDtypeStruct((EXPERTS // 2, SLAB, 128), F32)

    def slab_spec(begin):
        return pl.BlockSpec((GROUP, SLAB, 128), lambda i, core: (jnp.clip(i - begin, 0, 1), 0, 0))

    rest = [
        jax.ShapeDtypeStruct((56, WIDTH), F32),
        jax.ShapeDtypeStruct((WIDTH, wide), F32),
        jax.ShapeDtypeStruct((TASKS, rows), F32),
        jax.ShapeDtypeStruct((8, TOWER), F32),
        jax.ShapeDtypeStruct((TASKS, WIDTH, TOWER), F32),
    ]
    tower_specs = [fixed(a.shape) for a in tower_in]
    tower_specs[3] = pl.BlockSpec(memory_space=pltpu.SMEM)
    return pl.pallas_call(
        functools.partial(main_kernel, rows),
        grid_spec=pltpu.PrefetchScalarGridSpec(
            num_scalar_prefetch=1,
            grid=(2 * WAVES,),
            in_specs=[
                fixed(u.shape),
                fixed(codes.shape),
                fixed(mixing.shape),
                pl.BlockSpec((WIDTH, GROUP * HID), lambda i, core: (0, order(i, core))),
                pl.BlockSpec((1, GROUP, HID), lambda i, core: (order(i, core), 0, 0)),
                pl.BlockSpec((GROUP, HID, WIDTH), lambda i, core: (order(i, core), 0, 0)),
                fixed(outer_bias.shape),
            ]
            + tower_specs,
            out_specs=[slab_spec(WAVES), slab_spec(WAVES + 2)]
            + [pl.BlockSpec((1, GROUP, HID), lambda i, core: (back(i, core), 0, 0))]
            + [fixed(s.shape) for s in rest],
            scratch_shapes=[
                *[pltpu.VMEM((EXPERTS, HID, wide), BF16)] * 3,
                pltpu.VMEM((EXPERTS, wide), F32),
                pltpu.VMEM((32, wide), F32),
                pltpu.VMEM((8, wide), F32),
                pltpu.VMEM((WIDTH + 16, wide), BF16),
                pltpu.VMEM((WIDTH, wide), BF16),
                pltpu.VMEM((WIDTH, wide), F32),
                pltpu.VMEM((WIDTH, wide), F32),
                pltpu.VMEM((EXPERTS, wide), F32),
                pltpu.VMEM((32, wide), F32),
                pltpu.VMEM((8, wide), F32),
                pltpu.VMEM((GROUP, WIDTH, wide), BF16),
                pltpu.VMEM((GROUP * HID, wide), BF16),
                *[pltpu.VMEM((HID, wide), F32)] * 4,
            ],
        ),
        out_shape=[slab, slab, jax.ShapeDtypeStruct((WAVES, GROUP, HID), F32)] + rest,
        cost_estimate=pl.CostEstimate(flops=14_000_000_000, bytes_accessed=40_000_000, transcendentals=0),
        compiler_params=pltpu.CompilerParams(
            dimension_semantics=("arbitrary",), vmem_limit_bytes=BYTES
        ),
        name="main_part",
    )(
        core,
        u,
        codes,
        mixing,
        inner,
        inner_bias.reshape(WAVES, GROUP, HID),
        outer,
        outer_bias,
        *tower_in,
    )


def last_kernel(sending, rows, core_ref, *refs):
    (u_ref, inner_ref, outer_ref, hid_ref, slope_ref, out_ref, gate_ref, dy_ref), refs = refs[:8], refs[8:]
    step = pl.program_id(0)
    if sending:
        (slab_ref, bias_ref, acc_ref, dgate_ref), refs = refs[:4], refs[4:]
        aug, dout_ref, dpre_ref, *work = refs
        wave = step + 2 * (1 - core_ref[0])
        bias_at = bias_ref
    else:
        (acc_in, dgate_in, codes_ref, mixing_ref, outer_bias_ref, code_ref, mix_ref), refs = refs[:7], refs[7:]
        (other_bias, bias_two, rest_two, little, tower_inner), refs = refs[:5], refs[5:]
        (slab_ref, back_ref, small_send, small_keep), refs = refs[:4], refs[4:]
        aug, dout_ref, dpre_ref, acc_ref, dgate_ref, dcode_ref, dmix_ref, bias_ref, rest_ref, small_ref, *work = refs
        wave = step + 2 * core_ref[0]
        bias_at = bias_ref.at[pl.ds(step, 1)]

    @pl.when(step == 0)
    def _():
        extend(aug, u_ref[...])
        if sending:
            acc_ref[...] = jnp.zeros_like(acc_ref)
            dgate_ref[...] = jnp.zeros_like(dgate_ref)
        else:
            acc_ref[...] = acc_in[...]
            dgate_ref[...] = dgate_in[...]

    def state(p):
        return hid_ref.at[p], slope_ref.at[p], out_ref.at[p]

    backward_wave(True, rows, wave, aug, inner_ref, outer_ref, state, gate_ref, dy_ref, acc_ref, dgate_ref, slab_ref, bias_at, dout_ref, dpre_ref, work)
    if sending:
        return

    @pl.when(step == 1)
    def _():
        du = finish(True, rows, u_ref[...], codes_ref, mixing_ref, outer_bias_ref, code_ref, mix_ref, gate_ref, dy_ref, dgate_ref, acc_ref, dcode_ref, dmix_ref, rest_ref)
        back_ref[...] = du.T
        core = core_ref[0]
        small_ref[0:256, :] = tower_inner[0]
        small_ref[256:512, :] = tower_inner[1]
        small_ref[808:, :] = jnp.zeros((SMALL - 808, 128), F32)
        for at, ref in ((512, rest_ref), (624, rest_two)):
            small_ref[at : at + 56, :] = ref[:, :128]
            small_ref[at + 56 : at + 112, :] = ref[:, 128:]
        for w in range(WAVES):
            mine, j = core == w // 2, w % 2
            rows_one = jnp.where(mine, bias_ref[j], other_bias[w])
            for at, found in ((736, rows_one), (768, bias_two[w])):
                at += GROUP * w
                small_ref[at : at + GROUP, :] = found[:, :128]
                small_ref[at + 16 : at + 16 + GROUP, :] = found[:, 128:]
        small_ref[800:808, :] = little[...]
        small_send[...] = small_ref[pl.ds((1 - core) * 512, 512), :]
        small_keep[...] = small_ref[pl.ds(core * 512, 512), :]


def last_part(sending, core, u, inner, outer, state, gate, dy, more):
    rows = u.shape[1]

    def wave(i, core):
        return i + 2 * (1 - core[0] if sending else core[0])

    state_spec = pl.BlockSpec((GROUP, HID, rows), lambda i, core: (wave(i, core), 0, 0))
    arrays = [u, inner, outer, *state, gate, dy, *more]
    in_specs = [
        fixed(u.shape),
        pl.BlockSpec((WIDTH, GROUP * HID), lambda i, core: (0, wave(i, core))),
        pl.BlockSpec((GROUP, HID, WIDTH), lambda i, core: (wave(i, core), 0, 0)),
        state_spec,
        state_spec,
        state_spec,
    ]
    in_specs += [fixed(a.shape) for a in arrays[6:]]
    out_shape = [jax.ShapeDtypeStruct((EXPERTS // 2, SLAB, 128), F32)]
    out_specs = [pl.BlockSpec((GROUP, SLAB, 128), lambda i, core: (i, 0, 0))]
    scratch = [
        pltpu.VMEM((WIDTH + 16, rows), BF16),
        pltpu.VMEM((GROUP, WIDTH, rows), BF16),
        pltpu.VMEM((GROUP * HID, rows), BF16),
    ]
    if sending:
        out_shape.append(jax.ShapeDtypeStruct((WAVES, GROUP, HID), F32))
        out_specs.append(pl.BlockSpec((1, GROUP, HID), lambda i, core: (wave(i, core), 0, 0)))
        added = [
            jax.ShapeDtypeStruct((WIDTH, rows), F32),
            jax.ShapeDtypeStruct((EXPERTS, TASKS * rows), F32),
        ]
    else:
        added = [
            jax.ShapeDtypeStruct((rows, WIDTH), F32),
            jax.ShapeDtypeStruct((SMALL // 2, 128), F32),
            jax.ShapeDtypeStruct((SMALL // 2, 128), F32),
        ]
        scratch += [
            pltpu.VMEM((WIDTH, rows), F32),
            pltpu.VMEM((EXPERTS, TASKS * rows), F32),
            pltpu.VMEM((32, rows), F32),
            pltpu.VMEM((8, rows), F32),
            pltpu.VMEM((2, GROUP, HID), F32),
            pltpu.VMEM((56, WIDTH), F32),
            pltpu.VMEM((SMALL, 128), F32),
        ]
    scratch += [pltpu.VMEM((HID, rows), F32)] * 2
    out_shape += added
    out_specs += [fixed(s.shape) for s in added]
    return pl.pallas_call(
        functools.partial(last_kernel, sending, rows),
        grid_spec=pltpu.PrefetchScalarGridSpec(
            num_scalar_prefetch=1,
            grid=(2,),
            in_specs=in_specs,
            out_specs=out_specs,
            scratch_shapes=scratch,
        ),
        out_shape=out_shape,
        cost_estimate=pl.CostEstimate(flops=8_000_000_000, bytes_accessed=20_000_000, transcendentals=0),
        compiler_params=pltpu.CompilerParams(
            dimension_semantics=("arbitrary",), vmem_limit_bytes=40 * 1024 * 1024
        ),
        name="last_send" if sending else "last_keep",
    )(core, *arrays)


def place(chip, core):
    found = []
    for axes in AXES:
        halves = []
        for shift in axes:
            low, high = (chip >> shift) & 1, (chip >> (shift + 1)) & 1
            halves += [jnp.where(core == 0, low ^ high, high), jnp.where(core == 0, high, low)]
        found.append(halves)
    return found


def swaps(shift, step):
    pairs = []
    for chip in range(64):
        c = (chip >> shift) & 3
        for core in range(2):
            n = c ^ 1 if (core + step) % 2 == 0 else 3 - c
            pairs.append((chip * 2 + core, (chip + ((n - c) << shift)) * 2 + core))
    return pairs


def swap(step, sent):
    return [
        lax.ppermute(s, ("chip", "core"), swaps(axes[step // 2], step))
        for s, axes in zip(sent, AXES)
    ]


def plain_call(kernel, sizes, name, chip, core, *arrays, scratch=()):
    smem = pl.BlockSpec(memory_space=pltpu.SMEM)
    vmem = pl.BlockSpec(memory_space=pltpu.VMEM)
    return pl.pallas_call(
        kernel,
        in_specs=[smem, smem] + [vmem] * len(arrays),
        out_specs=[vmem] * len(sizes),
        out_shape=[jax.ShapeDtypeStruct((n, 128), F32) for n in sizes],
        scratch_shapes=scratch,
        cost_estimate=pl.CostEstimate(flops=0, bytes_accessed=2_000_000, transcendentals=0),
        compiler_params=pltpu.CompilerParams(vmem_limit_bytes=28 * 1024 * 1024),
        name=name,
    )(chip, core, *arrays)


def span(at, h, size):
    return pl.ds(pl.multiple_of(at + h * size, 8), size)


def open_kernel(counts, with_small, chip_ref, core_ref, keep_ref, got_ref, *refs):
    if with_small:
        (small_keep, small_got), refs = refs[:2], refs[2:]
        tail_ref = refs[-1]
        tail_ref[:2048, :] = keep_ref[6144:, :] + got_ref[6144:, :]
        tail_ref[2048:, :] = small_keep[...] + small_got[...]
    places = place(chip_ref[0], core_ref[0])
    at = kept = 0
    for i, m in enumerate(counts):
        size, h = 32 * m, places[i][0]

        def read(h):
            if with_small and i == 2:
                return tail_ref[span(0, h, size), :]
            return keep_ref[span(at, h, size), :] + got_ref[span(at, h, size), :]

        refs[i][...] = read(1 - h)
        refs[3][kept : kept + size, :] = read(h)
        at, kept = at + 2 * size, kept + size


def open_rows(counts, chip, core, keep, got, *small):
    sizes = [32 * m for m in counts]
    return plain_call(
        functools.partial(open_kernel, counts, bool(small)),
        sizes + [sum(sizes)],
        "open_one" if small else "open_two",
        chip,
        core,
        keep.reshape(HALF_ROWS, 128),
        got.reshape(HALF_ROWS, 128),
        *small,
        scratch=[pltpu.VMEM((2560, 128), F32)] if small else [],
    )


def halve_kernel(step, sizes, chip_ref, core_ref, keep_ref, *refs):
    got, sent, kept_ref = refs[:3], refs[3:6], refs[6]
    places = place(chip_ref[0], core_ref[0])
    at = kept = 0
    for i, size in enumerate(sizes):
        half, h = size // 2, places[i][step]
        sent[i][...] = keep_ref[span(at, 1 - h, half), :] + got[i][span(0, 1 - h, half), :]
        kept_ref[kept : kept + half, :] = keep_ref[span(at, h, half), :] + got[i][span(0, h, half), :]
        at, kept = at + size, kept + half


def halve(step, sizes, chip, core, keep, got):
    halves = [s // 2 for s in sizes]
    return plain_call(
        functools.partial(halve_kernel, step, sizes),
        halves + [sum(halves)],
        "halve_%d" % step,
        chip,
        core,
        keep,
        *got,
    )


def blend_kernel(chip_ref, core_ref, one_ref, two_ref, *refs):
    got_one, got_two, sent, kept_ref = refs[:3], refs[3:6], refs[6:9], refs[9]
    places = place(chip_ref[0], core_ref[0])
    at_one = at_two = 0
    for i in range(3):
        h = places[i][2]
        for ref, got, at, m, begin in (
            (one_ref, got_one[i], at_one, ONE[i], 0),
            (two_ref, got_two[i], at_two, TWO[i], ONE[i]),
        ):
            for k in range(8):
                for side, out, base in ((1 - h, sent[i], 0), (h, kept_ref, 704 * i)):
                    start = pl.multiple_of(side * (8 * m) + m * k, 8)
                    value = ref[pl.ds(at + start, m), :] + got[pl.ds(start, m), :]
                    out[base + CHUNK * k + begin : base + CHUNK * k + begin + m, :] = value
        at_one, at_two = at_one + 16 * ONE[i], at_two + 16 * TWO[i]


def blend(chip, core, one, two, got_one, got_two):
    return plain_call(
        blend_kernel, [704] * 3 + [2112], "blend", chip, core, one, two, *got_one, *got_two
    )


def close_kernel(chip_ref, core_ref, keep_ref, *refs):
    for i in range(3):
        refs[3 + i][...] = keep_ref[CHUNK * i : CHUNK * (i + 1), :] + refs[i][...]


def double_kernel(step, chip_ref, core_ref, *refs):
    places = place(chip_ref[0], core_ref[0])
    for i in range(3):
        own, got, out = refs[i], refs[3 + i], refs[6 + i]
        n, h = own.shape[0], places[i][step]
        out[span(0, h, n), :] = own[...]
        out[span(0, 1 - h, n), :] = got[...]


def double(step, chip, core, own, got):
    return plain_call(
        functools.partial(double_kernel, step),
        [2 * own[0].shape[0]] * 3,
        "double_%d" % step,
        chip,
        core,
        *own,
        *got,
    )


def layer_rows(layer):
    counts, begin = (ONE, (0, 0, 0)) if layer == 0 else (TWO, ONE)
    return [(i, counts[i], begin[i]) for i in range(3)]


def lay_kernel(mine, chip_ref, core_ref, *refs):
    own, got, refs = refs[:3], refs[3:6], refs[6:]
    if not mine:
        small_in, refs = refs[0], refs[5:]
    outs, refs = refs[:4], refs[4:]
    core = core_ref[0] if mine else 1 - core_ref[0]
    first = [p[0] for p in place(chip_ref[0], core)]
    step = pl.program_id(0)

    def rows_of(i, chunk, begin, count):
        lower = chunk < 32
        at = (chunk % 32) * CHUNK + begin
        a, b = own[i][at : at + count, :], got[i][at : at + count, :]
        return jnp.where((first[i] == 0) == lower, a, b)

    def put(layer, row, value):
        e, part, at = row // SLAB % PAIR, row // 256 % 4, row % 256
        count = value.shape[0]
        lanes = slice(128 * (part // 2), 128 * (part // 2 + 1))
        if part % 2 == 0:
            outs[2 * layer + 1][e, at : at + count, lanes] = value
        else:
            lanes = slice(e * HID + lanes.start, e * HID + lanes.stop)
            outs[2 * layer][at : at + count, lanes] = value

    for s in range(4):

        @pl.when(step == s)
        def _():
            for layer in range(2):
                base = 0
                for i, m, begin in layer_rows(layer):
                    for chunk in range(64):
                        row = base + chunk * m
                        low, high = max(row, s * 2 * SLAB), min(row + m, (s + 1) * 2 * SLAB)
                        while low < high:
                            stop = min(high, (low // 256 + 1) * 256)
                            put(layer, low, rows_of(i, chunk, begin + low - row, stop - low))
                            low = stop
                    base += 64 * m

    def small_rows():
        found = []
        m = ONE[2]
        for chunk in range(64):
            row = 6144 + chunk * m
            low = max(row, HALF_ROWS)
            if low < row + m:
                found.append((low - HALF_ROWS, rows_of(2, chunk, low - row, row + m - low)))
        return found

    if mine:
        (small_out,) = refs

        @pl.when(step == 0)
        def _():
            for at, value in small_rows():
                small_out[at : at + value.shape[0], :] = value

        return

    codes_one, mix_one, back_one, bias_one = refs[:4]
    codes_two, mix_two, back_two, bias_two = refs[4:8]
    tower_inner, tower_bias, tower_outer, tower_last, acc_ref = refs[8:]

    @pl.when(step == 0)
    def _():
        half = 512 * core
        acc_ref[pl.ds(pl.multiple_of(512 - half, 8), 512), :] = small_in[...]
        for at, value in small_rows():
            acc_ref[pl.ds(pl.multiple_of(half + at, 8), value.shape[0]), :] = value
        tower_inner[0] = acc_ref[0:256, :]
        tower_inner[1] = acc_ref[256:512, :]
        for s in range(2):
            lanes = slice(s * 128, (s + 1) * 128)
            for at, codes, mix, back in (
                (512, codes_one, mix_one, back_one),
                (624, codes_two, mix_two, back_two),
            ):
                at += 56 * s
                codes[:, lanes] = acc_ref[at : at + 32, :]
                mix[:, lanes] = acc_ref[at + 32 : at + 40, :]
                back[:, lanes] = acc_ref[at + 40 : at + 56, :]
            bias_one[:, lanes] = acc_ref[736 + 16 * s : 752 + 16 * s, :]
            bias_two[:, lanes] = acc_ref[768 + 16 * s : 784 + 16 * s, :]
        tower_outer[...] = acc_ref[800:802, :]
        tower_bias[...] = acc_ref[802:804, :]
        lane = lax.broadcasted_iota(jnp.int32, (1, 128), 1)
        tower_last[...] = jnp.where(lane == 0, acc_ref[804:805, :], acc_ref[805:806, :])


def lay(mine, chip, core, own, got, more):
    def at(core):
        return core[0] if mine else 1 - core[0]

    shapes = [(WIDTH, EXPERTS * HID), (EXPERTS, HID, WIDTH)] * 2
    out_specs = [
        pl.BlockSpec((WIDTH, PAIR * HID), lambda i, chip, core: (0, 4 * at(core) + i)),
        pl.BlockSpec((PAIR, HID, WIDTH), lambda i, chip, core: (4 * at(core) + i, 0, 0)),
    ] * 2

    def still(shape):
        return pl.BlockSpec(shape, lambda i, chip, core: (0,) * len(shape))

    in_specs = [still(a.shape) for a in (*own, *got)]
    if mine:
        little = [(SMALL // 2, 128)]
        scratch, aliases = [], {}
    else:
        in_specs += [still(more[0].shape)] + [pl.BlockSpec(memory_space=pl.ANY)] * 4
        aliases = {9: 0, 10: 1, 11: 2, 12: 3}
        little = [(32, WIDTH), (8, WIDTH), (EXPERTS, WIDTH), (EXPERTS, HID)] * 2
        little += [(TASKS, WIDTH, TOWER), (TASKS, TOWER), (TASKS, TOWER), (1, 128)]
        scratch = [pltpu.VMEM((SMALL, 128), F32)]
    shapes += little
    out_specs += [still(s) for s in little]
    return pl.pallas_call(
        functools.partial(lay_kernel, mine),
        grid_spec=pltpu.PrefetchScalarGridSpec(
            num_scalar_prefetch=2,
            grid=(4,),
            in_specs=in_specs,
            out_specs=out_specs,
            scratch_shapes=scratch,
        ),
        out_shape=[jax.ShapeDtypeStruct(s, F32) for s in shapes],
        input_output_aliases=aliases,
        cost_estimate=pl.CostEstimate(flops=0, bytes_accessed=16_000_000, transcendentals=0),
        compiler_params=pltpu.CompilerParams(
            dimension_semantics=("arbitrary",), vmem_limit_bytes=32 * 1024 * 1024
        ),
        name="lay_own" if mine else "lay_other",
    )(chip, core, *own, *got, *more)


def on_device(
    tokens,
    labels,
    lengths,
    codes_one,
    mixing_one,
    inner_one,
    inner_bias_one,
    outer_one,
    outer_bias_one,
    codes_two,
    mixing_two,
    inner_two,
    inner_bias_two,
    outer_two,
    outer_bias_two,
    tower_inner,
    tower_inner_bias,
    tower_outer,
    tower_outer_bias,
):
    rows = tokens.shape[0]
    core = lax.axis_index("core").astype(jnp.int32).reshape(1)
    chip = lax.axis_index("chip").astype(jnp.int32).reshape(1)
    base = (lax.axis_index(("chip", "core")) * rows).astype(jnp.int32).reshape(1)

    def cross(a):
        return lax.ppermute(a, "core", [(0, 1), (1, 0)])

    codes_one, mixing_one, codes_two, mixing_two = (
        codes_one.T,
        mixing_one.T,
        codes_two.T,
        mixing_two.T,
    )
    count = jnp.sum(labels.astype(F32), axis=0)
    sent = jnp.broadcast_to(jnp.pad(count, (0, 126))[None, :], (128, 128))
    counts = lax.all_to_all(sent, ("chip", "core"), 0, 0, tiled=True)
    *state, gate, code, mix, u, u_two = first_part(
        tokens, codes_one, mixing_one, inner_one, inner_bias_one, outer_one, outer_bias_one
    )
    towers = (tower_inner, tower_inner_bias, tower_outer, tower_outer_bias.reshape(1, TASKS))
    towers = (labels.T, counts, lengths.reshape(1, -1), base, *towers)
    send, keep_two, bias_two, rest_two, dy, predictions, little, grad_tower_inner = main_part(
        core, u_two, codes_two, mixing_two, inner_two, inner_bias_two, outer_two, outer_bias_two, towers
    )
    got_two = cross(send)
    send, bias_one, acc, dgate = last_part(
        True, core, u, inner_one, outer_one, state, gate, dy, ()
    )
    got_one = cross(send)
    *sent, kept_two = open_rows(TWO, chip, core, keep_two, got_two)
    got_two = swap(0, sent)
    more = (acc, dgate, codes_one, mixing_one, outer_bias_one, code, mix)
    more += (bias_one, bias_two, rest_two, little, grad_tower_inner)
    keep_one, grad_tokens, small_send, small_keep = last_part(
        False, core, u, inner_one, outer_one, state, gate, dy, more
    )
    small_got = cross(small_send)
    *got_two, keep_one = lax.optimization_barrier((*got_two, keep_one))
    *sent, kept_two = halve(1, [32 * m for m in TWO], chip, core, kept_two, got_two)
    got_two = swap(1, sent)
    *sent, kept_one = open_rows(ONE, chip, core, keep_one, got_one, small_keep, small_got)
    got_one = swap(0, sent)
    *sent, kept_one = halve(1, [32 * m for m in ONE], chip, core, kept_one, got_one)
    got_one = swap(1, sent)
    *sent, kept = blend(chip, core, kept_one, kept_two, got_one, got_two)
    for step in (3, 4, 5):
        got = swap(step - 1, sent)
        *sent, kept = halve(step, [CHUNK * 64 >> step] * 3, chip, core, kept, got)
    got = swap(5, sent)
    own = plain_call(close_kernel, [CHUNK] * 3, "close", chip, core, kept, *got)
    for step in (5, 4, 3, 2, 1):
        own = double(step, chip, core, own, swap(step, own))
    got = swap(0, own)
    own_other = [cross(a) for a in own]
    got_other = [cross(a) for a in got]
    *found, small = lay(True, chip, core, own, got, ())
    found = lay(False, chip, core, own_other, got_other, (small, *found))
    inner_one, outer_one, inner_two, outer_two = found[:4]
    codes_one, mix_one, back_one, bias_one, codes_two, mix_two, back_two, bias_two = found[4:12]
    tower_inner, tower_bias, tower_outer, tower_last = found[12:]
    return (
        predictions.T,
        grad_tokens,
        codes_one.T,
        mix_one.T,
        inner_one,
        bias_one.reshape(-1),
        outer_one,
        back_one,
        codes_two.T,
        mix_two.T,
        inner_two,
        bias_two.reshape(-1),
        outer_two,
        back_two,
        tower_inner,
        tower_bias,
        tower_outer,
        tower_last[0, :2],
    )


def solution(mesh):
    chips = Mesh(mesh.devices.reshape(-1, 2), ("chip", "core"))
    rows, copied = P(("chip", "core"), None), P()
    return jax.shard_map(
        on_device,
        mesh=chips,
        in_specs=(rows, rows) + (copied,) * 17,
        out_specs=(rows, rows) + (copied,) * 16,
        check_vma=False,
    )
```

```python
import functools

import jax
import jax.numpy as jnp
from jax import lax
from jax.experimental import pallas as pl
from jax.experimental.pallas import tpu as pltpu
from jax.sharding import Mesh, PartitionSpec as P

EXPERTS = 16
SEL = 4
BITS = 4
TASKS = 2
WIDTH = 256
HID = 256
TOWER = 128
PAIR = 2
STEPS = EXPERTS // PAIR
HALF = STEPS // 2
GROUP = 4
WAVES = EXPERTS // GROUP
SLAB = 1024
SMALL = 672
SHARE = SMALL // 2
OWN = 144
HALF_ROWS = 8 * SLAB
ONE = (48, 48, 40)
TWO = (40, 40, 48)
CHUNK = 88
AXES = ((0, 4, 2), (4, 2, 0), (2, 0, 4))
F32 = jnp.float32
BF16 = jnp.bfloat16
ROOT = 0.7978845608028654
CUBE = 0.044715
MIB = 1024 * 1024


def nn(a, b):
    return lax.dot_general(a, b, (((1,), (0,)), ((), ())), preferred_element_type=F32)


def nt(a, b):
    return lax.dot_general(a, b, (((1,), (1,)), ((), ())), preferred_element_type=F32)


def tn(a, b):
    return lax.dot_general(a, b, (((0,), (0,)), ((), ())), preferred_element_type=F32)


def pieces(x):
    hi = x.astype(BF16)
    rest = x - hi.astype(F32)
    mid = rest.astype(BF16)
    return hi, mid, (rest - mid.astype(F32)).astype(BF16)


def gelu_both(x):
    square = x * x
    slope = square * (ROOT * CUBE) + ROOT
    s = 0.5 + 0.5 * jnp.tanh(x * slope)
    value = x * s
    return value, s + value * (1.0 - s) * (slope * 6.0 - 4.0 * ROOT)


def soft_parts(mix):
    top = jnp.maximum(jnp.maximum(mix[0], mix[1]), jnp.maximum(mix[2], mix[3]))
    raised = [jnp.exp(m - top) for m in mix]
    total = raised[0] + raised[1] + raised[2] + raised[3]
    return [r / total for r in raised]


def bit_factors(code):
    rows = code[0].shape[1]
    expert = lax.broadcasted_iota(jnp.int32, (EXPERTS, rows), 0)
    found = []
    for i in range(SEL):
        per_bit = []
        for b in range(BITS):
            k = jnp.clip(code[i * BITS + b], -5.0, 5.0)
            s = -0.002 * (k * k * k) + 0.15 * k + 0.5
            on = (expert >> b) & 1 == 1
            per_bit.append(jnp.where(on, s, 1.0 - s))
        found.append(per_bit)
    return found


def gate_of(code, mix):
    w = soft_parts(mix)
    total = None
    for i, f in enumerate(bit_factors(code)):
        r = w[i] * ((f[0] * f[1]) * (f[2] * f[3]))
        total = r if total is None else total + r
    return total


def gate_back(code, mix, grad):
    rows = grad.shape[1]
    expert = lax.broadcasted_iota(jnp.int32, (EXPERTS, rows), 0)
    w = soft_parts(mix)
    grad_w, grad_code = [], []
    for i, f in enumerate(bit_factors(code)):
        low, high = f[0] * f[1], f[2] * f[3]
        grad_w.append(jnp.sum(grad * (low * high), axis=0, keepdims=True))
        up = grad * w[i]
        others = (f[1] * high, f[0] * high, low * f[3], low * f[2])
        for b in range(BITS):
            on = (expert >> b) & 1 == 1
            term = up * others[b]
            ds = jnp.sum(jnp.where(on, term, -term), axis=0, keepdims=True)
            c = code[i * BITS + b]
            k = jnp.clip(c, -5.0, 5.0)
            inside = jnp.where(jnp.abs(c) <= 5.0, 0.15 - 0.006 * (k * k), 0.0)
            grad_code.append(ds * inside)
    mean = w[0] * grad_w[0] + w[1] * grad_w[1] + w[2] * grad_w[2] + w[3] * grad_w[3]
    return grad_code, [w[i] * (grad_w[i] - mean) for i in range(SEL)]


def task_rows(logits, mixes, task, lanes):
    code = [logits[task * 16 + k : task * 16 + k + 1, lanes] for k in range(16)]
    mix = [mixes[task * 4 + k : task * 4 + k + 1, lanes] for k in range(4)]
    return code, mix


def task_lanes(task, rows, shared):
    return slice(0, rows) if shared else slice(task * rows, (task + 1) * rows)


def whole(shape):
    return pl.BlockSpec(shape, lambda *_: (0,) * len(shape))


def tower(
    rows,
    v_ref,
    labels_ref,
    counts_ref,
    lengths_ref,
    base_ref,
    inner_ref,
    bias_ref,
    outer_ref,
    outer_bias_ref,
    predictions_ref,
    small_ref,
    grad_inner_ref,
    dy_ref,
):
    sessions = lengths_ref.shape[1]
    lens = jnp.broadcast_to(lengths_ref[...], (8, sessions)).astype(F32).astype(BF16)
    before = lax.broadcasted_iota(jnp.int32, (sessions, sessions), 0)
    after = lax.broadcasted_iota(jnp.int32, (sessions, sessions), 1)
    upto = jnp.where(before <= after, 1.0, 0.0).astype(BF16)
    ends = nn(lens, upto)[0:1, :]
    starts = ends - lens[0:1, :].astype(F32)
    ids = (lax.broadcasted_iota(jnp.int32, (rows, sessions), 0) + base_ref[0]).astype(F32)
    inside = jnp.where((ids >= starts) & (ids < ends), 1.0, 0.0).astype(BF16)
    row_length = nt(lens, inside)[0:1, :]
    all_rows = float(rows * counts_ref.shape[0])
    weight = (all_rows / sessions) / row_length
    positives = jnp.sum(counts_ref[...], axis=0, keepdims=True)
    bias = bias_ref[...].astype(F32).T
    columns = outer_ref[...].astype(F32).T
    small_ref[...] = jnp.zeros_like(small_ref)
    for t in range(TASKS):
        lanes = slice(t * rows, (t + 1) * rows)
        v = v_ref[:, lanes]
        pre = tn(inner_ref[t], v) + bias[:, t : t + 1]
        hid, slope = gelu_both(pre)
        hid = hid.astype(BF16)
        column = columns[:, t : t + 1]
        logit = jnp.sum(hid.astype(F32) * column, axis=0, keepdims=True)
        logit = logit + outer_bias_ref[0:1, t : t + 1].astype(F32)
        y = labels_ref[t : t + 1, :].astype(F32)
        count = positives[:, t : t + 1]
        ratio = (all_rows - count) / count
        chance = jax.nn.sigmoid(logit)
        predictions_ref[t : t + 1, :] = chance
        grad = weight * (-ratio * y * jax.nn.sigmoid(-logit) + (1.0 - y) * chance)
        grad = grad.astype(BF16)
        back = (grad.astype(F32) * column * slope).astype(BF16)
        picked = lax.broadcasted_iota(jnp.int32, (16, rows), 0)
        stack = jnp.where(picked == 0, grad.astype(F32), jnp.where(picked == 1, 1.0, 0.0))
        stack = stack.astype(BF16)
        by_hid = nt(stack, hid)
        by_back = nt(stack, back)
        small_ref[t : t + 1, :TOWER] = by_hid[0:1]
        small_ref[2 + t : 3 + t, :TOWER] = by_back[1:2]
        total = jnp.sum(grad.astype(F32), axis=1, keepdims=True)
        small_ref[4 + t : 5 + t, :TOWER] = jnp.broadcast_to(total, (1, TOWER))
        grad_inner_ref[t] = nt(v, back)
        dy_ref[:, lanes] = nn(inner_ref[t], back)


def pipeline(count, tiles, stages):
    for slot in range(count + len(stages) - 1):
        for q in range(tiles):
            for late, stage in enumerate(stages):
                if 0 <= slot - late < count:
                    stage(slot - late, q)


def prepare(shared, rows, u, codes_ref, mixing_ref, outer_bias_ref, code_ref, mix_ref, gate_ref, acc_ref):
    code_ref[...] = nn(codes_ref[...], u)
    mix_ref[...] = nn(mixing_ref[...], u)
    outer_bias = outer_bias_ref[...]
    for t in range(TASKS):
        code, mix = task_rows(code_ref, mix_ref, t, task_lanes(t, rows, shared))
        gate = gate_of(code, mix)
        span = slice(t * rows, (t + 1) * rows)
        gate_ref[:, span] = gate
        hi, mid, low = pieces(gate)
        acc_ref[:, span] = tn(outer_bias, hi) + tn(outer_bias, mid) + tn(outer_bias, low)


def forward_wave(shared, rows, wave, u_ref, inner_ref, bias_ref, outer_ref, state, gate_ref, acc_ref, work):
    bias = bias_ref[...].astype(F32).T
    lanes = rows if shared else rows * TASKS
    tiles = lanes // 256
    part = WIDTH // tiles
    tall = 16 * 1024 // lanes
    pre_refs, mid_refs = work[:2], work[2:]
    kept = {}

    def start_pre(p, q):
        if q == 0:
            kept["inner", p] = inner_ref[:, p * HID : (p + 1) * HID].T
        span = slice(q * 256, (q + 1) * 256)
        pre_refs[p % 2][:, span] = nn(kept["inner", p], u_ref[:WIDTH, span])

    def bend(p, q):
        hid_ref, slope_ref, _ = state(p)
        for at in range(q * part, (q + 1) * part, tall):
            here = slice(at, at + tall)
            half, top = at // 128, at % 128
            column = bias[top : top + tall, 2 * p + half : 2 * p + half + 1]
            hid, slope = gelu_both(pre_refs[p % 2][here, :lanes] + column)
            hid_ref[here, :] = hid.astype(BF16)
            slope_ref[here, :] = slope.astype(BF16)

    def start_out(p, q):
        if q == 0:
            kept["outer", p] = outer_ref[p].T
        span = slice(q * 256, (q + 1) * 256)
        mid_refs[p % 2][:, span] = nn(kept["outer", p], state(p)[0][:, span])

    def combine(p, q):
        if q == 0:
            kept["gate", p] = gate_ref[pl.ds(wave * GROUP + p, 1), :]
        gate = kept["gate", p]
        for at in range(q * part, (q + 1) * part, tall):
            here = slice(at, at + tall)
            out = mid_refs[p % 2][here, :lanes]
            state(p)[2][here, :] = out.astype(BF16)
            for t in range(TASKS if shared else 1):
                span = slice(t * rows, (t + 1) * rows) if shared else slice(0, lanes)
                acc_ref[here, span] += gate[:, span] * out

    pipeline(GROUP, tiles, (start_pre, bend, start_out, combine))


def backward_wave(shared, rows, wave, aug_ref, inner_ref, outer_ref, state, gate_ref, dy_ref, acc_ref, dgate_ref, slab_ref, bias_ref, dout_ref, dpre_ref, work):
    lanes = rows if shared else rows * TASKS
    tiles = lanes // 256
    part = WIDTH // tiles
    tall = 16 * 1024 // lanes
    tasks = TASKS if shared else 1
    spans = [slice(t * rows, (t + 1) * rows) if shared else slice(0, lanes) for t in range(tasks)]
    kept = {}

    def share(p, q):
        e = pl.ds(wave * GROUP + p, 1)
        if q == 0:
            kept["gate", p] = gate_ref[e, :]
            kept["sum", p] = [None] * tasks
        gate, sums = kept["gate", p], kept["sum", p]
        for at in range(q * part, (q + 1) * part, tall):
            here = slice(at, at + tall)
            dys = [dy_ref[here, s] for s in spans]
            dout = gate[:, spans[0]] * dys[0]
            if shared:
                dout = dout + gate[:, spans[1]] * dys[1]
            dout_ref[p, here, :] = dout.astype(BF16)
            out = state(p)[2][here, :].astype(F32)
            for t in range(tasks):
                term = jnp.sum((out * dys[t]).reshape(tall // 8, 8, -1), axis=0)
                sums[t] = term if at == 0 else sums[t] + term
        if q == tiles - 1:
            for t in range(tasks):
                dgate_ref[e, spans[t]] = jnp.sum(sums[t], axis=0, keepdims=True)

    def back_out(p, q):
        span = slice(q * 256, (q + 1) * 256)
        work[p % 2][:, span] = nn(outer_ref[p], dout_ref[p, :, span])

    def unbend(p, q):
        slope_ref = state(p)[1]
        for at in range(q * part, (q + 1) * part, tall):
            here = slice(at, at + tall)
            dpre = work[p % 2][here, :lanes] * slope_ref[here, :].astype(F32)
            dpre_ref[p * HID + at : p * HID + at + tall, :] = dpre.astype(BF16)

    def grads(p, q):
        if q == 0:
            grad = nt(state(p)[0][...], dout_ref[p])
            slab_ref[p, :HID] = grad[:, :128]
            slab_ref[p, 512 : 512 + HID] = grad[:, 128:]
        if q == tiles // 2:
            grad = nt(aug_ref[...], dpre_ref[p * HID : (p + 1) * HID, :])
            slab_ref[p, HID:512] = grad[:WIDTH, :128]
            slab_ref[p, 512 + HID :] = grad[:WIDTH, 128:]
            bias_ref[0, p : p + 1, :] = grad[WIDTH : WIDTH + 1]

    pipeline(GROUP, tiles, (share, back_out, unbend, grads))
    acc_ref[...] += nn(inner_ref[...], dpre_ref[...])


def finish(shared, rows, u, codes_ref, mixing_ref, outer_bias_ref, code_ref, mix_ref, gate_ref, dy_ref, dgate_ref, acc_ref, dcode_ref, dmix_ref, rest_ref):
    dcode_ref[...] = jnp.zeros_like(dcode_ref)
    dmix_ref[...] = jnp.zeros_like(dmix_ref)
    outer_bias = outer_bias_ref[...]
    for t in range(TASKS):
        span = slice(t * rows, (t + 1) * rows)
        here = task_lanes(t, rows, shared)
        hi, mid, low = pieces(dy_ref[:, span])
        upto = nn(outer_bias, hi) + nn(outer_bias, mid) + nn(outer_bias, low)
        code, mix = task_rows(code_ref, mix_ref, t, here)
        grad_code, grad_mix = gate_back(code, mix, dgate_ref[:, span] + upto)
        for k in range(16):
            dcode_ref[t * 16 + k : t * 16 + k + 1, here] = grad_code[k]
        for k in range(4):
            dmix_ref[t * 4 + k : t * 4 + k + 1, here] = grad_mix[k]
    dcode = dcode_ref[...].astype(BF16)
    dmix = dmix_ref[...].astype(BF16)
    rest_ref[:32, :] = nt(dcode, u)
    rest_ref[32:40, :] = nt(dmix, u)
    g_hi, g_mid, _ = pieces(gate_ref[...])
    y_hi, y_mid, _ = pieces(dy_ref[...])
    rest_ref[40:56, :] = nt(g_hi, y_hi) + nt(g_hi, y_mid) + nt(g_mid, y_hi)
    return acc_ref[...] + tn(codes_ref[...], dcode) + tn(mixing_ref[...], dmix)


def extend(aug_ref, u):
    aug_ref[:WIDTH, :] = u
    one = lax.broadcasted_iota(jnp.int32, (16, u.shape[1]), 0) == 0
    aug_ref[WIDTH:, :] = jnp.where(one, 1.0, 0.0).astype(BF16)


def first_kernel(rows, tokens_ref, codes_ref, mixing_ref, inner_ref, bias_ref, outer_ref, outer_bias_ref, *refs):
    (hid_ref, slope_ref, out_ref, gate_ref, code_ref, mix_ref, turned, next_ref, acc_ref), work = refs[:9], refs[9:]
    step = pl.program_id(0)

    @pl.when(step == 0)
    def _():
        turned[...] = tokens_ref[...].astype(F32).T.astype(BF16)
        prepare(True, rows, turned[...], codes_ref, mixing_ref, outer_bias_ref, code_ref, mix_ref, gate_ref, acc_ref)

    def state(p):
        return hid_ref.at[p], slope_ref.at[p], out_ref.at[p]

    forward_wave(True, rows, step, turned, inner_ref, bias_ref, outer_ref, state, gate_ref, acc_ref, work)

    @pl.when(step == WAVES - 1)
    def _():
        next_ref[...] = acc_ref[...].astype(BF16)


def first_part(tokens, codes, mixing, inner, inner_bias, outer, outer_bias):
    rows = tokens.shape[0]
    wide = rows * TASKS
    state = jax.ShapeDtypeStruct((EXPERTS, HID, rows), BF16)
    plain = [
        jax.ShapeDtypeStruct((EXPERTS, wide), F32),
        jax.ShapeDtypeStruct((32, rows), F32),
        jax.ShapeDtypeStruct((8, rows), F32),
        jax.ShapeDtypeStruct((WIDTH, rows), BF16),
        jax.ShapeDtypeStruct((WIDTH, wide), BF16),
    ]
    state_spec = pl.BlockSpec((GROUP, HID, rows), lambda i: (i, 0, 0))
    return pl.pallas_call(
        functools.partial(first_kernel, rows),
        grid=(WAVES,),
        in_specs=[
            whole(tokens.shape),
            whole(codes.shape),
            whole(mixing.shape),
            pl.BlockSpec((WIDTH, GROUP * HID), lambda i: (0, i)),
            pl.BlockSpec((2 * GROUP, 128), lambda i: (i, 0)),
            pl.BlockSpec((GROUP, HID, WIDTH), lambda i: (i, 0, 0)),
            whole(outer_bias.shape),
        ],
        out_specs=[state_spec] * 3 + [whole(s.shape) for s in plain],
        out_shape=[state] * 3 + plain,
        scratch_shapes=[pltpu.VMEM((WIDTH, wide), F32)] + [pltpu.VMEM((HID, rows), F32)] * 4,
        cost_estimate=pl.CostEstimate(flops=8_000_000_000, bytes_accessed=20_000_000, transcendentals=0),
        compiler_params=pltpu.CompilerParams(
            dimension_semantics=("arbitrary",), vmem_limit_bytes=61 * MIB
        ),
        name="first_part",
    )(tokens, codes, mixing, inner, inner_bias.reshape(2 * EXPERTS, 128), outer, outer_bias)


def main_kernel(rows, core_ref, *refs):
    (u_ref, codes_two, mixing_two, inner_two, bias_two, outer_two, outer_bias_two), refs = refs[:7], refs[7:]
    tower_in, refs = refs[:8], refs[8:]
    (send_ref, keep_ref, dy_one, predictions, small_send, small_keep), refs = refs[:6], refs[6:]
    (grad_bias, rest_ref, little, tower_inner, small_ref), refs = refs[:5], refs[5:]
    tower_out = (predictions, little, tower_inner)
    (hid_two, slope_two, out_two, gate_two, code_two, mix_two, aug, v_ref), refs = refs[:8], refs[8:]
    (acc_ref, dy_two, dgate_ref, dcode_ref, dmix_ref, dout_ref, dpre_ref), work = refs[:7], refs[7:]
    step = pl.program_id(0)

    def state_two(wave):
        return lambda p: tuple(r.at[wave * GROUP + p] for r in (hid_two, slope_two, out_two))

    @pl.when(step == 0)
    def _():
        extend(aug, u_ref[...])
        prepare(False, rows, u_ref[...], codes_two, mixing_two, outer_bias_two, code_two, mix_two, gate_two, acc_ref)

    @pl.when(step < WAVES)
    def _():
        forward_wave(False, rows, step, aug, inner_two, bias_two, outer_two, state_two(step), gate_two, acc_ref, work)

    @pl.when(step == WAVES)
    def _():
        v_ref[...] = acc_ref[...].astype(BF16)
        tower(rows, v_ref, *tower_in, *tower_out, dy_two)
        acc_ref[...] = jnp.zeros_like(acc_ref)

    def back(slab_ref):
        wave = (step + 2 * (1 - core_ref[0])) % WAVES
        backward_wave(False, rows, wave, aug, inner_two, outer_two, state_two(wave), gate_two, dy_two, acc_ref, dgate_ref, slab_ref, grad_bias.at[pl.ds(wave, 1)], dout_ref, dpre_ref, work)

    @pl.when((step >= WAVES) & (step < WAVES + 2))
    def _():
        back(send_ref)

    @pl.when(step >= WAVES + 2)
    def _():
        back(keep_ref)

    @pl.when(step == 2 * WAVES - 1)
    def _():
        dy_one[...] = finish(False, rows, u_ref[...], codes_two, mixing_two, outer_bias_two, code_two, mix_two, gate_two, dy_two, dgate_ref, acc_ref, dcode_ref, dmix_ref, rest_ref)
        small_ref[0:256, :] = tower_inner[0]
        small_ref[256:512, :] = tower_inner[1]
        small_ref[512:568, :] = rest_ref[:, :128]
        small_ref[568:624, :] = rest_ref[:, 128:]
        for w in range(WAVES):
            small_ref[624 + GROUP * w : 624 + GROUP * (w + 1), :] = grad_bias[w, :, :128]
            small_ref[640 + GROUP * w : 640 + GROUP * (w + 1), :] = grad_bias[w, :, 128:]
        small_ref[656:664, :] = little[...]
        small_ref[664:, :] = jnp.zeros((8, 128), F32)
        core = core_ref[0]
        small_send[...] = small_ref[pl.ds(pl.multiple_of((1 - core) * SHARE, 8), SHARE), :]
        small_keep[...] = small_ref[pl.ds(pl.multiple_of(core * SHARE, 8), SHARE), :]


def fixed(shape):
    return pl.BlockSpec(shape, lambda i, core: (0,) * len(shape))


def main_part(core, u, codes, mixing, inner, inner_bias, outer, outer_bias, tower_in):
    wide = u.shape[1]
    rows = wide // TASKS

    def order(i, core):
        return jnp.where(i < WAVES, i, (i + 2 * (1 - core[0])) % WAVES)

    slab = jax.ShapeDtypeStruct((EXPERTS // 2, SLAB, 128), F32)

    def slab_spec(begin):
        return pl.BlockSpec((GROUP, SLAB, 128), lambda i, core: (jnp.clip(i - begin, 0, 1), 0, 0))

    rest = [
        jax.ShapeDtypeStruct((WIDTH, wide), F32),
        jax.ShapeDtypeStruct((TASKS, rows), F32),
        jax.ShapeDtypeStruct((SHARE, 128), F32),
        jax.ShapeDtypeStruct((SHARE, 128), F32),
    ]
    tower_specs = [fixed(a.shape) for a in tower_in]
    tower_specs[3] = pl.BlockSpec(memory_space=pltpu.SMEM)
    return pl.pallas_call(
        functools.partial(main_kernel, rows),
        grid_spec=pltpu.PrefetchScalarGridSpec(
            num_scalar_prefetch=1,
            grid=(2 * WAVES,),
            in_specs=[
                fixed(u.shape),
                fixed(codes.shape),
                fixed(mixing.shape),
                pl.BlockSpec((WIDTH, GROUP * HID), lambda i, core: (0, order(i, core))),
                pl.BlockSpec((2 * GROUP, 128), lambda i, core: (order(i, core), 0)),
                pl.BlockSpec((GROUP, HID, WIDTH), lambda i, core: (order(i, core), 0, 0)),
                fixed(outer_bias.shape),
            ]
            + tower_specs,
            out_specs=[slab_spec(WAVES), slab_spec(WAVES + 2)]
            + [fixed(s.shape) for s in rest],
            scratch_shapes=[
                pltpu.VMEM((WAVES, GROUP, HID), F32),
                pltpu.VMEM((56, WIDTH), F32),
                pltpu.VMEM((8, TOWER), F32),
                pltpu.VMEM((TASKS, WIDTH, TOWER), F32),
                pltpu.VMEM((SMALL, 128), F32),
                *[pltpu.VMEM((EXPERTS, HID, wide), BF16)] * 3,
                pltpu.VMEM((EXPERTS, wide), F32),
                pltpu.VMEM((32, wide), F32),
                pltpu.VMEM((8, wide), F32),
                pltpu.VMEM((WIDTH + 16, wide), BF16),
                pltpu.VMEM((WIDTH, wide), BF16),
                pltpu.VMEM((WIDTH, wide), F32),
                pltpu.VMEM((WIDTH, wide), F32),
                pltpu.VMEM((EXPERTS, wide), F32),
                pltpu.VMEM((32, wide), F32),
                pltpu.VMEM((8, wide), F32),
                pltpu.VMEM((GROUP, WIDTH, wide), BF16),
                pltpu.VMEM((GROUP * HID, wide), BF16),
                *[pltpu.VMEM((HID, wide), F32)] * 4,
            ],
        ),
        out_shape=[slab, slab] + rest,
        cost_estimate=pl.CostEstimate(flops=14_000_000_000, bytes_accessed=40_000_000, transcendentals=0),
        compiler_params=pltpu.CompilerParams(
            dimension_semantics=("arbitrary",), vmem_limit_bytes=61 * MIB
        ),
        name="main_part",
    )(
        core,
        u,
        codes,
        mixing,
        inner,
        inner_bias.reshape(2 * EXPERTS, 128),
        outer,
        outer_bias,
        *tower_in,
    )


def last_kernel(sending, rows, core_ref, *refs):
    (u_ref, inner_ref, outer_ref, hid_ref, slope_ref, out_ref, gate_ref, dy_ref), refs = refs[:8], refs[8:]
    step = pl.program_id(0)
    if sending:
        (slab_ref, bias_ref, acc_ref, dgate_ref), refs = refs[:4], refs[4:]
        aug, dout_ref, dpre_ref, *work = refs
        wave = step + 2 * (1 - core_ref[0])
        bias_at = bias_ref
    else:
        (acc_in, dgate_in, codes_ref, mixing_ref, outer_bias_ref, code_ref, mix_ref), refs = refs[:7], refs[7:]
        (other_bias, slab_ref, back_ref, small_ref), refs = refs[:4], refs[4:]
        aug, dout_ref, dpre_ref, acc_ref, dgate_ref, dcode_ref, dmix_ref, bias_ref, rest_ref, *work = refs
        wave = step + 2 * core_ref[0]
        bias_at = bias_ref.at[pl.ds(step, 1)]

    @pl.when(step == 0)
    def _():
        extend(aug, u_ref[...])
        if sending:
            acc_ref[...] = jnp.zeros_like(acc_ref)
            dgate_ref[...] = jnp.zeros_like(dgate_ref)
        else:
            acc_ref[...] = acc_in[...]
            dgate_ref[...] = dgate_in[...]

    def state(p):
        return hid_ref.at[p], slope_ref.at[p], out_ref.at[p]

    backward_wave(True, rows, wave, aug, inner_ref, outer_ref, state, gate_ref, dy_ref, acc_ref, dgate_ref, slab_ref, bias_at, dout_ref, dpre_ref, work)
    if sending:
        return

    @pl.when(step == 1)
    def _():
        du = finish(True, rows, u_ref[...], codes_ref, mixing_ref, outer_bias_ref, code_ref, mix_ref, gate_ref, dy_ref, dgate_ref, acc_ref, dcode_ref, dmix_ref, rest_ref)
        back_ref[...] = du.T
        core = core_ref[0]
        small_ref[0:56, :] = rest_ref[:, :128]
        small_ref[56:112, :] = rest_ref[:, 128:]
        for w in range(WAVES):
            found = jnp.where(core == w // 2, bias_ref[w % 2], other_bias[w])
            small_ref[112 + GROUP * w : 112 + GROUP * (w + 1), :] = found[:, :128]
            small_ref[128 + GROUP * w : 128 + GROUP * (w + 1), :] = found[:, 128:]


def last_part(sending, core, u, inner, outer, state, gate, dy, more):
    rows = u.shape[1]

    def wave(i, core):
        return i + 2 * (1 - core[0] if sending else core[0])

    state_spec = pl.BlockSpec((GROUP, HID, rows), lambda i, core: (wave(i, core), 0, 0))
    arrays = [u, inner, outer, *state, gate, dy, *more]
    in_specs = [
        fixed(u.shape),
        pl.BlockSpec((WIDTH, GROUP * HID), lambda i, core: (0, wave(i, core))),
        pl.BlockSpec((GROUP, HID, WIDTH), lambda i, core: (wave(i, core), 0, 0)),
        state_spec,
        state_spec,
        state_spec,
    ]
    in_specs += [fixed(a.shape) for a in arrays[6:]]
    out_shape = [jax.ShapeDtypeStruct((EXPERTS // 2, SLAB, 128), F32)]
    out_specs = [pl.BlockSpec((GROUP, SLAB, 128), lambda i, core: (i, 0, 0))]
    scratch = [
        pltpu.VMEM((WIDTH + 16, rows), BF16),
        pltpu.VMEM((GROUP, WIDTH, rows), BF16),
        pltpu.VMEM((GROUP * HID, rows), BF16),
    ]
    if sending:
        out_shape.append(jax.ShapeDtypeStruct((WAVES, GROUP, HID), F32))
        out_specs.append(pl.BlockSpec((1, GROUP, HID), lambda i, core: (wave(i, core), 0, 0)))
        added = [
            jax.ShapeDtypeStruct((WIDTH, rows), F32),
            jax.ShapeDtypeStruct((EXPERTS, TASKS * rows), F32),
        ]
    else:
        added = [
            jax.ShapeDtypeStruct((rows, WIDTH), F32),
            jax.ShapeDtypeStruct((OWN, 128), F32),
        ]
        scratch += [
            pltpu.VMEM((WIDTH, rows), F32),
            pltpu.VMEM((EXPERTS, TASKS * rows), F32),
            pltpu.VMEM((32, rows), F32),
            pltpu.VMEM((8, rows), F32),
            pltpu.VMEM((2, GROUP, HID), F32),
            pltpu.VMEM((56, WIDTH), F32),
        ]
    scratch += [pltpu.VMEM((HID, rows), F32)] * 2
    out_shape += added
    out_specs += [fixed(s.shape) for s in added]
    return pl.pallas_call(
        functools.partial(last_kernel, sending, rows),
        grid_spec=pltpu.PrefetchScalarGridSpec(
            num_scalar_prefetch=1,
            grid=(2,),
            in_specs=in_specs,
            out_specs=out_specs,
            scratch_shapes=scratch,
        ),
        out_shape=out_shape,
        cost_estimate=pl.CostEstimate(flops=8_000_000_000, bytes_accessed=20_000_000, transcendentals=0),
        compiler_params=pltpu.CompilerParams(
            dimension_semantics=("arbitrary",), vmem_limit_bytes=40 * MIB
        ),
        name="last_send" if sending else "last_keep",
    )(core, *arrays)


def place(chip, core):
    found = []
    for axes in AXES:
        early, late = [], []
        for shift in axes:
            low, high = (chip >> shift) & 1, (chip >> (shift + 1)) & 1
            early.append(jnp.where(core == 0, low ^ high, high))
            late.append(jnp.where(core == 0, high, low))
        found.append(early + late)
    return found


def swaps(shift, step):
    pairs = []
    for chip in range(64):
        c = (chip >> shift) & 3
        for core in range(2):
            n = c ^ 1 if (core + step // 3) % 2 == 0 else 3 - c
            pairs.append((chip * 2 + core, (chip + ((n - c) << shift)) * 2 + core))
    return pairs


def swap(step, sent):
    return [
        lax.ppermute(s, ("chip", "core"), swaps(axes[step % 3], step))
        for s, axes in zip(sent, AXES)
    ]


def plain_call(kernel, sizes, name, chip, core, *arrays, scratch=()):
    smem = pl.BlockSpec(memory_space=pltpu.SMEM)
    vmem = pl.BlockSpec(memory_space=pltpu.VMEM)
    return pl.pallas_call(
        kernel,
        in_specs=[smem, smem] + [vmem] * len(arrays),
        out_specs=[vmem] * len(sizes),
        out_shape=[jax.ShapeDtypeStruct((n, 128), F32) for n in sizes],
        scratch_shapes=scratch,
        cost_estimate=pl.CostEstimate(flops=0, bytes_accessed=2_000_000, transcendentals=0),
        compiler_params=pltpu.CompilerParams(vmem_limit_bytes=28 * MIB),
        name=name,
    )(chip, core, *arrays)


def span(at, h, size):
    return pl.ds(pl.multiple_of(at + h * size, 8), size)


def open_kernel(counts, with_small, chip_ref, core_ref, keep_ref, got_ref, *refs):
    if with_small:
        (small_keep, small_got, small_own), refs = refs[:3], refs[3:]
        tail_ref = refs[-1]
        tail_ref[:2048, :] = keep_ref[6144:, :] + got_ref[6144:, :]
        tail_ref[2048 : 2048 + SHARE, :] = small_keep[...] + small_got[...]
        tail_ref[2048 + SHARE : 2048 + SHARE + OWN, :] = small_own[...]
        tail_ref[2048 + SHARE + OWN :, :] = jnp.zeros((512 - SHARE - OWN, 128), F32)
    places = place(chip_ref[0], core_ref[0])
    at = 0
    for i, m in enumerate(counts):
        size, h = 32 * m, places[i][0]

        def read(h):
            if with_small and i == 2:
                return tail_ref[span(0, h, size), :]
            return keep_ref[span(at, h, size), :] + got_ref[span(at, h, size), :]

        refs[i][...] = read(1 - h)
        refs[3 + i][...] = read(h)
        at += 2 * size


def open_rows(counts, chip, core, keep, got, *small):
    sizes = [32 * m for m in counts]
    return plain_call(
        functools.partial(open_kernel, counts, bool(small)),
        sizes * 2,
        "open_one" if small else "open_two",
        chip,
        core,
        keep.reshape(HALF_ROWS, 128),
        got.reshape(HALF_ROWS, 128),
        *small,
        scratch=[pltpu.VMEM((2560, 128), F32)] if small else [],
    )


def blend_kernel(i, chip_ref, core_ref, one_ref, two_ref, got_one, got_two, sent, kept):
    h = place(chip_ref[0], core_ref[0])[i][1]
    for ref, got, m, begin in ((one_ref, got_one, ONE[i], 0), (two_ref, got_two, TWO[i], ONE[i])):
        for k in range(16):
            to = slice(CHUNK * k + begin, CHUNK * k + begin + m)
            for side, out in ((1 - h, sent), (h, kept)):
                at = pl.ds(pl.multiple_of(side * (16 * m) + m * k, 8), m)
                out[to, :] = ref[at, :] + got[at, :]


def halve_kernel(i, step, chip_ref, core_ref, keep_ref, got_ref, sent, kept):
    n, h = sent.shape[0], place(chip_ref[0], core_ref[0])[i][step]
    sent[...] = keep_ref[span(0, 1 - h, n), :] + got_ref[span(0, 1 - h, n), :]
    kept[...] = keep_ref[span(0, h, n), :] + got_ref[span(0, h, n), :]


def add_kernel(chip_ref, core_ref, own_ref, got_ref, out_ref):
    out_ref[...] = own_ref[...] + got_ref[...]


def double_kernel(i, step, chip_ref, core_ref, own_ref, got_ref, out_ref):
    n, h = own_ref.shape[0], place(chip_ref[0], core_ref[0])[i][step]
    out_ref[span(0, h, n), :] = own_ref[...]
    out_ref[span(0, 1 - h, n), :] = got_ref[...]


def swap_one(i, step, sent):
    return lax.ppermute(sent, ("chip", "core"), swaps(AXES[i][step % 3], step))


def reduce_color(i, chip, core, kept_one, kept_two, got_one, got_two):
    at = (chip, core)
    name = "xyz"[i]
    sent, kept = plain_call(
        functools.partial(blend_kernel, i),
        [16 * CHUNK] * 2,
        "blend_" + name,
        *at,
        kept_one,
        kept_two,
        got_one,
        got_two,
    )
    for step in (2,):
        got = swap_one(i, step - 1, sent)
        kernel = functools.partial(halve_kernel, i, step)
        sizes = [CHUNK * 32 >> step] * 2
        sent, kept = plain_call(kernel, sizes, "halve_%s%d" % (name, step), *at, kept, got)
    (own,) = plain_call(
        add_kernel, [8 * CHUNK], "close_" + name, *at, kept, swap_one(i, 2, sent)
    )
    for step in (3, 4, 5):
        (own,) = plain_call(
            add_kernel, [8 * CHUNK], "pair_%s%d" % (name, step), *at, own, swap_one(i, step, own)
        )
    for step in (2, 1):
        kernel = functools.partial(double_kernel, i, step)
        sizes = [2 * own.shape[0]]
        (own,) = plain_call(
            kernel, sizes, "double_%s%d" % (name, step), *at, own, swap_one(i, step, own)
        )
    return own


def layer_rows(layer):
    counts, begin = (ONE, (0, 0, 0)) if layer == 0 else (TWO, ONE)
    return [(i, counts[i], begin[i]) for i in range(3)]


def lay_kernel(mine, chip_ref, core_ref, *refs):
    own, got, refs = refs[:3], refs[3:6], refs[6:]
    if not mine:
        small_in, refs = refs[0], refs[5:]
    outs, refs = refs[:4], refs[4:]
    core = core_ref[0] if mine else 1 - core_ref[0]
    first = [p[0] for p in place(chip_ref[0], core)]
    step = pl.program_id(0)

    def rows_of(i, chunk, begin, count):
        lower = chunk < 32
        at = (chunk % 32) * CHUNK + begin
        a, b = own[i][at : at + count, :], got[i][at : at + count, :]
        return jnp.where((first[i] == 0) == lower, a, b)

    def put(layer, row, value):
        e, part, at = row // SLAB % PAIR, row // 256 % 4, row % 256
        count = value.shape[0]
        lanes = slice(128 * (part // 2), 128 * (part // 2 + 1))
        if part % 2 == 0:
            outs[2 * layer + 1][e, at : at + count, lanes] = value
        else:
            lanes = slice(e * HID + lanes.start, e * HID + lanes.stop)
            outs[2 * layer][at : at + count, lanes] = value

    for s in range(4):

        @pl.when(step == s)
        def _():
            for layer in range(2):
                base = 0
                for i, m, begin in layer_rows(layer):
                    for chunk in range(64):
                        row = base + chunk * m
                        low, high = max(row, s * 2 * SLAB), min(row + m, (s + 1) * 2 * SLAB)
                        while low < high:
                            stop = min(high, (low // 256 + 1) * 256)
                            put(layer, low, rows_of(i, chunk, begin + low - row, stop - low))
                            low = stop
                    base += 64 * m

    def small_rows():
        found = []
        m = ONE[2]
        for chunk in range(64):
            row = 6144 + chunk * m
            low = max(row, HALF_ROWS)
            if low < row + m:
                found.append((low - HALF_ROWS, rows_of(2, chunk, low - row, row + m - low)))
        return found

    if mine:
        (small_out,) = refs

        @pl.when(step == 0)
        def _():
            for at, value in small_rows():
                small_out[at : at + value.shape[0], :] = value

        return

    codes_one, mix_one, back_one, bias_one = refs[:4]
    codes_two, mix_two, back_two, bias_two = refs[4:8]
    tower_inner, tower_bias, tower_outer, tower_last, acc_ref = refs[8:]

    @pl.when(step == 0)
    def _():
        acc_ref[pl.ds(pl.multiple_of(512 * (1 - core), 8), 512), :] = small_in[...]
        for at, value in small_rows():
            acc_ref[pl.ds(pl.multiple_of(512 * core + at, 8), value.shape[0]), :] = value

        def early(at, count):
            parts = []
            if at < SHARE:
                parts.append(acc_ref[at : min(at + count, SHARE), :])
            if at + count > SHARE:
                parts.append(acc_ref[512 + max(at, SHARE) - SHARE : 512 + at + count - SHARE, :])
            return parts[0] if len(parts) == 1 else jnp.concatenate(parts, axis=0)

        def late(at, count):
            at += SHARE
            return acc_ref[at : at + count, :] + acc_ref[512 + at : 512 + at + count, :]

        tower_inner[0] = early(0, 256)
        tower_inner[1] = early(256, 256)
        for s in range(2):
            lanes = slice(s * 128, (s + 1) * 128)
            for at, read, codes, mix, back in (
                (0, late, codes_one, mix_one, back_one),
                (512, early, codes_two, mix_two, back_two),
            ):
                at += 56 * s
                codes[:, lanes] = read(at, 32)
                mix[:, lanes] = read(at + 32, 8)
                back[:, lanes] = read(at + 40, 16)
            for ref, found in ((bias_one, late(112 + 16 * s, 16)), (bias_two, early(624 + 16 * s, 16))):
                for e in range(EXPERTS):
                    ref[2 * e + s : 2 * e + s + 1, :] = found[e : e + 1]
        last = early(656, 8)
        tower_outer[...] = last[0:2]
        tower_bias[...] = last[2:4]
        tower_last[:, 0:1] = last[4:5, 0:1]
        tower_last[:, 1:2] = last[5:6, 0:1]


def lay(mine, chip, core, own, got, more):
    def at(core):
        return core[0] if mine else 1 - core[0]

    shapes = [(WIDTH, EXPERTS * HID), (EXPERTS, HID, WIDTH)] * 2
    out_specs = [
        pl.BlockSpec((WIDTH, PAIR * HID), lambda i, chip, core: (0, 4 * at(core) + i)),
        pl.BlockSpec((PAIR, HID, WIDTH), lambda i, chip, core: (4 * at(core) + i, 0, 0)),
    ] * 2

    def still(shape):
        return pl.BlockSpec(shape, lambda i, chip, core: (0,) * len(shape))

    in_specs = [still(a.shape) for a in (*own, *got)]
    if mine:
        little = [(512, 128)]
        scratch, aliases = [], {}
    else:
        in_specs += [still(more[0].shape)] + [pl.BlockSpec(memory_space=pl.ANY)] * 4
        aliases = {9: 0, 10: 1, 11: 2, 12: 3}
        little = [(32, WIDTH), (8, WIDTH), (EXPERTS, WIDTH), (2 * EXPERTS, 128)] * 2
        little += [(TASKS, WIDTH, TOWER), (TASKS, TOWER), (TASKS, TOWER), (1, TASKS)]
        scratch = [pltpu.VMEM((1024, 128), F32)]
    shapes += little
    out_specs += [still(s) for s in little]
    return pl.pallas_call(
        functools.partial(lay_kernel, mine),
        grid_spec=pltpu.PrefetchScalarGridSpec(
            num_scalar_prefetch=2,
            grid=(4,),
            in_specs=in_specs,
            out_specs=out_specs,
            scratch_shapes=scratch,
        ),
        out_shape=[jax.ShapeDtypeStruct(s, F32) for s in shapes],
        input_output_aliases=aliases,
        cost_estimate=pl.CostEstimate(flops=0, bytes_accessed=16_000_000, transcendentals=0),
        compiler_params=pltpu.CompilerParams(
            dimension_semantics=("arbitrary",), vmem_limit_bytes=32 * MIB
        ),
        name="lay_own" if mine else "lay_other",
    )(chip, core, *own, *got, *more)


def on_device(
    tokens,
    labels,
    lengths,
    codes_one,
    mixing_one,
    inner_one,
    inner_bias_one,
    outer_one,
    outer_bias_one,
    codes_two,
    mixing_two,
    inner_two,
    inner_bias_two,
    outer_two,
    outer_bias_two,
    tower_inner,
    tower_inner_bias,
    tower_outer,
    tower_outer_bias,
):
    rows = tokens.shape[0]
    core = lax.axis_index("core").astype(jnp.int32).reshape(1)
    chip = lax.axis_index("chip").astype(jnp.int32).reshape(1)
    base = (lax.axis_index(("chip", "core")) * rows).astype(jnp.int32).reshape(1)

    def cross(a):
        return lax.ppermute(a, "core", [(0, 1), (1, 0)])

    codes_one, mixing_one, codes_two, mixing_two = (
        codes_one.T,
        mixing_one.T,
        codes_two.T,
        mixing_two.T,
    )
    count = jnp.sum(labels.astype(F32), axis=0)
    sent = jnp.broadcast_to(jnp.pad(count, (0, 126))[None, :], (128, 128))
    counts = lax.all_to_all(sent, ("chip", "core"), 0, 0, tiled=True)
    *state, gate, code, mix, u, u_two = first_part(
        tokens, codes_one, mixing_one, inner_one, inner_bias_one, outer_one, outer_bias_one
    )
    towers = (tower_inner, tower_inner_bias, tower_outer, tower_outer_bias.reshape(1, TASKS))
    towers = (labels.T, counts, lengths.reshape(1, -1), base, *towers)
    send, keep_two, dy, predictions, small_send, small_keep = main_part(
        core, u_two, codes_two, mixing_two, inner_two, inner_bias_two, outer_two, outer_bias_two, towers
    )
    got_two = cross(send)
    small_got = cross(small_send)
    send, bias_one, acc, dgate = last_part(
        True, core, u, inner_one, outer_one, state, gate, dy, ()
    )
    got_one = cross(send)
    opened = open_rows(TWO, chip, core, keep_two, got_two)
    sent, kept_two = opened[:3], opened[3:]
    got_two = swap(0, sent)
    more = (acc, dgate, codes_one, mixing_one, outer_bias_one, code, mix)
    more += (bias_one,)
    keep_one, grad_tokens, small_own = last_part(
        False, core, u, inner_one, outer_one, state, gate, dy, more
    )
    *got_two, keep_one = lax.optimization_barrier((*got_two, keep_one))
    opened = open_rows(ONE, chip, core, keep_one, got_one, small_keep, small_got, small_own)
    got_one = swap(0, opened[:3])
    own = [
        reduce_color(i, chip, core, opened[3 + i], kept_two[i], got_one[i], got_two[i])
        for i in (2, 1, 0)
    ][::-1]
    got = swap(0, own)
    own_other = [cross(a) for a in own]
    got_other = [cross(a) for a in got]
    *found, small = lay(True, chip, core, own, got, ())
    found = lay(False, chip, core, own_other, got_other, (small, *found))
    inner_one, outer_one, inner_two, outer_two = found[:4]
    codes_one, mix_one, back_one, bias_one, codes_two, mix_two, back_two, bias_two = found[4:12]
    tower_inner, tower_bias, tower_outer, tower_last = found[12:]
    return (
        predictions.T,
        grad_tokens,
        codes_one.T,
        mix_one.T,
        inner_one,
        bias_one.reshape(-1),
        outer_one,
        back_one,
        codes_two.T,
        mix_two.T,
        inner_two,
        bias_two.reshape(-1),
        outer_two,
        back_two,
        tower_inner,
        tower_bias,
        tower_outer,
        tower_last.reshape(-1),
    )


def solution(mesh):
    chips = Mesh(mesh.devices.reshape(-1, 2), ("chip", "core"))
    rows, copied = P(("chip", "core"), None), P()
    return jax.shard_map(
        on_device,
        mesh=chips,
        in_specs=(rows, rows) + (copied,) * 17,
        out_specs=(rows, rows) + (copied,) * 16,
        check_vma=False,
    )
```

```python
import functools

import jax
import jax.numpy as jnp
from jax import lax
from jax.experimental import pallas as pl
from jax.experimental.pallas import tpu as pltpu
from jax.sharding import Mesh, PartitionSpec as P

EXPERTS = 16
SEL = 4
BITS = 4
TASKS = 2
WIDTH = 256
HID = 256
TOWER = 128
PAIR = 2
STEPS = EXPERTS // PAIR
HALF = STEPS // 2
GROUP = 4
WAVES = EXPERTS // GROUP
AHEAD = 4
ROUNDS = EXPERTS // AHEAD
SLAB = 1024
SMALL = 672
SHARE = SMALL // 2
OWN = 144
HALF_ROWS = 8 * SLAB
ONE = (48, 48, 40)
TWO = (40, 40, 48)
CHUNK = 88
AXES = ((0, 4, 2), (4, 2, 0), (2, 0, 4))
F32 = jnp.float32
BF16 = jnp.bfloat16
ROOT = 0.7978845608028654
CUBE = 0.044715
MIB = 1024 * 1024


def nn(a, b):
    return lax.dot_general(a, b, (((1,), (0,)), ((), ())), preferred_element_type=F32)


def nt(a, b):
    return lax.dot_general(a, b, (((1,), (1,)), ((), ())), preferred_element_type=F32)


def tn(a, b):
    return lax.dot_general(a, b, (((0,), (0,)), ((), ())), preferred_element_type=F32)


def pieces(x):
    hi = x.astype(BF16)
    rest = x - hi.astype(F32)
    mid = rest.astype(BF16)
    return hi, mid, (rest - mid.astype(F32)).astype(BF16)


def gelu_both(x):
    square = x * x
    slope = square * (ROOT * CUBE) + ROOT
    s = 0.5 + 0.5 * jnp.tanh(x * slope)
    value = x * s
    return value, s + value * (1.0 - s) * (slope * 6.0 - 4.0 * ROOT)


def soft_parts(mix):
    top = jnp.maximum(jnp.maximum(mix[0], mix[1]), jnp.maximum(mix[2], mix[3]))
    raised = [jnp.exp(m - top) for m in mix]
    total = raised[0] + raised[1] + raised[2] + raised[3]
    return [r / total for r in raised]


def bit_factors(code):
    rows = code[0].shape[1]
    expert = lax.broadcasted_iota(jnp.int32, (EXPERTS, rows), 0)
    found = []
    for i in range(SEL):
        per_bit = []
        for b in range(BITS):
            k = jnp.clip(code[i * BITS + b], -5.0, 5.0)
            s = -0.002 * (k * k * k) + 0.15 * k + 0.5
            on = (expert >> b) & 1 == 1
            per_bit.append(jnp.where(on, s, 1.0 - s))
        found.append(per_bit)
    return found


def gate_of(code, mix):
    w = soft_parts(mix)
    total = None
    for i, f in enumerate(bit_factors(code)):
        r = w[i] * ((f[0] * f[1]) * (f[2] * f[3]))
        total = r if total is None else total + r
    return total


def gate_back(code, mix, grad):
    rows = grad.shape[1]
    expert = lax.broadcasted_iota(jnp.int32, (EXPERTS, rows), 0)
    w = soft_parts(mix)
    grad_w, grad_code = [], []
    for i, f in enumerate(bit_factors(code)):
        low, high = f[0] * f[1], f[2] * f[3]
        grad_w.append(jnp.sum(grad * (low * high), axis=0, keepdims=True))
        up = grad * w[i]
        others = (f[1] * high, f[0] * high, low * f[3], low * f[2])
        for b in range(BITS):
            on = (expert >> b) & 1 == 1
            term = up * others[b]
            ds = jnp.sum(jnp.where(on, term, -term), axis=0, keepdims=True)
            c = code[i * BITS + b]
            k = jnp.clip(c, -5.0, 5.0)
            inside = jnp.where(jnp.abs(c) <= 5.0, 0.15 - 0.006 * (k * k), 0.0)
            grad_code.append(ds * inside)
    mean = w[0] * grad_w[0] + w[1] * grad_w[1] + w[2] * grad_w[2] + w[3] * grad_w[3]
    return grad_code, [w[i] * (grad_w[i] - mean) for i in range(SEL)]


def task_rows(logits, mixes, task, lanes):
    code = [logits[task * 16 + k : task * 16 + k + 1, lanes] for k in range(16)]
    mix = [mixes[task * 4 + k : task * 4 + k + 1, lanes] for k in range(4)]
    return code, mix


def task_lanes(task, rows, shared):
    return slice(0, rows) if shared else slice(task * rows, (task + 1) * rows)


def whole(shape):
    return pl.BlockSpec(shape, lambda *_: (0,) * len(shape), pipeline_mode=pl.Buffered(1))


def tower(
    rows,
    v_ref,
    labels_ref,
    counts_ref,
    lengths_ref,
    base_ref,
    inner_ref,
    bias_ref,
    outer_ref,
    outer_bias_ref,
    predictions_ref,
    small_ref,
    grad_inner_ref,
    dy_ref,
):
    sessions = lengths_ref.shape[1]
    lens = jnp.broadcast_to(lengths_ref[...], (8, sessions)).astype(F32).astype(BF16)
    before = lax.broadcasted_iota(jnp.int32, (sessions, sessions), 0)
    after = lax.broadcasted_iota(jnp.int32, (sessions, sessions), 1)
    upto = jnp.where(before <= after, 1.0, 0.0).astype(BF16)
    ends = nn(lens, upto)[0:1, :]
    starts = ends - lens[0:1, :].astype(F32)
    ids = (lax.broadcasted_iota(jnp.int32, (rows, sessions), 0) + base_ref[0]).astype(F32)
    inside = jnp.where((ids >= starts) & (ids < ends), 1.0, 0.0).astype(BF16)
    row_length = nt(lens, inside)[0:1, :]
    all_rows = float(rows * counts_ref.shape[0])
    weight = (all_rows / sessions) / row_length
    positives = jnp.sum(counts_ref[...], axis=0, keepdims=True)
    bias = bias_ref[...].astype(F32).T
    columns = outer_ref[...].astype(F32).T
    small_ref[...] = jnp.zeros_like(small_ref)
    for t in range(TASKS):
        lanes = slice(t * rows, (t + 1) * rows)
        v = v_ref[:, lanes]
        pre = tn(inner_ref[t], v) + bias[:, t : t + 1]
        hid, slope = gelu_both(pre)
        hid = hid.astype(BF16)
        column = columns[:, t : t + 1]
        logit = jnp.sum(hid.astype(F32) * column, axis=0, keepdims=True)
        logit = logit + outer_bias_ref[0:1, t : t + 1].astype(F32)
        y = labels_ref[t : t + 1, :].astype(F32)
        count = positives[:, t : t + 1]
        ratio = (all_rows - count) / count
        chance = jax.nn.sigmoid(logit)
        predictions_ref[t : t + 1, :] = chance
        grad = weight * (-ratio * y * jax.nn.sigmoid(-logit) + (1.0 - y) * chance)
        grad = grad.astype(BF16)
        back = (grad.astype(F32) * column * slope).astype(BF16)
        picked = lax.broadcasted_iota(jnp.int32, (16, rows), 0)
        stack = jnp.where(picked == 0, grad.astype(F32), jnp.where(picked == 1, 1.0, 0.0))
        stack = stack.astype(BF16)
        by_hid = nt(stack, hid)
        by_back = nt(stack, back)
        small_ref[t : t + 1, :TOWER] = by_hid[0:1]
        small_ref[2 + t : 3 + t, :TOWER] = by_back[1:2]
        total = jnp.sum(grad.astype(F32), axis=1, keepdims=True)
        small_ref[4 + t : 5 + t, :TOWER] = jnp.broadcast_to(total, (1, TOWER))
        grad_inner_ref[t] = nt(v, back)
        dy_ref[:, lanes] = nn(inner_ref[t], back)


def pipeline(count, tiles, stages):
    for slot in range(count + len(stages) - 1):
        for q in range(tiles):
            for late, stage in enumerate(stages):
                if 0 <= slot - late < count:
                    stage(slot - late, q)


def prepare(shared, rows, u, codes_ref, mixing_ref, outer_bias_ref, code_ref, mix_ref, gate_ref, acc_ref):
    code_ref[...] = nn(codes_ref[...], u)
    mix_ref[...] = nn(mixing_ref[...], u)
    outer_bias = outer_bias_ref[...]
    for t in range(TASKS):
        code, mix = task_rows(code_ref, mix_ref, t, task_lanes(t, rows, shared))
        gate = gate_of(code, mix)
        span = slice(t * rows, (t + 1) * rows)
        gate_ref[:, span] = gate
        hi, mid, low = pieces(gate)
        acc_ref[:, span] = tn(outer_bias, hi) + tn(outer_bias, mid) + tn(outer_bias, low)


def forward_wave(shared, rows, wave, u_ref, inner_ref, bias_ref, outer_ref, state, gate_ref, acc_ref, work, ready=None):
    bias = bias_ref[...].astype(F32).T
    lanes = rows if shared else rows * TASKS
    tiles = lanes // 256
    part = WIDTH // tiles
    tall = 16 * 1024 // lanes
    pre_refs, mid_refs = work[:2], work[2:]
    kept = {}

    def start_pre(p, q):
        if q == 0:
            kept["inner", p] = inner_ref[:, p * HID : (p + 1) * HID].T
        span = slice(q * 256, (q + 1) * 256)
        pre_refs[p % 2][:, span] = nn(kept["inner", p], u_ref[:WIDTH, span])

    def bend(p, q):
        hid_ref, slope_ref, _ = state(p)
        for at in range(q * part, (q + 1) * part, tall):
            here = slice(at, at + tall)
            half, top = at // 128, at % 128
            column = bias[top : top + tall, 2 * p + half : 2 * p + half + 1]
            hid, slope = gelu_both(pre_refs[p % 2][here, :lanes] + column)
            hid_ref[here, :] = hid.astype(BF16)
            slope_ref[here, :] = slope.astype(BF16)
        if ready and q == tiles - 1:
            ready(p, 0)
            ready(p, 1)

    def start_out(p, q):
        if q == 0:
            kept["outer", p] = outer_ref[p].T
        span = slice(q * 256, (q + 1) * 256)
        mid_refs[p % 2][:, span] = nn(kept["outer", p], state(p)[0][:, span])

    def combine(p, q):
        if q == 0:
            kept["gate", p] = gate_ref[pl.ds(wave * AHEAD + p, 1), :]
        gate = kept["gate", p]
        for at in range(q * part, (q + 1) * part, tall):
            here = slice(at, at + tall)
            out = mid_refs[p % 2][here, :lanes]
            state(p)[2][here, :] = out.astype(BF16)
            for t in range(TASKS if shared else 1):
                span = slice(t * rows, (t + 1) * rows) if shared else slice(0, lanes)
                acc_ref[here, span] += gate[:, span] * out
        if ready and q == tiles - 1:
            ready(p, 2)

    pipeline(AHEAD, tiles, (start_pre, bend, start_out, combine))


def backward_wave(shared, rows, wave, aug_ref, inner_ref, outer_ref, state, gate_ref, dy_ref, acc_ref, dgate_ref, slab_ref, bias_ref, dout_ref, dpre_ref, work):
    lanes = rows if shared else rows * TASKS
    tiles = lanes // 256
    part = WIDTH // tiles
    tall = 16 * 1024 // lanes
    tasks = TASKS if shared else 1
    spans = [slice(t * rows, (t + 1) * rows) if shared else slice(0, lanes) for t in range(tasks)]
    kept = {}

    def share(p, q):
        e = pl.ds(wave * GROUP + p, 1)
        if q == 0:
            kept["gate", p] = gate_ref[e, :]
            kept["sum", p] = [None] * tasks
        gate, sums = kept["gate", p], kept["sum", p]
        for at in range(q * part, (q + 1) * part, tall):
            here = slice(at, at + tall)
            dys = [dy_ref[here, s] for s in spans]
            dout = gate[:, spans[0]] * dys[0]
            if shared:
                dout = dout + gate[:, spans[1]] * dys[1]
            dout_ref[p, here, :] = dout.astype(BF16)
            out = state(p)[2][here, :].astype(F32)
            for t in range(tasks):
                term = jnp.sum((out * dys[t]).reshape(tall // 8, 8, -1), axis=0)
                sums[t] = term if at == 0 else sums[t] + term
        if q == tiles - 1:
            for t in range(tasks):
                dgate_ref[e, spans[t]] = jnp.sum(sums[t], axis=0, keepdims=True)

    def back_out(p, q):
        span = slice(q * 256, (q + 1) * 256)
        work[p % 2][:, span] = nn(outer_ref[p], dout_ref[p, :, span])

    def unbend(p, q):
        slope_ref = state(p)[1]
        for at in range(q * part, (q + 1) * part, tall):
            here = slice(at, at + tall)
            dpre = work[p % 2][here, :lanes] * slope_ref[here, :].astype(F32)
            dpre_ref[p * HID + at : p * HID + at + tall, :] = dpre.astype(BF16)

    def grads(p, q):
        if q == 0:
            grad = nt(state(p)[0][...], dout_ref[p])
            slab_ref[p, :HID] = grad[:, :128]
            slab_ref[p, 512 : 512 + HID] = grad[:, 128:]
        if q == tiles // 2:
            grad = nt(aug_ref[...], dpre_ref[p * HID : (p + 1) * HID, :])
            slab_ref[p, HID:512] = grad[:WIDTH, :128]
            slab_ref[p, 512 + HID :] = grad[:WIDTH, 128:]
            bias_ref[0, p : p + 1, :] = grad[WIDTH : WIDTH + 1]

    pipeline(GROUP, tiles, (share, back_out, unbend, grads))
    acc_ref[...] += nn(inner_ref[...], dpre_ref[...])


def finish(shared, rows, u, codes_ref, mixing_ref, outer_bias_ref, code_ref, mix_ref, gate_ref, dy_ref, dgate_ref, acc_ref, dcode_ref, dmix_ref, rest_ref):
    dcode_ref[...] = jnp.zeros_like(dcode_ref)
    dmix_ref[...] = jnp.zeros_like(dmix_ref)
    outer_bias = outer_bias_ref[...]
    y_hi, y_mid = pieces(dy_ref[...])[:2]
    bias_share = nn(outer_bias, y_hi) + nn(outer_bias, y_mid)
    for t in range(TASKS):
        span = slice(t * rows, (t + 1) * rows)
        here = task_lanes(t, rows, shared)
        upto = bias_share[:, span]
        code, mix = task_rows(code_ref, mix_ref, t, here)
        grad_code, grad_mix = gate_back(code, mix, dgate_ref[:, span] + upto)
        for k in range(16):
            dcode_ref[t * 16 + k : t * 16 + k + 1, here] = grad_code[k]
        for k in range(4):
            dmix_ref[t * 4 + k : t * 4 + k + 1, here] = grad_mix[k]
    dcode = dcode_ref[...].astype(BF16)
    dmix = dmix_ref[...].astype(BF16)
    rest_ref[:32, :] = nt(dcode, u)
    rest_ref[32:40, :] = nt(dmix, u)
    g_hi, g_mid = pieces(gate_ref[...])[:2]
    rest_ref[40:56, :] = nt(g_hi, y_hi) + nt(g_hi, y_mid) + nt(g_mid, y_hi)
    return acc_ref[...] + tn(codes_ref[...], dcode) + tn(mixing_ref[...], dmix)


def extend(aug_ref, u):
    aug_ref[:WIDTH, :] = u
    one = lax.broadcasted_iota(jnp.int32, (16, u.shape[1]), 0) == 0
    aug_ref[WIDTH:, :] = jnp.where(one, 1.0, 0.0).astype(BF16)


def first_kernel(rows, tokens_ref, codes_ref, mixing_ref, inner_ref, bias_ref, outer_ref, outer_bias_ref, *refs):
    far, (gate_ref, code_ref, mix_ref, turned, next_ref), refs = refs[:3], refs[3:8], refs[8:]
    near, (sems, acc_ref), work = refs[:3], refs[3:5], refs[5:]
    step = pl.program_id(0)

    @pl.when(step == 0)
    def _():
        turned[...] = tokens_ref[...].astype(F32).T.astype(BF16)
        prepare(True, rows, turned[...], codes_ref, mixing_ref, outer_bias_ref, code_ref, mix_ref, gate_ref, acc_ref)

    slot = step % 2

    def state(p):
        return tuple(r.at[slot, p] for r in near)

    def copy(wave, p, k):
        to = far[k].at[wave * AHEAD + p]
        return pltpu.make_async_copy(near[k].at[wave % 2, p], to, sems.at[k, wave % 2, p])

    def settle(wave):
        for p in range(AHEAD):
            for k in range(3):
                copy(wave, p, k).wait()

    @pl.when(step >= 2)
    def _():
        settle(step - 2)

    def ready(p, k):
        copy(step, p, k).start()

    forward_wave(True, rows, step, turned, inner_ref, bias_ref, outer_ref, state, gate_ref, acc_ref, work, ready)

    @pl.when(step == ROUNDS - 1)
    def _():
        next_ref[...] = acc_ref[...].astype(BF16)
        settle(step - 1)
        settle(step)


def first_part(tokens, codes, mixing, inner, inner_bias, outer, outer_bias):
    rows = tokens.shape[0]
    wide = rows * TASKS
    arrays = (tokens, codes, mixing, inner, inner_bias.reshape(2 * EXPERTS, 128), outer, outer_bias)
    arrays = [pltpu.with_memory_space_constraint(a, pltpu.HBM) for a in arrays]
    state = pltpu.HBM((EXPERTS, HID, rows), BF16)
    plain = [
        pltpu.HBM((EXPERTS, wide), F32),
        pltpu.HBM((32, rows), F32),
        pltpu.HBM((8, rows), F32),
        pltpu.HBM((WIDTH, rows), BF16),
        jax.ShapeDtypeStruct((WIDTH, wide), BF16),
    ]
    return pl.pallas_call(
        functools.partial(first_kernel, rows),
        grid=(ROUNDS,),
        in_specs=[
            whole(tokens.shape),
            whole(codes.shape),
            whole(mixing.shape),
            pl.BlockSpec((WIDTH, AHEAD * HID), lambda i: (0, i)),
            pl.BlockSpec((2 * AHEAD, 128), lambda i: (i, 0)),
            pl.BlockSpec((AHEAD, HID, WIDTH), lambda i: (i, 0, 0)),
            whole(outer_bias.shape),
        ],
        out_specs=[pl.BlockSpec(memory_space=pl.ANY)] * 3 + [whole(s.shape) for s in plain],
        out_shape=[state] * 3 + plain,
        scratch_shapes=[
            *[pltpu.VMEM((2, AHEAD, HID, rows), BF16)] * 3,
            pltpu.SemaphoreType.DMA((3, 2, AHEAD)),
            pltpu.VMEM((WIDTH, wide), F32),
        ]
        + [pltpu.VMEM((HID, rows), F32)] * 4,
        cost_estimate=pl.CostEstimate(flops=8_000_000_000, bytes_accessed=20_000_000, transcendentals=0),
        compiler_params=pltpu.CompilerParams(
            dimension_semantics=("arbitrary",), vmem_limit_bytes=26 * MIB
        ),
        name="first_part",
    )(*arrays)


def main_kernel(rows, core_ref, *refs):
    (u_ref, codes_two, mixing_two, inner_two, bias_two, outer_two, outer_bias_two), refs = refs[:7], refs[7:]
    (inner_back, outer_back), refs = refs[:2], refs[2:]
    tower_in, refs = refs[:8], refs[8:]
    (send_ref, keep_ref, dy_one, predictions, small_send, small_keep), refs = refs[:6], refs[6:]
    (grad_bias, rest_ref, little, tower_inner, small_ref), refs = refs[:5], refs[5:]
    tower_out = (predictions, little, tower_inner)
    (slab_ref, sems), refs = refs[:2], refs[2:]
    (hid_two, slope_two, out_two, gate_two, code_two, mix_two, aug, v_ref), refs = refs[:8], refs[8:]
    (acc_ref, dy_two, dgate_ref, dcode_ref, dmix_ref, dout_ref, dpre_ref), work = refs[:7], refs[7:]
    step = pl.program_id(0)

    def state_two(base):
        return lambda p: tuple(r.at[base + p] for r in (hid_two, slope_two, out_two))

    @pl.when(step == 0)
    def _():
        extend(aug, u_ref[...])
        prepare(False, rows, u_ref[...], codes_two, mixing_two, outer_bias_two, code_two, mix_two, gate_two, acc_ref)

    @pl.when(step < ROUNDS)
    def _():
        forward_wave(False, rows, step, aug, inner_two, bias_two, outer_two, state_two(step * AHEAD), gate_two, acc_ref, work)

    @pl.when(step == ROUNDS)
    def _():
        v_ref[...] = acc_ref[...].astype(BF16)
        tower(rows, v_ref, *tower_in, *tower_out, dy_two)
        acc_ref[...] = jnp.zeros_like(acc_ref)

    def carry(j):
        out_ref = send_ref if j < 2 else keep_ref
        at = pl.ds(GROUP * (j % 2), GROUP)
        return pltpu.make_async_copy(slab_ref.at[j % 2], out_ref.at[at], sems.at[j])

    for j in range(WAVES):

        @pl.when(step == ROUNDS + j)
        def _():
            if j >= 2:
                carry(j - 2).wait()

    @pl.when(step >= ROUNDS)
    def _():
        wave = (step - ROUNDS + 2 * (1 - core_ref[0])) % WAVES
        backward_wave(False, rows, wave, aug, inner_back, outer_back, state_two(wave * GROUP), gate_two, dy_two, acc_ref, dgate_ref, slab_ref.at[(step - ROUNDS) % 2], grad_bias.at[pl.ds(wave, 1)], dout_ref, dpre_ref, work)

    for j in range(WAVES):

        @pl.when(step == ROUNDS + j)
        def _():
            carry(j).start()

    @pl.when(step == ROUNDS + WAVES - 1)
    def _():
        dy_one[...] = finish(False, rows, u_ref[...], codes_two, mixing_two, outer_bias_two, code_two, mix_two, gate_two, dy_two, dgate_ref, acc_ref, dcode_ref, dmix_ref, rest_ref)
        small_ref[0:256, :] = tower_inner[0]
        small_ref[256:512, :] = tower_inner[1]
        small_ref[512:568, :] = rest_ref[:, :128]
        small_ref[568:624, :] = rest_ref[:, 128:]
        for w in range(WAVES):
            small_ref[624 + GROUP * w : 624 + GROUP * (w + 1), :] = grad_bias[w, :, :128]
            small_ref[640 + GROUP * w : 640 + GROUP * (w + 1), :] = grad_bias[w, :, 128:]
        small_ref[656:664, :] = little[...]
        small_ref[664:, :] = jnp.zeros((8, 128), F32)
        core = core_ref[0]
        small_send[...] = small_ref[pl.ds(pl.multiple_of((1 - core) * SHARE, 8), SHARE), :]
        small_keep[...] = small_ref[pl.ds(pl.multiple_of(core * SHARE, 8), SHARE), :]
        carry(2).wait()
        carry(3).wait()


fixed = whole


def main_part(core, u, codes, mixing, inner, inner_bias, outer, outer_bias, tower_in):
    wide = u.shape[1]
    rows = wide // TASKS

    def order(i, core):
        return jnp.minimum(i, ROUNDS - 1)

    def back(i, core):
        return (jnp.maximum(i - ROUNDS, 0) + 2 * (1 - core[0])) % WAVES

    slab = jax.ShapeDtypeStruct((EXPERTS // 2, SLAB, 128), F32)

    rest = [
        jax.ShapeDtypeStruct((WIDTH, wide), F32),
        jax.ShapeDtypeStruct((TASKS, rows), F32),
        jax.ShapeDtypeStruct((SHARE, 128), F32),
        jax.ShapeDtypeStruct((SHARE, 128), F32),
    ]
    inner, outer = [pltpu.with_memory_space_constraint(a, pltpu.HBM) for a in (inner, outer)]
    tower_specs = [fixed(a.shape) for a in tower_in]
    tower_specs[3] = pl.BlockSpec(memory_space=pltpu.SMEM)
    return pl.pallas_call(
        functools.partial(main_kernel, rows),
        grid_spec=pltpu.PrefetchScalarGridSpec(
            num_scalar_prefetch=1,
            grid=(ROUNDS + WAVES,),
            in_specs=[
                fixed(u.shape),
                fixed(codes.shape),
                fixed(mixing.shape),
                pl.BlockSpec((WIDTH, AHEAD * HID), lambda i, core: (0, order(i, core))),
                pl.BlockSpec((2 * AHEAD, 128), lambda i, core: (order(i, core), 0)),
                pl.BlockSpec((AHEAD, HID, WIDTH), lambda i, core: (order(i, core), 0, 0)),
                fixed(outer_bias.shape),
                pl.BlockSpec((WIDTH, GROUP * HID), lambda i, core: (0, back(i, core))),
                pl.BlockSpec((GROUP, HID, WIDTH), lambda i, core: (back(i, core), 0, 0)),
            ]
            + tower_specs,
            out_specs=[pl.BlockSpec(memory_space=pl.ANY)] * 2
            + [fixed(s.shape) for s in rest],
            scratch_shapes=[
                pltpu.VMEM((WAVES, GROUP, HID), F32),
                pltpu.VMEM((56, WIDTH), F32),
                pltpu.VMEM((8, TOWER), F32),
                pltpu.VMEM((TASKS, WIDTH, TOWER), F32),
                pltpu.VMEM((SMALL, 128), F32),
                pltpu.VMEM((2, GROUP, SLAB, 128), F32),
                pltpu.SemaphoreType.DMA((WAVES,)),
                *[pltpu.VMEM((EXPERTS, HID, wide), BF16)] * 3,
                pltpu.VMEM((EXPERTS, wide), F32),
                pltpu.VMEM((32, wide), F32),
                pltpu.VMEM((8, wide), F32),
                pltpu.VMEM((WIDTH + 16, wide), BF16),
                pltpu.VMEM((WIDTH, wide), BF16),
                pltpu.VMEM((WIDTH, wide), F32),
                pltpu.VMEM((WIDTH, wide), F32),
                pltpu.VMEM((EXPERTS, wide), F32),
                pltpu.VMEM((32, wide), F32),
                pltpu.VMEM((8, wide), F32),
                pltpu.VMEM((GROUP, WIDTH, wide), BF16),
                pltpu.VMEM((GROUP * HID, wide), BF16),
                *[pltpu.VMEM((HID, wide), F32)] * 4,
            ],
        ),
        out_shape=[slab, slab] + rest,
        cost_estimate=pl.CostEstimate(flops=14_000_000_000, bytes_accessed=40_000_000, transcendentals=0),
        compiler_params=pltpu.CompilerParams(
            dimension_semantics=("arbitrary",), vmem_limit_bytes=46 * MIB
        ),
        name="main_part",
    )(
        core,
        u,
        codes,
        mixing,
        inner,
        inner_bias.reshape(2 * EXPERTS, 128),
        outer,
        outer_bias,
        inner,
        outer,
        *tower_in,
    )


def last_kernel(sending, rows, core_ref, *refs):
    far, (u_ref, gate_ref, dy_ref), refs = refs[:5], refs[5:8], refs[8:]
    near, sems, refs = refs[-6:-1], refs[-1], refs[:-6]
    inner_ref, outer_ref, hid_ref, slope_ref, out_ref = near
    step = pl.program_id(0)
    if sending:
        (slab_ref, bias_ref, acc_ref, dgate_ref), refs = refs[:4], refs[4:]
        aug, dout_ref, dpre_ref, *work = refs
        wave = step + 2 * (1 - core_ref[0])
        bias_at = bias_ref
    else:
        (acc_in, dgate_in, codes_ref, mixing_ref, outer_bias_ref, code_ref, mix_ref), refs = refs[:7], refs[7:]
        (other_bias, slab_ref, back_ref, small_ref), refs = refs[:4], refs[4:]
        aug, dout_ref, dpre_ref, acc_ref, dgate_ref, dcode_ref, dmix_ref, bias_ref, rest_ref, *work = refs
        wave = step + 2 * core_ref[0]
        bias_at = bias_ref.at[pl.ds(step, 1)]

    def fetch(j):
        e = wave - step + j
        at = pl.ds(pl.multiple_of(e * GROUP, GROUP), GROUP)
        columns = pl.ds(pl.multiple_of(e * GROUP * HID, GROUP * HID), GROUP * HID)
        sources = [far[0].at[:, columns]] + [r.at[at] for r in far[1:]]
        return [
            pltpu.make_async_copy(a, b.at[j], sems.at[k, j])
            for k, (a, b) in enumerate(zip(sources, near))
        ]

    @pl.when(step == 0)
    def _():
        for j in range(2):
            for copy in fetch(j):
                copy.start()
        extend(aug, u_ref[...])
        if sending:
            acc_ref[...] = jnp.zeros_like(acc_ref)
            dgate_ref[...] = jnp.zeros_like(dgate_ref)
        else:
            acc_ref[...] = acc_in[...]
            dgate_ref[...] = dgate_in[...]

    for copy in fetch(step):
        copy.wait()

    def state(p):
        return hid_ref.at[step, p], slope_ref.at[step, p], out_ref.at[step, p]

    backward_wave(True, rows, wave, aug, inner_ref.at[step], outer_ref.at[step], state, gate_ref, dy_ref, acc_ref, dgate_ref, slab_ref, bias_at, dout_ref, dpre_ref, work)
    if sending:
        return

    @pl.when(step == 1)
    def _():
        du = finish(True, rows, u_ref[...], codes_ref, mixing_ref, outer_bias_ref, code_ref, mix_ref, gate_ref, dy_ref, dgate_ref, acc_ref, dcode_ref, dmix_ref, rest_ref)
        back_ref[...] = du.T
        core = core_ref[0]
        small_ref[0:56, :] = rest_ref[:, :128]
        small_ref[56:112, :] = rest_ref[:, 128:]
        for w in range(WAVES):
            found = jnp.where(core == w // 2, bias_ref[w % 2], other_bias[w])
            small_ref[112 + GROUP * w : 112 + GROUP * (w + 1), :] = found[:, :128]
            small_ref[128 + GROUP * w : 128 + GROUP * (w + 1), :] = found[:, 128:]


def last_part(sending, core, u, inner, outer, state, gate, dy, more):
    rows = u.shape[1]

    def wave(i, core):
        return i + 2 * (1 - core[0] if sending else core[0])

    inner, outer = [pltpu.with_memory_space_constraint(a, pltpu.HBM) for a in (inner, outer)]
    state = [pltpu.with_memory_space_constraint(a, pltpu.HBM) for a in state]
    arrays = [inner, outer, *state, u, gate, dy, *more]
    in_specs = [pl.BlockSpec(memory_space=pl.ANY)] * 5
    in_specs += [fixed(a.shape) for a in arrays[5:]]
    out_shape = [jax.ShapeDtypeStruct((EXPERTS // 2, SLAB, 128), F32)]
    out_specs = [pl.BlockSpec((GROUP, SLAB, 128), lambda i, core: (i, 0, 0))]
    scratch = [
        pltpu.VMEM((WIDTH + 16, rows), BF16),
        pltpu.VMEM((GROUP, WIDTH, rows), BF16),
        pltpu.VMEM((GROUP * HID, rows), BF16),
    ]
    if sending:
        out_shape.append(jax.ShapeDtypeStruct((WAVES, GROUP, HID), F32))
        out_specs.append(pl.BlockSpec((1, GROUP, HID), lambda i, core: (wave(i, core), 0, 0)))
        added = [
            jax.ShapeDtypeStruct((WIDTH, rows), F32),
            jax.ShapeDtypeStruct((EXPERTS, TASKS * rows), F32),
        ]
    else:
        added = [
            jax.ShapeDtypeStruct((rows, WIDTH), F32),
            jax.ShapeDtypeStruct((OWN, 128), F32),
        ]
        scratch += [
            pltpu.VMEM((WIDTH, rows), F32),
            pltpu.VMEM((EXPERTS, TASKS * rows), F32),
            pltpu.VMEM((32, rows), F32),
            pltpu.VMEM((8, rows), F32),
            pltpu.VMEM((2, GROUP, HID), F32),
            pltpu.VMEM((56, WIDTH), F32),
        ]
    scratch += [pltpu.VMEM((HID, rows), F32)] * 2
    scratch += [
        pltpu.VMEM((2, WIDTH, GROUP * HID), BF16),
        pltpu.VMEM((2, GROUP, HID, WIDTH), BF16),
        *[pltpu.VMEM((2, GROUP, HID, rows), BF16)] * 3,
        pltpu.SemaphoreType.DMA((5, 2)),
    ]
    out_shape += added
    out_specs += [fixed(s.shape) for s in added]
    return pl.pallas_call(
        functools.partial(last_kernel, sending, rows),
        grid_spec=pltpu.PrefetchScalarGridSpec(
            num_scalar_prefetch=1,
            grid=(2,),
            in_specs=in_specs,
            out_specs=out_specs,
            scratch_shapes=scratch,
        ),
        out_shape=out_shape,
        cost_estimate=pl.CostEstimate(flops=8_000_000_000, bytes_accessed=20_000_000, transcendentals=0),
        compiler_params=pltpu.CompilerParams(
            dimension_semantics=("arbitrary",), vmem_limit_bytes=(24 if sending else 24) * MIB
        ),
        name="last_send" if sending else "last_keep",
    )(core, *arrays)


def place(chip, core):
    found = []
    for axes in AXES:
        early, late = [], []
        for shift in axes:
            low, high = (chip >> shift) & 1, (chip >> (shift + 1)) & 1
            early.append(jnp.where(core == 0, low ^ high, high))
            late.append(jnp.where(core == 0, high, low))
        found.append(early + late)
    return found


def swaps(shift, step):
    pairs = []
    for chip in range(64):
        c = (chip >> shift) & 3
        for core in range(2):
            n = c ^ 1 if (core + step // 3) % 2 == 0 else 3 - c
            pairs.append((chip * 2 + core, (chip + ((n - c) << shift)) * 2 + core))
    return pairs


def swap(step, sent):
    return [
        lax.ppermute(s, ("chip", "core"), swaps(axes[step % 3], step))
        for s, axes in zip(sent, AXES)
    ]


def plain_call(kernel, sizes, name, chip, core, *arrays, scratch=()):
    smem = pl.BlockSpec(memory_space=pltpu.SMEM)
    vmem = pl.BlockSpec(memory_space=pltpu.VMEM)
    return pl.pallas_call(
        kernel,
        in_specs=[smem, smem] + [vmem] * len(arrays),
        out_specs=[vmem] * len(sizes),
        out_shape=[jax.ShapeDtypeStruct((n, 128), F32) for n in sizes],
        scratch_shapes=scratch,
        cost_estimate=pl.CostEstimate(flops=0, bytes_accessed=2_000_000, transcendentals=0),
        compiler_params=pltpu.CompilerParams(vmem_limit_bytes=28 * MIB),
        name=name,
    )(chip, core, *arrays)


def span(at, h, size):
    return pl.ds(pl.multiple_of(at + h * size, 8), size)


def open_kernel(counts, with_small, chip_ref, core_ref, keep_ref, got_ref, *refs):
    if with_small:
        (small_keep, small_got, small_own), refs = refs[:3], refs[3:]
        tail_ref = refs[-1]
        tail_ref[:2048, :] = keep_ref[6144:, :] + got_ref[6144:, :]
        tail_ref[2048 : 2048 + SHARE, :] = small_keep[...] + small_got[...]
        tail_ref[2048 + SHARE : 2048 + SHARE + OWN, :] = small_own[...]
        tail_ref[2048 + SHARE + OWN :, :] = jnp.zeros((512 - SHARE - OWN, 128), F32)
    places = place(chip_ref[0], core_ref[0])
    at = 0
    for i, m in enumerate(counts):
        size, h = 32 * m, places[i][0]

        def read(h):
            if with_small and i == 2:
                return tail_ref[span(0, h, size), :]
            return keep_ref[span(at, h, size), :] + got_ref[span(at, h, size), :]

        refs[i][...] = read(1 - h)
        refs[3 + i][...] = read(h)
        at += 2 * size


def open_rows(counts, chip, core, keep, got, *small):
    sizes = [32 * m for m in counts]
    return plain_call(
        functools.partial(open_kernel, counts, bool(small)),
        sizes * 2,
        "open_one" if small else "open_two",
        chip,
        core,
        keep.reshape(HALF_ROWS, 128),
        got.reshape(HALF_ROWS, 128),
        *small,
        scratch=[pltpu.VMEM((2560, 128), F32)] if small else [],
    )


def blend_kernel(i, chip_ref, core_ref, one_ref, two_ref, got_one, got_two, sent, kept):
    h = place(chip_ref[0], core_ref[0])[i][1]
    for ref, got, m, begin in ((one_ref, got_one, ONE[i], 0), (two_ref, got_two, TWO[i], ONE[i])):
        for k in range(16):
            to = slice(CHUNK * k + begin, CHUNK * k + begin + m)
            for side, out in ((1 - h, sent), (h, kept)):
                at = pl.ds(pl.multiple_of(side * (16 * m) + m * k, 8), m)
                out[to, :] = ref[at, :] + got[at, :]


def halve_kernel(i, step, chip_ref, core_ref, keep_ref, got_ref, sent, kept):
    n, h = sent.shape[0], place(chip_ref[0], core_ref[0])[i][step]
    sent[...] = keep_ref[span(0, 1 - h, n), :] + got_ref[span(0, 1 - h, n), :]
    kept[...] = keep_ref[span(0, h, n), :] + got_ref[span(0, h, n), :]


def add_kernel(chip_ref, core_ref, own_ref, got_ref, out_ref):
    out_ref[...] = own_ref[...] + got_ref[...]


def double_kernel(i, step, chip_ref, core_ref, own_ref, got_ref, out_ref):
    n, h = own_ref.shape[0], place(chip_ref[0], core_ref[0])[i][step]
    out_ref[span(0, h, n), :] = own_ref[...]
    out_ref[span(0, 1 - h, n), :] = got_ref[...]


def swap_one(i, step, sent):
    return lax.ppermute(sent, ("chip", "core"), swaps(AXES[i][step % 3], step))


def reduce_color(i, chip, core, kept_one, kept_two, got_one, got_two):
    at = (chip, core)
    name = "xyz"[i]
    sent, kept = plain_call(
        functools.partial(blend_kernel, i),
        [16 * CHUNK] * 2,
        "blend_" + name,
        *at,
        kept_one,
        kept_two,
        got_one,
        got_two,
    )
    for step in (2,):
        got = swap_one(i, step - 1, sent)
        kernel = functools.partial(halve_kernel, i, step)
        sizes = [CHUNK * 32 >> step] * 2
        sent, kept = plain_call(kernel, sizes, "halve_%s%d" % (name, step), *at, kept, got)
    (own,) = plain_call(
        add_kernel, [8 * CHUNK], "close_" + name, *at, kept, swap_one(i, 2, sent)
    )
    for step in (3, 4, 5):
        (own,) = plain_call(
            add_kernel, [8 * CHUNK], "pair_%s%d" % (name, step), *at, own, swap_one(i, step, own)
        )
    for step in (2, 1):
        kernel = functools.partial(double_kernel, i, step)
        sizes = [2 * own.shape[0]]
        (own,) = plain_call(
            kernel, sizes, "double_%s%d" % (name, step), *at, own, swap_one(i, step, own)
        )
    return own


def layer_rows(layer):
    counts, begin = (ONE, (0, 0, 0)) if layer == 0 else (TWO, ONE)
    return [(i, counts[i], begin[i]) for i in range(3)]


def lay_kernel(mine, chip_ref, core_ref, *refs):
    own, got, refs = refs[:3], refs[3:6], refs[6:]
    if not mine:
        small_in, refs = refs[0], refs[5:]
    outs, refs = refs[:4], refs[4:]
    core = core_ref[0] if mine else 1 - core_ref[0]
    first = [p[0] for p in place(chip_ref[0], core)]
    step = pl.program_id(0)

    def rows_of(i, chunk, begin, count):
        lower = chunk < 32
        at = (chunk % 32) * CHUNK + begin
        a, b = own[i][at : at + count, :], got[i][at : at + count, :]
        return jnp.where((first[i] == 0) == lower, a, b)

    def put(layer, row, value):
        e, part, at = row // SLAB % PAIR, row // 256 % 4, row % 256
        count = value.shape[0]
        lanes = slice(128 * (part // 2), 128 * (part // 2 + 1))
        if part % 2 == 0:
            outs[2 * layer + 1][e, at : at + count, lanes] = value
        else:
            lanes = slice(e * HID + lanes.start, e * HID + lanes.stop)
            outs[2 * layer][at : at + count, lanes] = value

    for s in range(4):

        @pl.when(step == s)
        def _():
            for layer in range(2):
                base = 0
                for i, m, begin in layer_rows(layer):
                    for chunk in range(64):
                        row = base + chunk * m
                        low, high = max(row, s * 2 * SLAB), min(row + m, (s + 1) * 2 * SLAB)
                        while low < high:
                            stop = min(high, (low // 256 + 1) * 256)
                            put(layer, low, rows_of(i, chunk, begin + low - row, stop - low))
                            low = stop
                    base += 64 * m

    def small_rows():
        found = []
        m = ONE[2]
        for chunk in range(64):
            row = 6144 + chunk * m
            low = max(row, HALF_ROWS)
            if low < row + m:
                found.append((low - HALF_ROWS, rows_of(2, chunk, low - row, row + m - low)))
        return found

    if mine:
        (small_out,) = refs

        @pl.when(step == 0)
        def _():
            for at, value in small_rows():
                small_out[at : at + value.shape[0], :] = value

        return

    codes_one, mix_one, back_one, bias_one = refs[:4]
    codes_two, mix_two, back_two, bias_two = refs[4:8]
    tower_inner, tower_bias, tower_outer, tower_last, acc_ref = refs[8:]

    @pl.when(step == 0)
    def _():
        acc_ref[pl.ds(pl.multiple_of(512 * (1 - core), 8), 512), :] = small_in[...]
        for at, value in small_rows():
            acc_ref[pl.ds(pl.multiple_of(512 * core + at, 8), value.shape[0]), :] = value

        def early(at, count):
            parts = []
            if at < SHARE:
                parts.append(acc_ref[at : min(at + count, SHARE), :])
            if at + count > SHARE:
                parts.append(acc_ref[512 + max(at, SHARE) - SHARE : 512 + at + count - SHARE, :])
            return parts[0] if len(parts) == 1 else jnp.concatenate(parts, axis=0)

        def late(at, count):
            at += SHARE
            return acc_ref[at : at + count, :] + acc_ref[512 + at : 512 + at + count, :]

        tower_inner[0] = early(0, 256)
        tower_inner[1] = early(256, 256)
        for s in range(2):
            lanes = slice(s * 128, (s + 1) * 128)
            for at, read, codes, mix, back in (
                (0, late, codes_one, mix_one, back_one),
                (512, early, codes_two, mix_two, back_two),
            ):
                at += 56 * s
                codes[:, lanes] = read(at, 32)
                mix[:, lanes] = read(at + 32, 8)
                back[:, lanes] = read(at + 40, 16)
            for ref, found in ((bias_one, late(112 + 16 * s, 16)), (bias_two, early(624 + 16 * s, 16))):
                for e in range(EXPERTS):
                    ref[2 * e + s : 2 * e + s + 1, :] = found[e : e + 1]
        last = early(656, 8)
        tower_outer[...] = last[0:2]
        tower_bias[...] = last[2:4]
        tower_last[:, 0:1] = last[4:5, 0:1]
        tower_last[:, 1:2] = last[5:6, 0:1]


def lay(mine, chip, core, own, got, more):
    def at(core):
        return core[0] if mine else 1 - core[0]

    shapes = [(WIDTH, EXPERTS * HID), (EXPERTS, HID, WIDTH)] * 2
    out_specs = [
        pl.BlockSpec((WIDTH, PAIR * HID), lambda i, chip, core: (0, 4 * at(core) + i)),
        pl.BlockSpec((PAIR, HID, WIDTH), lambda i, chip, core: (4 * at(core) + i, 0, 0)),
    ] * 2

    def still(shape):
        return pl.BlockSpec(shape, lambda i, chip, core: (0,) * len(shape))

    in_specs = [still(a.shape) for a in (*own, *got)]
    if mine:
        little = [(512, 128)]
        scratch, aliases = [], {}
    else:
        in_specs += [still(more[0].shape)] + [pl.BlockSpec(memory_space=pl.ANY)] * 4
        aliases = {9: 0, 10: 1, 11: 2, 12: 3}
        little = [(32, WIDTH), (8, WIDTH), (EXPERTS, WIDTH), (2 * EXPERTS, 128)] * 2
        little += [(TASKS, WIDTH, TOWER), (TASKS, TOWER), (TASKS, TOWER), (1, TASKS)]
        scratch = [pltpu.VMEM((1024, 128), F32)]
    shapes += little
    out_specs += [still(s) for s in little]
    return pl.pallas_call(
        functools.partial(lay_kernel, mine),
        grid_spec=pltpu.PrefetchScalarGridSpec(
            num_scalar_prefetch=2,
            grid=(4,),
            in_specs=in_specs,
            out_specs=out_specs,
            scratch_shapes=scratch,
        ),
        out_shape=[jax.ShapeDtypeStruct(s, F32) for s in shapes],
        input_output_aliases=aliases,
        cost_estimate=pl.CostEstimate(flops=0, bytes_accessed=16_000_000, transcendentals=0),
        compiler_params=pltpu.CompilerParams(
            dimension_semantics=("arbitrary",), vmem_limit_bytes=32 * MIB
        ),
        name="lay_own" if mine else "lay_other",
    )(chip, core, *own, *got, *more)


def count_kernel(labels_ref, out_ref):
    count = jnp.sum(labels_ref[...].astype(F32), axis=1, keepdims=True)
    lane = lax.broadcasted_iota(jnp.int32, (1, 128), 1)
    row = jnp.where(lane == 0, count[0:1], jnp.where(lane == 1, count[1:2], 0.0))
    out_ref[...] = jnp.broadcast_to(row, (128, 128))


def on_device(
    tokens,
    labels,
    lengths,
    codes_one,
    mixing_one,
    inner_one,
    inner_bias_one,
    outer_one,
    outer_bias_one,
    codes_two,
    mixing_two,
    inner_two,
    inner_bias_two,
    outer_two,
    outer_bias_two,
    tower_inner,
    tower_inner_bias,
    tower_outer,
    tower_outer_bias,
):
    rows = tokens.shape[0]
    core = lax.axis_index("core").astype(jnp.int32).reshape(1)
    chip = lax.axis_index("chip").astype(jnp.int32).reshape(1)
    base = (lax.axis_index(("chip", "core")) * rows).astype(jnp.int32).reshape(1)

    def cross(a):
        return lax.ppermute(a, "core", [(0, 1), (1, 0)])

    codes_one, mixing_one, codes_two, mixing_two = (
        codes_one.T,
        mixing_one.T,
        codes_two.T,
        mixing_two.T,
    )
    labels = labels.T
    sent = pl.pallas_call(
        count_kernel, out_shape=jax.ShapeDtypeStruct((128, 128), F32), name="count"
    )(labels)
    counts = lax.all_to_all(sent, ("chip", "core"), 0, 0, tiled=True)
    *state, gate, code, mix, u, u_two = first_part(
        tokens, codes_one, mixing_one, inner_one, inner_bias_one, outer_one, outer_bias_one
    )
    towers = (tower_inner, tower_inner_bias, tower_outer, tower_outer_bias.reshape(1, TASKS))
    towers = (labels, counts, lengths.reshape(1, -1), base, *towers)
    send, keep_two, dy, predictions, small_send, small_keep = main_part(
        core, u_two, codes_two, mixing_two, inner_two, inner_bias_two, outer_two, outer_bias_two, towers
    )
    got_two = cross(send)
    small_got = cross(small_send)
    send, bias_one, acc, dgate = last_part(
        True, core, u, inner_one, outer_one, state, gate, dy, ()
    )
    got_one = cross(send)
    opened = open_rows(TWO, chip, core, keep_two, got_two)
    sent, kept_two = opened[:3], opened[3:]
    got_two = swap(0, sent)
    more = (acc, dgate, codes_one, mixing_one, outer_bias_one, code, mix)
    more += (bias_one,)
    keep_one, grad_tokens, small_own = last_part(
        False, core, u, inner_one, outer_one, state, gate, dy, more
    )
    *got_two, keep_one = lax.optimization_barrier((*got_two, keep_one))
    opened = open_rows(ONE, chip, core, keep_one, got_one, small_keep, small_got, small_own)
    got_one = swap(0, opened[:3])
    own = [
        reduce_color(i, chip, core, opened[3 + i], kept_two[i], got_one[i], got_two[i])
        for i in (2, 1, 0)
    ][::-1]
    got = swap(0, own)
    own_other = [cross(a) for a in own]
    got_other = [cross(a) for a in got]
    *found, small = lay(True, chip, core, own, got, ())
    found = lay(False, chip, core, own_other, got_other, (small, *found))
    inner_one, outer_one, inner_two, outer_two = found[:4]
    codes_one, mix_one, back_one, bias_one, codes_two, mix_two, back_two, bias_two = found[4:12]
    tower_inner, tower_bias, tower_outer, tower_last = found[12:]
    return (
        predictions.T,
        grad_tokens,
        codes_one.T,
        mix_one.T,
        inner_one,
        bias_one.reshape(-1),
        outer_one,
        back_one,
        codes_two.T,
        mix_two.T,
        inner_two,
        bias_two.reshape(-1),
        outer_two,
        back_two,
        tower_inner,
        tower_bias,
        tower_outer,
        tower_last.reshape(-1),
    )


def solution(mesh):
    chips = Mesh(mesh.devices.reshape(-1, 2), ("chip", "core"))
    rows, copied = P(("chip", "core"), None), P()
    return jax.shard_map(
        on_device,
        mesh=chips,
        in_specs=(rows, rows) + (copied,) * 17,
        out_specs=(rows, rows) + (copied,) * 16,
        check_vma=False,
    )
```

```python
import functools

import jax
import jax.numpy as jnp
from jax import lax
from jax.experimental import pallas as pl
from jax.experimental.pallas import tpu as pltpu
from jax.sharding import Mesh, PartitionSpec as P

EXPERTS = 16
SEL = 4
BITS = 4
TASKS = 2
WIDTH = 256
HID = 256
TOWER = 128
PAIR = 2
STEPS = EXPERTS // PAIR
HALF = STEPS // 2
GROUP = 4
WAVES = EXPERTS // GROUP
AHEAD = 8
ROUNDS = EXPERTS // AHEAD
SLAB = 1024
SMALL = 672
SHARE = SMALL // 2
OWN = 144
HALF_ROWS = 8 * SLAB
ONE = (48, 48, 40)
TWO = (40, 40, 48)
CHUNK = 88
AXES = ((0, 4, 2), (4, 2, 0), (2, 0, 4))
F32 = jnp.float32
BF16 = jnp.bfloat16
ROOT = 0.7978845608028654
CUBE = 0.044715
MIB = 1024 * 1024


def nn(a, b):
    return lax.dot_general(a, b, (((1,), (0,)), ((), ())), preferred_element_type=F32)


def nt(a, b):
    return lax.dot_general(a, b, (((1,), (1,)), ((), ())), preferred_element_type=F32)


def tn(a, b):
    return lax.dot_general(a, b, (((0,), (0,)), ((), ())), preferred_element_type=F32)


def pieces(x):
    hi = x.astype(BF16)
    rest = x - hi.astype(F32)
    mid = rest.astype(BF16)
    return hi, mid, (rest - mid.astype(F32)).astype(BF16)


def gelu_both(x):
    square = x * x
    slope = square * (ROOT * CUBE) + ROOT
    s = 0.5 + 0.5 * jnp.tanh(x * slope)
    value = x * s
    return value, s + value * (1.0 - s) * (slope * 6.0 - 4.0 * ROOT)


def soft_parts(mix):
    top = jnp.maximum(jnp.maximum(mix[0], mix[1]), jnp.maximum(mix[2], mix[3]))
    raised = [jnp.exp(m - top) for m in mix]
    total = raised[0] + raised[1] + raised[2] + raised[3]
    return [r / total for r in raised]


def bit_factors(code):
    rows = code[0].shape[1]
    expert = lax.broadcasted_iota(jnp.int32, (EXPERTS, rows), 0)
    found = []
    for i in range(SEL):
        per_bit = []
        for b in range(BITS):
            k = jnp.clip(code[i * BITS + b], -5.0, 5.0)
            s = -0.002 * (k * k * k) + 0.15 * k + 0.5
            on = (expert >> b) & 1 == 1
            per_bit.append(jnp.where(on, s, 1.0 - s))
        found.append(per_bit)
    return found


def gate_of(code, mix):
    w = soft_parts(mix)
    total = None
    for i, f in enumerate(bit_factors(code)):
        r = w[i] * ((f[0] * f[1]) * (f[2] * f[3]))
        total = r if total is None else total + r
    return total


def gate_back(code, mix, grad):
    rows = grad.shape[1]
    expert = lax.broadcasted_iota(jnp.int32, (EXPERTS, rows), 0)
    w = soft_parts(mix)
    grad_w, grad_code = [], []
    for i, f in enumerate(bit_factors(code)):
        low, high = f[0] * f[1], f[2] * f[3]
        grad_w.append(jnp.sum(grad * (low * high), axis=0, keepdims=True))
        up = grad * w[i]
        others = (f[1] * high, f[0] * high, low * f[3], low * f[2])
        for b in range(BITS):
            on = (expert >> b) & 1 == 1
            term = up * others[b]
            ds = jnp.sum(jnp.where(on, term, -term), axis=0, keepdims=True)
            c = code[i * BITS + b]
            k = jnp.clip(c, -5.0, 5.0)
            inside = jnp.where(jnp.abs(c) <= 5.0, 0.15 - 0.006 * (k * k), 0.0)
            grad_code.append(ds * inside)
    mean = w[0] * grad_w[0] + w[1] * grad_w[1] + w[2] * grad_w[2] + w[3] * grad_w[3]
    return grad_code, [w[i] * (grad_w[i] - mean) for i in range(SEL)]


def task_rows(logits, mixes, task, lanes):
    code = [logits[task * 16 + k : task * 16 + k + 1, lanes] for k in range(16)]
    mix = [mixes[task * 4 + k : task * 4 + k + 1, lanes] for k in range(4)]
    return code, mix


def task_lanes(task, rows, shared):
    return slice(0, rows) if shared else slice(task * rows, (task + 1) * rows)


def whole(shape):
    return pl.BlockSpec(shape, lambda *_: (0,) * len(shape), pipeline_mode=pl.Buffered(1))


def tower(
    rows,
    v_ref,
    labels_ref,
    counts_ref,
    lengths_ref,
    base_ref,
    inner_ref,
    bias_ref,
    outer_ref,
    outer_bias_ref,
    predictions_ref,
    small_ref,
    grad_inner_ref,
    dy_ref,
):
    sessions = lengths_ref.shape[1]
    lens = jnp.broadcast_to(lengths_ref[...], (8, sessions)).astype(F32).astype(BF16)
    before = lax.broadcasted_iota(jnp.int32, (sessions, sessions), 0)
    after = lax.broadcasted_iota(jnp.int32, (sessions, sessions), 1)
    upto = jnp.where(before <= after, 1.0, 0.0).astype(BF16)
    ends = nn(lens, upto)[0:1, :]
    starts = ends - lens[0:1, :].astype(F32)
    ids = (lax.broadcasted_iota(jnp.int32, (rows, sessions), 0) + base_ref[0]).astype(F32)
    inside = jnp.where((ids >= starts) & (ids < ends), 1.0, 0.0).astype(BF16)
    row_length = nt(lens, inside)[0:1, :]
    all_rows = float(rows * counts_ref.shape[0])
    weight = (all_rows / sessions) / row_length
    positives = jnp.sum(counts_ref[...], axis=0, keepdims=True)
    bias = bias_ref[...].astype(F32).T
    columns = outer_ref[...].astype(F32).T
    small_ref[...] = jnp.zeros_like(small_ref)
    for t in range(TASKS):
        lanes = slice(t * rows, (t + 1) * rows)
        v = v_ref[:, lanes]
        pre = tn(inner_ref[t], v) + bias[:, t : t + 1]
        hid, slope = gelu_both(pre)
        hid = hid.astype(BF16)
        column = columns[:, t : t + 1]
        logit = jnp.sum(hid.astype(F32) * column, axis=0, keepdims=True)
        logit = logit + outer_bias_ref[0:1, t : t + 1].astype(F32)
        y = labels_ref[t : t + 1, :].astype(F32)
        count = positives[:, t : t + 1]
        ratio = (all_rows - count) / count
        chance = jax.nn.sigmoid(logit)
        predictions_ref[t : t + 1, :] = chance
        grad = weight * (-ratio * y * jax.nn.sigmoid(-logit) + (1.0 - y) * chance)
        grad = grad.astype(BF16)
        back = (grad.astype(F32) * column * slope).astype(BF16)
        picked = lax.broadcasted_iota(jnp.int32, (16, rows), 0)
        stack = jnp.where(picked == 0, grad.astype(F32), jnp.where(picked == 1, 1.0, 0.0))
        stack = stack.astype(BF16)
        by_hid = nt(stack, hid)
        by_back = nt(stack, back)
        small_ref[t : t + 1, :TOWER] = by_hid[0:1]
        small_ref[2 + t : 3 + t, :TOWER] = by_back[1:2]
        total = jnp.sum(grad.astype(F32), axis=1, keepdims=True)
        small_ref[4 + t : 5 + t, :TOWER] = jnp.broadcast_to(total, (1, TOWER))
        grad_inner_ref[t] = nt(v, back)
        dy_ref[:, lanes] = nn(inner_ref[t], back)


def pipeline(count, tiles, stages):
    for slot in range(count + len(stages) - 1):
        for q in range(tiles):
            for late, stage in enumerate(stages):
                if 0 <= slot - late < count:
                    stage(slot - late, q)


def prepare(shared, rows, u, codes_ref, mixing_ref, outer_bias_ref, code_ref, mix_ref, gate_ref, acc_ref):
    code_ref[...] = nn(codes_ref[...], u)
    mix_ref[...] = nn(mixing_ref[...], u)
    outer_bias = outer_bias_ref[...]
    for t in range(TASKS):
        code, mix = task_rows(code_ref, mix_ref, t, task_lanes(t, rows, shared))
        gate = gate_of(code, mix)
        span = slice(t * rows, (t + 1) * rows)
        gate_ref[:, span] = gate
        hi, mid, low = pieces(gate)
        acc_ref[:, span] = tn(outer_bias, hi) + tn(outer_bias, mid) + tn(outer_bias, low)


def forward_wave(shared, rows, wave, u_ref, inner_ref, bias_ref, outer_ref, state, gate_ref, acc_ref, work, ready=None):
    bias = bias_ref[...].astype(F32).T
    lanes = rows if shared else rows * TASKS
    tiles = lanes // 256
    part = WIDTH // tiles
    tall = 16 * 1024 // lanes
    pre_refs, mid_refs = work[:2], work[2:]
    kept = {}

    def start_pre(p, q):
        if q == 0:
            kept["inner", p] = inner_ref[:, p * HID : (p + 1) * HID].T
        span = slice(q * 256, (q + 1) * 256)
        pre_refs[p % 2][:, span] = nn(kept["inner", p], u_ref[:WIDTH, span])

    def bend(p, q):
        hid_ref, slope_ref, _ = state(p)
        for at in range(q * part, (q + 1) * part, tall):
            here = slice(at, at + tall)
            half, top = at // 128, at % 128
            column = bias[top : top + tall, 2 * p + half : 2 * p + half + 1]
            hid, slope = gelu_both(pre_refs[p % 2][here, :lanes] + column)
            hid_ref[here, :] = hid.astype(BF16)
            slope_ref[here, :] = slope.astype(BF16)
        if ready and q == tiles - 1:
            ready(p, 0)
            ready(p, 1)

    def start_out(p, q):
        if q == 0:
            kept["outer", p] = outer_ref[p].T
        span = slice(q * 256, (q + 1) * 256)
        mid_refs[p % 2][:, span] = nn(kept["outer", p], state(p)[0][:, span])

    def combine(p, q):
        if q == 0:
            kept["gate", p] = gate_ref[pl.ds(wave * AHEAD + p, 1), :]
        gate = kept["gate", p]
        for at in range(q * part, (q + 1) * part, tall):
            here = slice(at, at + tall)
            out = mid_refs[p % 2][here, :lanes]
            state(p)[2][here, :] = out.astype(BF16)
            for t in range(TASKS if shared else 1):
                span = slice(t * rows, (t + 1) * rows) if shared else slice(0, lanes)
                acc_ref[here, span] += gate[:, span] * out
        if ready and q == tiles - 1:
            ready(p, 2)

    pipeline(AHEAD, tiles, (start_pre, bend, start_out, combine))


def backward_wave(shared, rows, wave, aug_ref, inner_ref, outer_ref, state, gate_ref, dy_ref, acc_ref, dgate_ref, slab_ref, bias_ref, dout_ref, dpre_ref, work):
    lanes = rows if shared else rows * TASKS
    tiles = lanes // 256
    part = WIDTH // tiles
    tall = 16 * 1024 // lanes
    tasks = TASKS if shared else 1
    spans = [slice(t * rows, (t + 1) * rows) if shared else slice(0, lanes) for t in range(tasks)]
    kept = {}

    def share(p, q):
        e = pl.ds(wave * GROUP + p, 1)
        if q == 0:
            kept["gate", p] = gate_ref[e, :]
            kept["sum", p] = [None] * tasks
        gate, sums = kept["gate", p], kept["sum", p]
        for at in range(q * part, (q + 1) * part, tall):
            here = slice(at, at + tall)
            dys = [dy_ref[here, s] for s in spans]
            dout = gate[:, spans[0]] * dys[0]
            if shared:
                dout = dout + gate[:, spans[1]] * dys[1]
            dout_ref[p, here, :] = dout.astype(BF16)
            out = state(p)[2][here, :].astype(F32)
            for t in range(tasks):
                term = jnp.sum((out * dys[t]).reshape(tall // 8, 8, -1), axis=0)
                sums[t] = term if at == 0 else sums[t] + term
        if q == tiles - 1:
            for t in range(tasks):
                dgate_ref[e, spans[t]] = jnp.sum(sums[t], axis=0, keepdims=True)

    def back_out(p, q):
        span = slice(q * 256, (q + 1) * 256)
        work[p % 2][:, span] = nn(outer_ref[p], dout_ref[p, :, span])
        if q == tiles - 1:
            grad = nt(state(p)[0][...], dout_ref[p])
            slab_ref[p, :HID] = grad[:, :128]
            slab_ref[p, 512 : 512 + HID] = grad[:, 128:]

    def unbend(p, q):
        slope_ref = state(p)[1]
        for at in range(q * part, (q + 1) * part, tall):
            here = slice(at, at + tall)
            dpre = work[p % 2][here, :lanes] * slope_ref[here, :].astype(F32)
            dpre_ref[p * HID + at : p * HID + at + tall, :] = dpre.astype(BF16)

    def grads(p, q):
        if q == 0:
            grad = nt(aug_ref[...], dpre_ref[p * HID : (p + 1) * HID, :])
            slab_ref[p, HID:512] = grad[:WIDTH, :128]
            slab_ref[p, 512 + HID :] = grad[:WIDTH, 128:]
            bias_ref[0, p : p + 1, :] = grad[WIDTH : WIDTH + 1]

    pipeline(GROUP, tiles, (share, back_out, unbend, grads))
    acc_ref[...] += nn(inner_ref[...], dpre_ref[...])


def finish(shared, rows, u, codes_ref, mixing_ref, outer_bias_ref, code_ref, mix_ref, gate_ref, dy_ref, dgate_ref, acc_ref, dcode_ref, dmix_ref, rest_ref):
    dcode_ref[...] = jnp.zeros_like(dcode_ref)
    dmix_ref[...] = jnp.zeros_like(dmix_ref)
    outer_bias = outer_bias_ref[...]
    y_hi, y_mid = pieces(dy_ref[...])[:2]
    bias_share = nn(outer_bias, y_hi) + nn(outer_bias, y_mid)
    for t in range(TASKS):
        span = slice(t * rows, (t + 1) * rows)
        here = task_lanes(t, rows, shared)
        upto = bias_share[:, span]
        code, mix = task_rows(code_ref, mix_ref, t, here)
        grad_code, grad_mix = gate_back(code, mix, dgate_ref[:, span] + upto)
        for k in range(16):
            dcode_ref[t * 16 + k : t * 16 + k + 1, here] = grad_code[k]
        for k in range(4):
            dmix_ref[t * 4 + k : t * 4 + k + 1, here] = grad_mix[k]
    dcode = dcode_ref[...].astype(BF16)
    dmix = dmix_ref[...].astype(BF16)
    rest_ref[:32, :] = nt(dcode, u)
    rest_ref[32:40, :] = nt(dmix, u)
    g_hi, g_mid = pieces(gate_ref[...])[:2]
    rest_ref[40:56, :] = nt(g_hi, y_hi) + nt(g_hi, y_mid) + nt(g_mid, y_hi)
    return acc_ref[...] + tn(codes_ref[...], dcode) + tn(mixing_ref[...], dmix)


def extend(aug_ref, u):
    aug_ref[:WIDTH, :] = u
    one = lax.broadcasted_iota(jnp.int32, (16, u.shape[1]), 0) == 0
    aug_ref[WIDTH:, :] = jnp.where(one, 1.0, 0.0).astype(BF16)


def first_kernel(rows, tokens_ref, codes_ref, mixing_ref, inner_ref, bias_ref, outer_ref, outer_bias_ref, *refs):
    far, (gate_ref, code_ref, mix_ref, turned, next_ref), refs = refs[:3], refs[3:8], refs[8:]
    near, (sems, acc_ref), work = refs[:3], refs[3:5], refs[5:]
    step = pl.program_id(0)

    @pl.when(step == 0)
    def _():
        turned[...] = tokens_ref[...].astype(F32).T.astype(BF16)
        prepare(True, rows, turned[...], codes_ref, mixing_ref, outer_bias_ref, code_ref, mix_ref, gate_ref, acc_ref)

    slot = step % 2

    def state(p):
        return tuple(r.at[slot, p] for r in near)

    def copy(wave, p, k):
        to = far[k].at[wave * AHEAD + p]
        return pltpu.make_async_copy(near[k].at[wave % 2, p], to, sems.at[k, wave % 2, p])

    def settle(wave):
        for p in range(AHEAD):
            for k in range(3):
                copy(wave, p, k).wait()

    @pl.when(step >= 2)
    def _():
        settle(step - 2)

    def ready(p, k):
        copy(step, p, k).start()

    forward_wave(True, rows, step, turned, inner_ref, bias_ref, outer_ref, state, gate_ref, acc_ref, work, ready)

    @pl.when(step == ROUNDS - 1)
    def _():
        next_ref[...] = acc_ref[...].astype(BF16)
        settle(step - 1)
        settle(step)


def first_part(tokens, codes, mixing, inner, inner_bias, outer, outer_bias):
    rows = tokens.shape[0]
    wide = rows * TASKS
    arrays = (tokens, codes, mixing, inner, inner_bias.reshape(2 * EXPERTS, 128), outer, outer_bias)
    arrays = [pltpu.with_memory_space_constraint(a, pltpu.HBM) for a in arrays]
    state = pltpu.HBM((EXPERTS, HID, rows), BF16)
    plain = [
        pltpu.HBM((EXPERTS, wide), F32),
        pltpu.HBM((32, rows), F32),
        pltpu.HBM((8, rows), F32),
        pltpu.HBM((WIDTH, rows), BF16),
        jax.ShapeDtypeStruct((WIDTH, wide), BF16),
    ]
    return pl.pallas_call(
        functools.partial(first_kernel, rows),
        grid=(ROUNDS,),
        in_specs=[
            whole(tokens.shape),
            whole(codes.shape),
            whole(mixing.shape),
            pl.BlockSpec((WIDTH, AHEAD * HID), lambda i: (0, i)),
            pl.BlockSpec((2 * AHEAD, 128), lambda i: (i, 0)),
            pl.BlockSpec((AHEAD, HID, WIDTH), lambda i: (i, 0, 0)),
            whole(outer_bias.shape),
        ],
        out_specs=[pl.BlockSpec(memory_space=pl.ANY)] * 3 + [whole(s.shape) for s in plain],
        out_shape=[state] * 3 + plain,
        scratch_shapes=[
            *[pltpu.VMEM((2, AHEAD, HID, rows), BF16)] * 3,
            pltpu.SemaphoreType.DMA((3, 2, AHEAD)),
            pltpu.VMEM((WIDTH, wide), F32),
        ]
        + [pltpu.VMEM((HID, rows), F32)] * 4,
        cost_estimate=pl.CostEstimate(flops=8_000_000_000, bytes_accessed=20_000_000, transcendentals=0),
        compiler_params=pltpu.CompilerParams(
            dimension_semantics=("arbitrary",), vmem_limit_bytes=26 * MIB
        ),
        name="first_part",
    )(*arrays)


def main_kernel(rows, core_ref, *refs):
    (u_ref, codes_two, mixing_two, inner_two, bias_two, outer_two, outer_bias_two), refs = refs[:7], refs[7:]
    (inner_back, outer_back), refs = refs[:2], refs[2:]
    tower_in, refs = refs[:8], refs[8:]
    (send_ref, keep_ref, dy_one, predictions, small_send, small_keep), refs = refs[:6], refs[6:]
    (grad_bias, rest_ref, little, tower_inner, small_ref), refs = refs[:5], refs[5:]
    tower_out = (predictions, little, tower_inner)
    (slab_ref, sems), refs = refs[:2], refs[2:]
    (hid_two, slope_two, out_two, gate_two, code_two, mix_two, aug, v_ref), refs = refs[:8], refs[8:]
    (acc_ref, dy_two, dgate_ref, dcode_ref, dmix_ref, dout_ref, dpre_ref), work = refs[:7], refs[7:]
    step = pl.program_id(0)

    def state_two(base):
        return lambda p: tuple(r.at[base + p] for r in (hid_two, slope_two, out_two))

    @pl.when(step == 0)
    def _():
        extend(aug, u_ref[...])
        prepare(False, rows, u_ref[...], codes_two, mixing_two, outer_bias_two, code_two, mix_two, gate_two, acc_ref)

    @pl.when(step < ROUNDS)
    def _():
        forward_wave(False, rows, step, aug, inner_two, bias_two, outer_two, state_two(step * AHEAD), gate_two, acc_ref, work)

    @pl.when(step == ROUNDS)
    def _():
        v_ref[...] = acc_ref[...].astype(BF16)
        tower(rows, v_ref, *tower_in, *tower_out, dy_two)
        acc_ref[...] = jnp.zeros_like(acc_ref)

    def carry(j):
        out_ref = send_ref if j < 2 else keep_ref
        at = pl.ds(GROUP * (j % 2), GROUP)
        return pltpu.make_async_copy(slab_ref.at[j % 2], out_ref.at[at], sems.at[j])

    for j in range(WAVES):

        @pl.when(step == ROUNDS + j)
        def _():
            if j >= 2:
                carry(j - 2).wait()

    @pl.when(step >= ROUNDS)
    def _():
        wave = (step - ROUNDS + 2 * (1 - core_ref[0])) % WAVES
        backward_wave(False, rows, wave, aug, inner_back, outer_back, state_two(wave * GROUP), gate_two, dy_two, acc_ref, dgate_ref, slab_ref.at[(step - ROUNDS) % 2], grad_bias.at[pl.ds(wave, 1)], dout_ref, dpre_ref, work)

    for j in range(WAVES):

        @pl.when(step == ROUNDS + j)
        def _():
            carry(j).start()

    @pl.when(step == ROUNDS + WAVES - 1)
    def _():
        dy_one[...] = finish(False, rows, u_ref[...], codes_two, mixing_two, outer_bias_two, code_two, mix_two, gate_two, dy_two, dgate_ref, acc_ref, dcode_ref, dmix_ref, rest_ref)
        small_ref[0:256, :] = tower_inner[0]
        small_ref[256:512, :] = tower_inner[1]
        small_ref[512:568, :] = rest_ref[:, :128]
        small_ref[568:624, :] = rest_ref[:, 128:]
        for w in range(WAVES):
            small_ref[624 + GROUP * w : 624 + GROUP * (w + 1), :] = grad_bias[w, :, :128]
            small_ref[640 + GROUP * w : 640 + GROUP * (w + 1), :] = grad_bias[w, :, 128:]
        small_ref[656:664, :] = little[...]
        small_ref[664:, :] = jnp.zeros((8, 128), F32)
        core = core_ref[0]
        small_send[...] = small_ref[pl.ds(pl.multiple_of((1 - core) * SHARE, 8), SHARE), :]
        small_keep[...] = small_ref[pl.ds(pl.multiple_of(core * SHARE, 8), SHARE), :]
        carry(2).wait()
        carry(3).wait()


fixed = whole


def main_part(core, u, codes, mixing, inner, inner_bias, outer, outer_bias, tower_in):
    wide = u.shape[1]
    rows = wide // TASKS

    def order(i, core):
        return jnp.minimum(i, ROUNDS - 1)

    def back(i, core):
        return (jnp.maximum(i - ROUNDS, 0) + 2 * (1 - core[0])) % WAVES

    slab = jax.ShapeDtypeStruct((EXPERTS // 2, SLAB, 128), F32)

    rest = [
        jax.ShapeDtypeStruct((WIDTH, wide), F32),
        jax.ShapeDtypeStruct((TASKS, rows), F32),
        jax.ShapeDtypeStruct((SHARE, 128), F32),
        jax.ShapeDtypeStruct((SHARE, 128), F32),
    ]
    inner, outer = [pltpu.with_memory_space_constraint(a, pltpu.HBM) for a in (inner, outer)]
    tower_specs = [fixed(a.shape) for a in tower_in]
    tower_specs[3] = pl.BlockSpec(memory_space=pltpu.SMEM)
    return pl.pallas_call(
        functools.partial(main_kernel, rows),
        grid_spec=pltpu.PrefetchScalarGridSpec(
            num_scalar_prefetch=1,
            grid=(ROUNDS + WAVES,),
            in_specs=[
                fixed(u.shape),
                fixed(codes.shape),
                fixed(mixing.shape),
                pl.BlockSpec((WIDTH, AHEAD * HID), lambda i, core: (0, order(i, core))),
                pl.BlockSpec((2 * AHEAD, 128), lambda i, core: (order(i, core), 0)),
                pl.BlockSpec((AHEAD, HID, WIDTH), lambda i, core: (order(i, core), 0, 0)),
                fixed(outer_bias.shape),
                pl.BlockSpec((WIDTH, GROUP * HID), lambda i, core: (0, back(i, core))),
                pl.BlockSpec((GROUP, HID, WIDTH), lambda i, core: (back(i, core), 0, 0)),
            ]
            + tower_specs,
            out_specs=[pl.BlockSpec(memory_space=pl.ANY)] * 2
            + [fixed(s.shape) for s in rest],
            scratch_shapes=[
                pltpu.VMEM((WAVES, GROUP, HID), F32),
                pltpu.VMEM((56, WIDTH), F32),
                pltpu.VMEM((8, TOWER), F32),
                pltpu.VMEM((TASKS, WIDTH, TOWER), F32),
                pltpu.VMEM((SMALL, 128), F32),
                pltpu.VMEM((2, GROUP, SLAB, 128), F32),
                pltpu.SemaphoreType.DMA((WAVES,)),
                *[pltpu.VMEM((EXPERTS, HID, wide), BF16)] * 3,
                pltpu.VMEM((EXPERTS, wide), F32),
                pltpu.VMEM((32, wide), F32),
                pltpu.VMEM((8, wide), F32),
                pltpu.VMEM((WIDTH + 16, wide), BF16),
                pltpu.VMEM((WIDTH, wide), BF16),
                pltpu.VMEM((WIDTH, wide), F32),
                pltpu.VMEM((WIDTH, wide), F32),
                pltpu.VMEM((EXPERTS, wide), F32),
                pltpu.VMEM((32, wide), F32),
                pltpu.VMEM((8, wide), F32),
                pltpu.VMEM((GROUP, WIDTH, wide), BF16),
                pltpu.VMEM((GROUP * HID, wide), BF16),
                *[pltpu.VMEM((HID, wide), F32)] * 4,
            ],
        ),
        out_shape=[slab, slab] + rest,
        cost_estimate=pl.CostEstimate(flops=14_000_000_000, bytes_accessed=40_000_000, transcendentals=0),
        compiler_params=pltpu.CompilerParams(
            dimension_semantics=("arbitrary",), vmem_limit_bytes=50 * MIB
        ),
        name="main_part",
    )(
        core,
        u,
        codes,
        mixing,
        inner,
        inner_bias.reshape(2 * EXPERTS, 128),
        outer,
        outer_bias,
        inner,
        outer,
        *tower_in,
    )


def last_kernel(sending, rows, core_ref, *refs):
    far, (u_ref, gate_ref, dy_ref), refs = refs[:5], refs[5:8], refs[8:]
    near, sems, refs = refs[-6:-1], refs[-1], refs[:-6]
    inner_ref, outer_ref, hid_ref, slope_ref, out_ref = near
    step = pl.program_id(0)
    if sending:
        (slab_ref, bias_ref, acc_ref, dgate_ref), refs = refs[:4], refs[4:]
        aug, dout_ref, dpre_ref, *work = refs
        wave = step + 2 * (1 - core_ref[0])
        bias_at = bias_ref
    else:
        (acc_in, dgate_in, codes_ref, mixing_ref, outer_bias_ref, code_ref, mix_ref), refs = refs[:7], refs[7:]
        (other_bias, slab_ref, back_ref, small_ref), refs = refs[:4], refs[4:]
        aug, dout_ref, dpre_ref, acc_ref, dgate_ref, dcode_ref, dmix_ref, bias_ref, rest_ref, *work = refs
        wave = step + 2 * core_ref[0]
        bias_at = bias_ref.at[pl.ds(step, 1)]

    def fetch(j):
        e = wave - step + j
        at = pl.ds(pl.multiple_of(e * GROUP, GROUP), GROUP)
        columns = pl.ds(pl.multiple_of(e * GROUP * HID, GROUP * HID), GROUP * HID)
        sources = [far[0].at[:, columns]] + [r.at[at] for r in far[1:]]
        return [
            pltpu.make_async_copy(a, b.at[j], sems.at[k, j])
            for k, (a, b) in enumerate(zip(sources, near))
        ]

    @pl.when(step == 0)
    def _():
        for j in range(2):
            for copy in fetch(j):
                copy.start()
        extend(aug, u_ref[...])
        if sending:
            acc_ref[...] = jnp.zeros_like(acc_ref)
            dgate_ref[...] = jnp.zeros_like(dgate_ref)
        else:
            acc_ref[...] = acc_in[...]
            dgate_ref[...] = dgate_in[...]

    for copy in fetch(step):
        copy.wait()

    def state(p):
        return hid_ref.at[step, p], slope_ref.at[step, p], out_ref.at[step, p]

    backward_wave(True, rows, wave, aug, inner_ref.at[step], outer_ref.at[step], state, gate_ref, dy_ref, acc_ref, dgate_ref, slab_ref, bias_at, dout_ref, dpre_ref, work)
    if sending:
        return

    @pl.when(step == 1)
    def _():
        du = finish(True, rows, u_ref[...], codes_ref, mixing_ref, outer_bias_ref, code_ref, mix_ref, gate_ref, dy_ref, dgate_ref, acc_ref, dcode_ref, dmix_ref, rest_ref)
        back_ref[...] = du.T
        core = core_ref[0]
        small_ref[0:56, :] = rest_ref[:, :128]
        small_ref[56:112, :] = rest_ref[:, 128:]
        for w in range(WAVES):
            found = jnp.where(core == w // 2, bias_ref[w % 2], other_bias[w])
            small_ref[112 + GROUP * w : 112 + GROUP * (w + 1), :] = found[:, :128]
            small_ref[128 + GROUP * w : 128 + GROUP * (w + 1), :] = found[:, 128:]


def last_part(sending, core, u, inner, outer, state, gate, dy, more):
    rows = u.shape[1]

    def wave(i, core):
        return i + 2 * (1 - core[0] if sending else core[0])

    inner, outer = [pltpu.with_memory_space_constraint(a, pltpu.HBM) for a in (inner, outer)]
    state = [pltpu.with_memory_space_constraint(a, pltpu.HBM) for a in state]
    arrays = [inner, outer, *state, u, gate, dy, *more]
    in_specs = [pl.BlockSpec(memory_space=pl.ANY)] * 5
    in_specs += [fixed(a.shape) for a in arrays[5:]]
    out_shape = [jax.ShapeDtypeStruct((EXPERTS // 2, SLAB, 128), F32)]
    out_specs = [pl.BlockSpec((GROUP, SLAB, 128), lambda i, core: (i, 0, 0))]
    scratch = [
        pltpu.VMEM((WIDTH + 16, rows), BF16),
        pltpu.VMEM((GROUP, WIDTH, rows), BF16),
        pltpu.VMEM((GROUP * HID, rows), BF16),
    ]
    if sending:
        out_shape.append(jax.ShapeDtypeStruct((WAVES, GROUP, HID), F32))
        out_specs.append(pl.BlockSpec((1, GROUP, HID), lambda i, core: (wave(i, core), 0, 0)))
        added = [
            jax.ShapeDtypeStruct((WIDTH, rows), F32),
            jax.ShapeDtypeStruct((EXPERTS, TASKS * rows), F32),
        ]
    else:
        added = [
            jax.ShapeDtypeStruct((rows, WIDTH), F32),
            jax.ShapeDtypeStruct((OWN, 128), F32),
        ]
        scratch += [
            pltpu.VMEM((WIDTH, rows), F32),
            pltpu.VMEM((EXPERTS, TASKS * rows), F32),
            pltpu.VMEM((32, rows), F32),
            pltpu.VMEM((8, rows), F32),
            pltpu.VMEM((2, GROUP, HID), F32),
            pltpu.VMEM((56, WIDTH), F32),
        ]
    scratch += [pltpu.VMEM((HID, rows), F32)] * 2
    scratch += [
        pltpu.VMEM((2, WIDTH, GROUP * HID), BF16),
        pltpu.VMEM((2, GROUP, HID, WIDTH), BF16),
        *[pltpu.VMEM((2, GROUP, HID, rows), BF16)] * 3,
        pltpu.SemaphoreType.DMA((5, 2)),
    ]
    out_shape += added
    out_specs += [fixed(s.shape) for s in added]
    return pl.pallas_call(
        functools.partial(last_kernel, sending, rows),
        grid_spec=pltpu.PrefetchScalarGridSpec(
            num_scalar_prefetch=1,
            grid=(2,),
            in_specs=in_specs,
            out_specs=out_specs,
            scratch_shapes=scratch,
        ),
        out_shape=out_shape,
        cost_estimate=pl.CostEstimate(flops=8_000_000_000, bytes_accessed=20_000_000, transcendentals=0),
        compiler_params=pltpu.CompilerParams(
            dimension_semantics=("arbitrary",), vmem_limit_bytes=(24 if sending else 24) * MIB
        ),
        name="last_send" if sending else "last_keep",
    )(core, *arrays)


def place(chip, core):
    found = []
    for axes in AXES:
        early, late = [], []
        for shift in axes:
            low, high = (chip >> shift) & 1, (chip >> (shift + 1)) & 1
            early.append(jnp.where(core == 0, low ^ high, high))
            late.append(jnp.where(core == 0, high, low))
        found.append(early + late)
    return found


def swaps(shift, step):
    pairs = []
    for chip in range(64):
        c = (chip >> shift) & 3
        for core in range(2):
            n = c ^ 1 if (core + step // 3) % 2 == 0 else 3 - c
            pairs.append((chip * 2 + core, (chip + ((n - c) << shift)) * 2 + core))
    return pairs


def swap(step, sent):
    return [
        lax.ppermute(s, ("chip", "core"), swaps(axes[step % 3], step))
        for s, axes in zip(sent, AXES)
    ]


def plain_call(kernel, sizes, name, chip, core, *arrays, scratch=()):
    smem = pl.BlockSpec(memory_space=pltpu.SMEM)
    vmem = pl.BlockSpec(memory_space=pltpu.VMEM)
    return pl.pallas_call(
        kernel,
        in_specs=[smem, smem] + [vmem] * len(arrays),
        out_specs=[vmem] * len(sizes),
        out_shape=[jax.ShapeDtypeStruct((n, 128), F32) for n in sizes],
        scratch_shapes=scratch,
        cost_estimate=pl.CostEstimate(flops=0, bytes_accessed=1000, transcendentals=0),
        compiler_params=pltpu.CompilerParams(vmem_limit_bytes=28 * MIB),
        name=name,
    )(chip, core, *arrays)


def span(at, h, size):
    return pl.ds(pl.multiple_of(at + h * size, 8), size)


def open_kernel(counts, with_small, chip_ref, core_ref, keep_ref, got_ref, *refs):
    if with_small:
        (small_keep, small_got, small_own), refs = refs[:3], refs[3:]
        tail_ref = refs[-1]
        tail_ref[:2048, :] = keep_ref[6144:, :] + got_ref[6144:, :]
        tail_ref[2048 : 2048 + SHARE, :] = small_keep[...] + small_got[...]
        tail_ref[2048 + SHARE : 2048 + SHARE + OWN, :] = small_own[...]
        tail_ref[2048 + SHARE + OWN :, :] = jnp.zeros((512 - SHARE - OWN, 128), F32)
    places = place(chip_ref[0], core_ref[0])
    at = 0
    for i, m in enumerate(counts):
        size, h = 32 * m, places[i][0]

        def read(h):
            if with_small and i == 2:
                return tail_ref[span(0, h, size), :]
            return keep_ref[span(at, h, size), :] + got_ref[span(at, h, size), :]

        refs[i][...] = read(1 - h)
        refs[3 + i][...] = read(h)
        at += 2 * size


def open_rows(counts, chip, core, keep, got, *small):
    sizes = [32 * m for m in counts]
    return plain_call(
        functools.partial(open_kernel, counts, bool(small)),
        sizes * 2,
        "open_one" if small else "open_two",
        chip,
        core,
        keep.reshape(HALF_ROWS, 128),
        got.reshape(HALF_ROWS, 128),
        *small,
        scratch=[pltpu.VMEM((2560, 128), F32)] if small else [],
    )


def blend_kernel(i, chip_ref, core_ref, one_ref, two_ref, got_one, got_two, sent, kept):
    h = place(chip_ref[0], core_ref[0])[i][1]
    for ref, got, m, begin in ((one_ref, got_one, ONE[i], 0), (two_ref, got_two, TWO[i], ONE[i])):
        for k in range(16):
            to = slice(CHUNK * k + begin, CHUNK * k + begin + m)
            for side, out in ((1 - h, sent), (h, kept)):
                at = pl.ds(pl.multiple_of(side * (16 * m) + m * k, 8), m)
                out[to, :] = ref[at, :] + got[at, :]


def halve_kernel(i, step, chip_ref, core_ref, keep_ref, got_ref, sent, kept):
    n, h = sent.shape[0], place(chip_ref[0], core_ref[0])[i][step]
    sent[...] = keep_ref[span(0, 1 - h, n), :] + got_ref[span(0, 1 - h, n), :]
    kept[...] = keep_ref[span(0, h, n), :] + got_ref[span(0, h, n), :]


def add_kernel(chip_ref, core_ref, own_ref, got_ref, out_ref):
    out_ref[...] = own_ref[...] + got_ref[...]


def double_kernel(i, step, chip_ref, core_ref, own_ref, got_ref, out_ref):
    n, h = own_ref.shape[0], place(chip_ref[0], core_ref[0])[i][step]
    out_ref[span(0, h, n), :] = own_ref[...]
    out_ref[span(0, 1 - h, n), :] = got_ref[...]


def swap_one(i, step, sent):
    return lax.ppermute(sent, ("chip", "core"), swaps(AXES[i][step % 3], step))


def reduce_color(i, chip, core, kept_one, kept_two, got_one, got_two):
    at = (chip, core)
    name = "xyz"[i]
    sent, kept = plain_call(
        functools.partial(blend_kernel, i),
        [16 * CHUNK] * 2,
        "blend_" + name,
        *at,
        kept_one,
        kept_two,
        got_one,
        got_two,
    )
    for step in (2,):
        got = swap_one(i, step - 1, sent)
        kernel = functools.partial(halve_kernel, i, step)
        sizes = [CHUNK * 32 >> step] * 2
        sent, kept = plain_call(kernel, sizes, "halve_%s%d" % (name, step), *at, kept, got)
    (own,) = plain_call(
        add_kernel, [8 * CHUNK], "close_" + name, *at, kept, swap_one(i, 2, sent)
    )
    for step in (3, 4, 5):
        (own,) = plain_call(
            add_kernel, [8 * CHUNK], "pair_%s%d" % (name, step), *at, own, swap_one(i, step, own)
        )
    for step in (2, 1):
        kernel = functools.partial(double_kernel, i, step)
        sizes = [2 * own.shape[0]]
        (own,) = plain_call(
            kernel, sizes, "double_%s%d" % (name, step), *at, own, swap_one(i, step, own)
        )
    return own


def layer_rows(layer):
    counts, begin = (ONE, (0, 0, 0)) if layer == 0 else (TWO, ONE)
    return [(i, counts[i], begin[i]) for i in range(3)]


def lay_kernel(mine, chip_ref, core_ref, *refs):
    own, got, refs = refs[:3], refs[3:6], refs[6:]
    if not mine:
        small_in, refs = refs[0], refs[5:]
    outs, refs = refs[:4], refs[4:]
    core = core_ref[0] if mine else 1 - core_ref[0]
    first = [p[0] for p in place(chip_ref[0], core)]
    step = pl.program_id(0)

    def rows_of(i, chunk, begin, count):
        lower = chunk < 32
        at = (chunk % 32) * CHUNK + begin
        a, b = own[i][at : at + count, :], got[i][at : at + count, :]
        return jnp.where((first[i] == 0) == lower, a, b)

    def put(layer, row, value):
        e, part, at = row // SLAB % PAIR, row // 256 % 4, row % 256
        count = value.shape[0]
        lanes = slice(128 * (part // 2), 128 * (part // 2 + 1))
        if part % 2 == 0:
            outs[2 * layer + 1][e, at : at + count, lanes] = value
        else:
            lanes = slice(e * HID + lanes.start, e * HID + lanes.stop)
            outs[2 * layer][at : at + count, lanes] = value

    for s in range(4):

        @pl.when(step == s)
        def _():
            for layer in range(2):
                base = 0
                for i, m, begin in layer_rows(layer):
                    for chunk in range(64):
                        row = base + chunk * m
                        low, high = max(row, s * 2 * SLAB), min(row + m, (s + 1) * 2 * SLAB)
                        while low < high:
                            stop = min(high, (low // 256 + 1) * 256)
                            put(layer, low, rows_of(i, chunk, begin + low - row, stop - low))
                            low = stop
                    base += 64 * m

    def small_rows():
        found = []
        m = ONE[2]
        for chunk in range(64):
            row = 6144 + chunk * m
            low = max(row, HALF_ROWS)
            if low < row + m:
                found.append((low - HALF_ROWS, rows_of(2, chunk, low - row, row + m - low)))
        return found

    if mine:
        (small_out,) = refs

        @pl.when(step == 0)
        def _():
            for at, value in small_rows():
                small_out[at : at + value.shape[0], :] = value

        return

    codes_one, mix_one, back_one, bias_one = refs[:4]
    codes_two, mix_two, back_two, bias_two = refs[4:8]
    tower_inner, tower_bias, tower_outer, tower_last, acc_ref = refs[8:]

    @pl.when(step == 0)
    def _():
        acc_ref[pl.ds(pl.multiple_of(512 * (1 - core), 8), 512), :] = small_in[...]
        for at, value in small_rows():
            acc_ref[pl.ds(pl.multiple_of(512 * core + at, 8), value.shape[0]), :] = value

        def early(at, count):
            parts = []
            if at < SHARE:
                parts.append(acc_ref[at : min(at + count, SHARE), :])
            if at + count > SHARE:
                parts.append(acc_ref[512 + max(at, SHARE) - SHARE : 512 + at + count - SHARE, :])
            return parts[0] if len(parts) == 1 else jnp.concatenate(parts, axis=0)

        def late(at, count):
            at += SHARE
            return acc_ref[at : at + count, :] + acc_ref[512 + at : 512 + at + count, :]

        tower_inner[0] = early(0, 256)
        tower_inner[1] = early(256, 256)
        for s in range(2):
            lanes = slice(s * 128, (s + 1) * 128)
            for at, read, codes, mix, back in (
                (0, late, codes_one, mix_one, back_one),
                (512, early, codes_two, mix_two, back_two),
            ):
                at += 56 * s
                codes[:, lanes] = read(at, 32)
                mix[:, lanes] = read(at + 32, 8)
                back[:, lanes] = read(at + 40, 16)
            for ref, found in ((bias_one, late(112 + 16 * s, 16)), (bias_two, early(624 + 16 * s, 16))):
                for e in range(EXPERTS):
                    ref[2 * e + s : 2 * e + s + 1, :] = found[e : e + 1]
        last = early(656, 8)
        tower_outer[...] = last[0:2]
        tower_bias[...] = last[2:4]
        tower_last[:, 0:1] = last[4:5, 0:1]
        tower_last[:, 1:2] = last[5:6, 0:1]


def lay(mine, chip, core, own, got, more):
    def at(core):
        return core[0] if mine else 1 - core[0]

    shapes = [(WIDTH, EXPERTS * HID), (EXPERTS, HID, WIDTH)] * 2
    out_specs = [
        pl.BlockSpec((WIDTH, PAIR * HID), lambda i, chip, core: (0, 4 * at(core) + i)),
        pl.BlockSpec((PAIR, HID, WIDTH), lambda i, chip, core: (4 * at(core) + i, 0, 0)),
    ] * 2

    def still(shape):
        return pl.BlockSpec(shape, lambda i, chip, core: (0,) * len(shape))

    in_specs = [still(a.shape) for a in (*own, *got)]
    if mine:
        little = [(512, 128)]
        scratch, aliases = [], {}
    else:
        in_specs += [still(more[0].shape)] + [pl.BlockSpec(memory_space=pl.ANY)] * 4
        aliases = {9: 0, 10: 1, 11: 2, 12: 3}
        little = [(32, WIDTH), (8, WIDTH), (EXPERTS, WIDTH), (2 * EXPERTS, 128)] * 2
        little += [(TASKS, WIDTH, TOWER), (TASKS, TOWER), (TASKS, TOWER), (1, TASKS)]
        scratch = [pltpu.VMEM((1024, 128), F32)]
    shapes += little
    out_specs += [still(s) for s in little]
    return pl.pallas_call(
        functools.partial(lay_kernel, mine),
        grid_spec=pltpu.PrefetchScalarGridSpec(
            num_scalar_prefetch=2,
            grid=(4,),
            in_specs=in_specs,
            out_specs=out_specs,
            scratch_shapes=scratch,
        ),
        out_shape=[jax.ShapeDtypeStruct(s, F32) for s in shapes],
        input_output_aliases=aliases,
        cost_estimate=pl.CostEstimate(flops=0, bytes_accessed=16_000_000, transcendentals=0),
        compiler_params=pltpu.CompilerParams(
            dimension_semantics=("arbitrary",), vmem_limit_bytes=32 * MIB
        ),
        name="lay_own" if mine else "lay_other",
    )(chip, core, *own, *got, *more)


def count_kernel(labels_ref, out_ref):
    count = jnp.sum(labels_ref[...].astype(F32), axis=1, keepdims=True)
    lane = lax.broadcasted_iota(jnp.int32, (1, 128), 1)
    row = jnp.where(lane == 0, count[0:1], jnp.where(lane == 1, count[1:2], 0.0))
    out_ref[...] = jnp.broadcast_to(row, (128, 128))


def on_device(
    tokens,
    labels,
    lengths,
    codes_one,
    mixing_one,
    inner_one,
    inner_bias_one,
    outer_one,
    outer_bias_one,
    codes_two,
    mixing_two,
    inner_two,
    inner_bias_two,
    outer_two,
    outer_bias_two,
    tower_inner,
    tower_inner_bias,
    tower_outer,
    tower_outer_bias,
):
    rows = tokens.shape[0]
    core = lax.axis_index("core").astype(jnp.int32).reshape(1)
    chip = lax.axis_index("chip").astype(jnp.int32).reshape(1)
    base = (lax.axis_index(("chip", "core")) * rows).astype(jnp.int32).reshape(1)

    def cross(a):
        return lax.ppermute(a, "core", [(0, 1), (1, 0)])

    codes_one, mixing_one, codes_two, mixing_two = (
        codes_one.T,
        mixing_one.T,
        codes_two.T,
        mixing_two.T,
    )
    labels = labels.T
    sent = pl.pallas_call(
        count_kernel, out_shape=jax.ShapeDtypeStruct((128, 128), F32), name="count"
    )(labels)
    counts = lax.all_to_all(sent, ("chip", "core"), 0, 0, tiled=True)
    *state, gate, code, mix, u, u_two = first_part(
        tokens, codes_one, mixing_one, inner_one, inner_bias_one, outer_one, outer_bias_one
    )
    towers = (tower_inner, tower_inner_bias, tower_outer, tower_outer_bias.reshape(1, TASKS))
    towers = (labels, counts, lengths.reshape(1, -1), base, *towers)
    send, keep_two, dy, predictions, small_send, small_keep = main_part(
        core, u_two, codes_two, mixing_two, inner_two, inner_bias_two, outer_two, outer_bias_two, towers
    )
    got_two = cross(send)
    small_got = cross(small_send)
    send, bias_one, acc, dgate = last_part(
        True, core, u, inner_one, outer_one, state, gate, dy, ()
    )
    got_one = cross(send)
    opened = open_rows(TWO, chip, core, keep_two, got_two)
    sent, kept_two = opened[:3], opened[3:]
    got_two = swap(0, sent)
    more = (acc, dgate, codes_one, mixing_one, outer_bias_one, code, mix)
    more += (bias_one,)
    keep_one, grad_tokens, small_own = last_part(
        False, core, u, inner_one, outer_one, state, gate, dy, more
    )
    *got_two, keep_one = lax.optimization_barrier((*got_two, keep_one))
    opened = open_rows(ONE, chip, core, keep_one, got_one, small_keep, small_got, small_own)
    got_one = swap(0, opened[:3])
    own = [
        reduce_color(i, chip, core, opened[3 + i], kept_two[i], got_one[i], got_two[i])
        for i in (2, 1, 0)
    ][::-1]
    got = swap(0, own)
    own_other = [cross(a) for a in own]
    got_other = [cross(a) for a in got]
    *found, small = lay(True, chip, core, own, got, ())
    found = lay(False, chip, core, own_other, got_other, (small, *found))
    inner_one, outer_one, inner_two, outer_two = found[:4]
    codes_one, mix_one, back_one, bias_one, codes_two, mix_two, back_two, bias_two = found[4:12]
    tower_inner, tower_bias, tower_outer, tower_last = found[12:]
    return (
        predictions.T,
        grad_tokens,
        codes_one.T,
        mix_one.T,
        inner_one,
        bias_one.reshape(-1),
        outer_one,
        back_one,
        codes_two.T,
        mix_two.T,
        inner_two,
        bias_two.reshape(-1),
        outer_two,
        back_two,
        tower_inner,
        tower_bias,
        tower_outer,
        tower_last.reshape(-1),
    )


def solution(mesh):
    chips = Mesh(mesh.devices.reshape(-1, 2), ("chip", "core"))
    rows, copied = P(("chip", "core"), None), P()
    return jax.shard_map(
        on_device,
        mesh=chips,
        in_specs=(rows, rows) + (copied,) * 17,
        out_specs=(rows, rows) + (copied,) * 16,
        check_vma=False,
    )
```
